32 devices in a mesh: dp: 4 (over y, x), group: 8 (over z, core).
Axes of the slice: x: 2, y: 2, z: 4, core: 2. Of those that a mesh axis runs over, the one named last changes fastest.
Arguments:
- source: bfloat16 [512, 9, 9, 2048], P('dp', None, None, 'group'), may hold values from -32 to 32
- offsets: int32 [512, 2], P('dp'), may hold values from 0 to 2
- cotangent: bfloat16 [512, 7, 7, 2048], P('dp', None, None, 'group'), may hold values from -6 to 6
- reduce_weight: float32 [2048, 1024], P('group'), may hold values from -0.125 to 0.125
- reduce_first: float32 [2048, 1024], P('group'), may hold values from -0.0068359375 to 0.0068359375
- reduce_second: float32 [2048, 1024], P('group'), may hold values from 2.223503e-07 to 8.894012e-07
- group_weight: float32 [3, 3, 32, 1024], P(None, None, None, 'group'), may hold values from -0.375 to 0.375
- group_first: float32 [3, 3, 32, 1024], P(None, None, None, 'group'), may hold values from -0.0068359375 to 0.0068359375
- group_second: float32 [3, 3, 32, 1024], P(None, None, None, 'group'), may hold values from 2.223503e-07 to 8.894012e-07
- expand_weight: float32 [1024, 2048], P(None, 'group'), may hold values from -0.1875 to 0.1875
- expand_first: float32 [1024, 2048], P(None, 'group'), may hold values from -0.0068359375 to 0.0068359375
- expand_second: float32 [1024, 2048], P(None, 'group'), may hold values from 2.223503e-07 to 8.894012e-07
- mid_norms: float32 [4, 1024], P(None, 'group'), may hold values from -1 to 3
- mid_first: float32 [4, 1024], P(None, 'group'), may hold values from -0.0068359375 to 0.0068359375
- mid_second: float32 [4, 1024], P(None, 'group'), may hold values from 2.223503e-07 to 8.894012e-07
- out_norms: float32 [2, 2048], P(None, 'group'), may hold values from -1 to 3
- out_first: float32 [2, 2048], P(None, 'group'), may hold values from -0.0068359375 to 0.0068359375
- out_second: float32 [2, 2048], P(None, 'group'), may hold values from 2.223503e-07 to 8.894012e-07
Outputs:
- output: bfloat16 [512, 7, 7, 2048], P('dp', None, None, 'group')
- input_grad: bfloat16 [512, 7, 7, 2048], P('dp', None, None, 'group')
- grad_norm: float32 [], replicated
- reduce_master: float32 [2048, 1024], P('group')
- reduce_momentum: float32 [2048, 1024], P('group')
- reduce_variance: float32 [2048, 1024], P('group')
- reduce_copy: bfloat16 [2048, 1024], P('group')
- group_master: float32 [3, 3, 32, 1024], P(None, None, None, 'group')
- group_momentum: float32 [3, 3, 32, 1024], P(None, None, None, 'group')
- group_variance: float32 [3, 3, 32, 1024], P(None, None, None, 'group')
- group_copy: bfloat16 [3, 3, 32, 1024], P(None, None, None, 'group')
- expand_master: float32 [1024, 2048], P(None, 'group')
- expand_momentum: float32 [1024, 2048], P(None, 'group')
- expand_variance: float32 [1024, 2048], P(None, 'group')
- expand_copy: bfloat16 [1024, 2048], P(None, 'group')
- mid_master: float32 [4, 1024], P(None, 'group')
- mid_momentum: float32 [4, 1024], P(None, 'group')
- mid_variance: float32 [4, 1024], P(None, 'group')
- mid_copy: bfloat16 [4, 1024], P(None, 'group')
- out_master: float32 [2, 2048], P(None, 'group')
- out_momentum: float32 [2, 2048], P(None, 'group')
- out_variance: float32 [2, 2048], P(None, 'group')
- out_copy: bfloat16 [2, 2048], P(None, 'group')
The draws below stay inside these ranges and needn't reach their ends.
All inputs are finite; a program needn't handle non-finite values.
Results may differ from the reference program's by a relative error of at most 0.023.
Values may be sent and summed in bfloat16 or wider, within the bound.
No kernel may reach another device: no remote copies, remote signals or barrier semaphores. Data moves between devices by JAX's collectives and lax.ppermute only.
A program may use at most 256 MiB of HBM per device.

```python
import math
import jax
import jax.numpy as jnp
from jax import lax

CIN = 2048
GROUPS = 32
GW = 32
HW = 7
STEP = 10
MID = 1024
SRC = 9
COPIES = 512
NPARAM = 4497408


def rising_norms(key, width, low_end, reach):
    gain_key, shift_key = jax.random.split(jax.random.fold_in(key, 7))
    position = jnp.arange(width, dtype=jnp.float32) / max(width - 1, 1)
    gain_rows = (low_end + position)[None, :] * jax.random.uniform(gain_key, (2, width), jnp.float32, 0.85, 1.15)
    shift_rows = jax.random.uniform(shift_key, (2, width), jnp.float32, -reach, reach)
    return (gain_rows, shift_rows)


def draw_source(key, part):
    noise_key, jitter_key = jax.random.split(jax.random.fold_in(key, 3))
    position = jnp.arange(COPIES, dtype=jnp.float32) / max(COPIES - 1, 1)
    values = jnp.clip(jax.random.normal(noise_key, (COPIES, SRC, SRC, CIN), jnp.float32), -6.0, 6.0)
    growth = 3.0 ** position
    jitter = jax.random.uniform(jitter_key, (COPIES,), jnp.float32, 0.8, 1.25)
    return (values * (growth * jitter)[:, None, None, None]).astype(jnp.bfloat16)


def draw_mid_norms(key, part):
    gain_rows, shift_rows = rising_norms(key, MID, 0.5, 0.5)
    return jnp.stack([gain_rows[0], shift_rows[0], gain_rows[1], shift_rows[1]]).astype(jnp.float32)


def draw_out_norms(key, part):
    gain_rows, shift_rows = rising_norms(key, CIN, 0.5, 0.5)
    return jnp.stack([gain_rows[0], shift_rows[0]]).astype(jnp.float32)


def with_ends(values, stream_key, smallest, high):
    index_at = [jax.random.randint(jax.random.fold_in(stream_key, axis), (), 0, length) for axis, length in enumerate(values.shape)]
    longest = values.shape.index(max(values.shape))
    next_to = index_at[:longest] + [(index_at[longest] + 1) % values.shape[longest]] + index_at[longest + 1:]
    return values.at[tuple(index_at)].set(smallest).at[tuple(next_to)].set(high)


def shard_levels(key, shape, shards, least, top_value):
    gain, own = 1.0, jax.random.fold_in(key, 6)
    for axis_at, blocks in shards:
        steps = jnp.exp(jax.random.uniform(jax.random.fold_in(own, axis_at), (blocks,), jnp.float32, least / len(shards), top_value / len(shards)))
        gain = gain * jnp.repeat(steps, shape[axis_at] // blocks).reshape([-1 if axis == axis_at else 1 for axis in range(len(shape))])
    return gain


def normal_values(rng, extent, scale, bound, cuts=(), held_as=jnp.bfloat16):
    drawn = scale * jax.random.normal(rng, extent, jnp.float32)
    if cuts:
        drawn = drawn * shard_levels(rng, extent, cuts, -0.22, 0.18)
    return jnp.clip(drawn, -bound, bound).astype(held_as)


def setup_inputs(seed: int = 0) -> dict:
    key_list = jax.random.split(jax.random.key(seed), 19)
    return {
        "source": draw_source(jax.random.fold_in(key_list[18], 71), 0),
        "offsets": with_ends(jax.random.randint(key_list[1], (COPIES, 2), 0, SRC - HW + 1), jax.random.fold_in(key_list[1], 1), 0, SRC - HW).astype(jnp.int32),
        "cotangent": normal_values(key_list[2], (COPIES, HW, HW, CIN), 1.0, 6.0, ((0, 4), (3, 8))),
        "reduce_weight": normal_values(key_list[3], (CIN, MID), CIN ** -0.5, 0.125, ((0, 8),), jnp.float32),
        "reduce_first": normal_values(key_list[4], (CIN, MID), (NPARAM ** -0.5), 0.0068359375, ((0, 8),), jnp.float32),
        "reduce_second": jnp.clip(jnp.exp(math.log(8.894011784832401e-07) - 1.3862944 * jax.random.uniform(key_list[5], (CIN, MID), jnp.float32) ** shard_levels(key_list[5], (CIN, MID), ((0, 8),), -0.2, 0.2)), 2.2235029462081002e-07, 8.894011784832401e-07),
        "group_weight": normal_values(key_list[6], (3, 3, GW, MID), (9 * GW) ** -0.5, 0.375, ((3, 8),), jnp.float32),
        "group_first": normal_values(key_list[7], (3, 3, GW, MID), (NPARAM ** -0.5), 0.0068359375, ((3, 8),), jnp.float32),
        "group_second": jnp.clip(jnp.exp(math.log(8.894011784832401e-07) - 1.3862944 * jax.random.uniform(key_list[8], (3, 3, GW, MID), jnp.float32) ** shard_levels(key_list[8], (3, 3, GW, MID), ((3, 8),), -0.2, 0.2)), 2.2235029462081002e-07, 8.894011784832401e-07),
        "expand_weight": normal_values(key_list[9], (MID, CIN), MID ** -0.5, 0.1875, ((1, 8),), jnp.float32),
        "expand_first": normal_values(key_list[10], (MID, CIN), (NPARAM ** -0.5), 0.0068359375, ((1, 8),), jnp.float32),
        "expand_second": jnp.clip(jnp.exp(math.log(8.894011784832401e-07) - 1.3862944 * jax.random.uniform(key_list[11], (MID, CIN), jnp.float32) ** shard_levels(key_list[11], (MID, CIN), ((1, 8),), -0.2, 0.2)), 2.2235029462081002e-07, 8.894011784832401e-07),
        "mid_norms": draw_mid_norms(jax.random.fold_in(key_list[18], 71), 0),
        "mid_first": normal_values(key_list[13], (4, MID), (NPARAM ** -0.5), 0.0068359375, ((1, 8),), jnp.float32),
        "mid_second": jnp.clip(jnp.exp(math.log(8.894011784832401e-07) - 1.3862944 * jax.random.uniform(key_list[14], (4, MID), jnp.float32) ** shard_levels(key_list[14], (4, MID), ((1, 8),), -0.2, 0.2)), 2.2235029462081002e-07, 8.894011784832401e-07),
        "out_norms": draw_out_norms(jax.random.fold_in(key_list[18], 71), 0),
        "out_first": normal_values(key_list[16], (2, CIN), (NPARAM ** -0.5), 0.0068359375, ((1, 8),), jnp.float32),
        "out_second": jnp.clip(jnp.exp(math.log(8.894011784832401e-07) - 1.3862944 * jax.random.uniform(key_list[17], (2, CIN), jnp.float32) ** shard_levels(key_list[17], (2, CIN), ((1, 8),), -0.2, 0.2)), 2.2235029462081002e-07, 8.894011784832401e-07),
    }


@jax.custom_vjp
def low(v):
    return lax.optimization_barrier(v.astype(jnp.bfloat16)).astype(jnp.float32)

@jax.custom_vjp
def low_back(v):
    return v

def low_keep(v):
    return (low(v), None)

def low_pass(kept, grad):
    return (grad,)

def back_keep(v):
    return (v, None)

def back_low(kept, grad):
    return (low(grad),)
low.defvjp(low_keep, low_pass)
low_back.defvjp(back_keep, back_low)
norm_eps = 1e-05
adam_eps = 1e-08
clip_norm = 1.0
moment_decay = 0.5
highest = lax.Precision.HIGHEST

def crop_images(images, offsets):

    def crop_one(one_image, offset):
        return lax.dynamic_slice(one_image, (offset[0].astype(jnp.int32), offset[1].astype(jnp.int32), jnp.zeros((), jnp.int32)), (HW, HW, one_image.shape[2]))
    return jax.vmap(crop_one)(images, offsets)

def batch_norm(values, gain_row, shifts):
    center = lax.optimization_barrier(jnp.mean(values, axis=(0, 1, 2), keepdims=True))
    spread = lax.optimization_barrier(jnp.mean(values * values, axis=(0, 1, 2), keepdims=True)) - center * center
    return (values - center) * lax.rsqrt(spread + norm_eps) * gain_row + shifts

def forward(pixels, reduce_weight, group_weight, expand_weight, mid_norms, out_norms):
    first_pre = low_back(jnp.einsum('nhwc,cm->nhwm', pixels, low(reduce_weight), precision=highest))
    first_act = low(jax.nn.gelu(batch_norm(first_pre, mid_norms[0], mid_norms[1])))
    second_pre = low_back(lax.conv_general_dilated(first_act, low(group_weight), (1, 1), 'SAME', dimension_numbers=('NHWC', 'HWIO', 'NHWC'), feature_group_count=GROUPS, precision=highest))
    second_act = low(jax.nn.gelu(batch_norm(second_pre, mid_norms[2], mid_norms[3])))
    expanded = low_back(jnp.einsum('nhwm,mc->nhwc', second_act, low(expand_weight), precision=highest))
    return jax.nn.gelu(batch_norm(expanded, out_norms[0], out_norms[1]) + pixels)

def adam_step(weight, gradient, momentum, variance, learn_rate, decay_rate):
    momentum_new = moment_decay * momentum + (1.0 - moment_decay) * gradient
    variance_new = moment_decay * variance + (1.0 - moment_decay) * gradient * gradient
    correction = 1.0 - moment_decay ** STEP
    direction = momentum_new / correction / (jnp.sqrt(variance_new / correction) + adam_eps)
    weight_new = weight - learn_rate * (direction + decay_rate * weight)
    return (weight_new, momentum_new, variance_new, weight_new.astype(jnp.bfloat16))

def reference(source, offsets, cotangent, reduce_weight, reduce_first, reduce_second, group_weight, group_first, group_second, expand_weight, expand_first, expand_second, mid_norms, mid_first, mid_second, out_norms, out_first, out_second):
    pixels = crop_images(source, offsets).astype(jnp.float32)
    result, pull = jax.vjp(forward, pixels, reduce_weight, group_weight, expand_weight, mid_norms, out_norms)
    grads = pull(cotangent.astype(jnp.float32))
    input_grad = grads[0].astype(jnp.bfloat16)
    total_sq = jnp.zeros((), jnp.float32)
    for grad_item in grads[1:]:
        total_sq = total_sq + jnp.sum(grad_item * grad_item)
    grad_norm = jnp.sqrt(total_sq)
    clip_scale = jnp.minimum(1.0, clip_norm / (grad_norm + 1e-06))
    reduce_out = adam_step(reduce_weight, grads[1] * clip_scale, reduce_first, reduce_second, 1.0 / jnp.sqrt(1.0 * CIN), 0.1)
    group_out = adam_step(group_weight, grads[2] * clip_scale, group_first, group_second, 1.0 / jnp.sqrt(9.0 * GW), 0.1)
    expand_out = adam_step(expand_weight, grads[3] * clip_scale, expand_first, expand_second, 1.0 / jnp.sqrt(1.0 * MID), 0.1)
    mid_out = adam_step(mid_norms, grads[4] * clip_scale, mid_first, mid_second, 0.5, 0.0)
    out_out = adam_step(out_norms, grads[5] * clip_scale, out_first, out_second, 0.5, 0.0)
    return (result.astype(jnp.bfloat16), input_grad, grad_norm, reduce_out[0], reduce_out[1], reduce_out[2], reduce_out[3], group_out[0], group_out[1], group_out[2], group_out[3], expand_out[0], expand_out[1], expand_out[2], expand_out[3], mid_out[0], mid_out[1], mid_out[2], mid_out[3], out_out[0], out_out[1], out_out[2], out_out[3])
```

```python
import functools

import jax
import jax.numpy as jnp
from jax import lax
from jax.experimental import pallas as pl
from jax.experimental.pallas import tpu as pltpu
from jax.sharding import PartitionSpec as P

CIN = 2048
GW = 32
HW = 7
STEP = 10
MID = 1024
SRC = 9
NQ = 4
QW = MID // NQ
SPOTS = HW * HW

norm_eps = 1e-05
adam_eps = 1e-08
clip_norm = 1.0
moment_decay = 0.5

GELU_K = 0.7978845608028654
GELU_C = 0.044715
VMEM_MB = 56
BF = jnp.bfloat16
F32 = jnp.float32


def dot(a, b):
    return jnp.dot(a, b, preferred_element_type=F32)


def dot_t(a, b):
    return lax.dot_general(a, b, (((1,), (1,)), ((), ())), preferred_element_type=F32)


def dot_rows(a, b):
    return lax.dot_general(a, b, (((0,), (0,)), ((), ())), preferred_element_type=F32)


def gelu(u):
    t = jnp.tanh(GELU_K * (u + GELU_C * (u * u * u)))
    return 0.5 * u * (1.0 + t)


def gelu_both(u):
    u2 = u * u
    t = jnp.tanh(GELU_K * (u + GELU_C * (u2 * u)))
    half = 0.5 * (1.0 + t)
    slope = half + (0.5 * GELU_K) * u * (1.0 - t * t) * (1.0 + (3.0 * GELU_C) * u2)
    return u * half, slope


def norm_rows(total, squares, count):
    center = total / count
    spread = squares / count - center * center
    return center, lax.rsqrt(spread + norm_eps)


def whole(shape):
    return pl.BlockSpec(shape, lambda *_: (0,) * len(shape))


def call(body, name, grid, in_specs, out_specs, out_shape, scratch=(), flops=0, aliases=None):
    nbytes = sum(s.size * s.dtype.itemsize for s in jax.tree.leaves(out_shape))
    return pl.pallas_call(
        body,
        grid_spec=pltpu.PrefetchScalarGridSpec(
            num_scalar_prefetch=1,
            grid=grid,
            in_specs=in_specs,
            out_specs=out_specs,
            scratch_shapes=list(scratch),
        ),
        out_shape=out_shape,
        compiler_params=pltpu.CompilerParams(vmem_limit_bytes=VMEM_MB * 1024 * 1024),
        cost_estimate=pl.CostEstimate(flops=flops, bytes_accessed=3 * nbytes, transcendentals=0),
        input_output_aliases=aliases or {},
        name=name,
    )


def sds(shape, dtype):
    return jax.ShapeDtypeStruct(shape, dtype)


def crop_kernel(sc, src, off, out):
    images = src.shape[2]
    lanes = src.shape[3]
    row = jnp.broadcast_to(off[:, 0:1], (images, lanes))
    col = jnp.broadcast_to(off[:, 1:2], (images, lanes))
    r0, r1 = row == 0, row == 1
    c0, c1 = col == 0, col == 1

    def step(i, carry):
        for j in range(HW):
            picks = []
            for a in range(SRC - HW + 1):
                x0 = src[i + a, j].astype(F32)
                x1 = src[i + a, j + 1].astype(F32)
                x2 = src[i + a, j + 2].astype(F32)
                picks.append(jnp.where(c0, x0, jnp.where(c1, x1, x2)))
            best = jnp.where(r0, picks[0], jnp.where(r1, picks[1], picks[2]))
            out[i * HW + j] = best.astype(out.dtype)
        return carry

    lax.fori_loop(0, HW, step, 0)


def split_store(sc, k, value, own, other):
    q = sc[0] ^ k
    mine = (q // 2) == sc[1]

    @pl.when(mine)
    def _():
        own[pl.ds(q % 2, 1)] = value[None]

    @pl.when(jnp.logical_not(mine))
    def _():
        other[pl.ds(q % 2, 1)] = value.astype(other.dtype)[None]


def fill_quarters(sc, own, rec, quarters):
    for h in range(2):
        quarters[pl.ds(2 * sc[1] + h, 1)] = own[h : h + 1]
        quarters[pl.ds(2 * (1 - sc[1]) + h, 1)] = rec[h : h + 1]


def quarter(sc, quarters, k):
    return quarters[pl.ds(sc[0] ^ k, 1)][0]


def reduce_kernel(nz, sc, *refs):
    xs, ws, (own, other) = refs[:nz], refs[nz : nz + NQ], refs[nz + NQ :]
    x = jnp.concatenate([r[...] for r in xs], axis=1)
    for k in range(NQ):
        split_store(sc, k, dot(x, ws[k][...].reshape(x.shape[1], QW)), own, other)


def add_sums(sums, index, first, second):
    rows = jnp.concatenate(
        [jnp.sum(first, axis=0, keepdims=True), jnp.sum(second, axis=0, keepdims=True)], axis=0
    )
    sums[pl.ds(index, 1)] += rows[None]


def start_sums(sums):
    @pl.when(pl.program_id(0) == 0)
    def _():
        sums[...] = jnp.zeros_like(sums)


def first_sums_kernel(sc, own, rec, sums):
    start_sums(sums)
    for h in range(2):
        v = own[h] + rec[h].astype(F32)
        add_sums(sums, h, v, v * v)


def zero_border(pad, images):
    span = pad.shape[1]
    pad[0] = jnp.zeros_like(pad[0])
    pad[SRC - 1] = jnp.zeros_like(pad[0])
    edge = jnp.zeros((HW, images, pad.shape[2]), pad.dtype)
    pad[1 : HW + 1, 0:images] = edge
    pad[1 : HW + 1, span - images : span] = edge


def conv_kernel(count, images, sc, own, rec, tot, par, diag, act, v2, sums, pad):
    rows = HW * images
    center, inv = norm_rows(tot[0, 0:1], tot[0, 1:2], count)
    gain, shift = par[0, 0:1], par[0, 1:2]
    zero_border(pad, images)

    def fill(i, carry):
        at = pl.ds(pl.multiple_of(i * rows, rows), rows)
        v = own[0, at] + rec[0, at].astype(F32)
        a = gelu((v - center) * inv * gain + shift).astype(BF)
        act[0, at] = a
        pad[pl.ds(i + 1, 1), images : images + rows] = a[None]
        return carry

    lax.fori_loop(0, HW, fill, 0)
    sums[...] = jnp.zeros_like(sums)

    def taps(i, carry):
        acc = jnp.zeros((rows, QW), F32)
        for di in range(3):
            line = pad[pl.ds(i + di, 1)][0]
            for dj in range(3):
                acc = acc + dot(line[dj * images : dj * images + rows], diag[0, di * 3 + dj])
        v2[0, pl.ds(pl.multiple_of(i * rows, rows), rows)] = acc
        add_sums(sums, 0, acc, acc * acc)
        return carry

    lax.fori_loop(0, HW, taps, 0)


def second_act_kernel(count, sc, v2, tot, par, out):
    for h in range(2):
        center, inv = norm_rows(tot[h, 0:1], tot[h, 1:2], count)
        u = (v2[h] - center) * inv * par[h, 2:3] + par[h, 3:4]
        out[h] = gelu(u).astype(BF)


def expand_kernel(nz, sc, own, rec, *refs):
    ws, (e, sums, quarters) = refs[:NQ], refs[NQ:]
    start_sums(sums)
    fill_quarters(sc, own, rec, quarters)
    for d in range(nz):
        acc = dot(quarter(sc, quarters, 0), ws[0][d])
        for k in range(1, NQ):
            acc = acc + dot(quarter(sc, quarters, k), ws[k][d])
        e[d] = acc
        add_sums(sums, (sc[2] + (nz - d)) % nz, acc, acc * acc)


def out_kernel(nz, count, sc, e, tot, par, *refs):
    xs, cots, outs, (up, sums) = (
        refs[:nz],
        refs[nz : 2 * nz],
        refs[2 * nz : 3 * nz],
        refs[3 * nz :],
    )
    start_sums(sums)
    for d in range(nz):
        zs = (sc[2] + (nz - d)) % nz
        t = tot[pl.ds(zs, 1)][0]
        center, inv = norm_rows(t[0:1], t[1:2], count)
        hat = (e[d] - center) * inv
        value, slope = gelu_both(hat * par[d, 0:1] + par[d, 1:2] + xs[d][...].astype(F32))
        outs[d][...] = value.astype(BF)
        u = cots[d][...].astype(F32) * slope
        up[d] = u
        add_sums(sums, zs, u, u * hat)


def expand_back_kernel(nz, count, sc, e, up, tot, tot_b, par, *refs):
    ws, (eg, own, other) = refs[:NQ], refs[NQ:]
    grads = []
    for d in range(nz):
        zs = (sc[2] + (nz - d)) % nz
        t, b = tot[pl.ds(zs, 1)][0], tot_b[pl.ds(zs, 1)][0]
        center, inv = norm_rows(t[0:1], t[1:2], count)
        hat = (e[d] - center) * inv
        g = (inv * par[d, 0:1]) * (up[d] - b[0:1] / count - hat * (b[1:2] / count))
        grads.append(g.astype(BF))
        eg[d] = grads[d]
    for k in range(NQ):
        acc = dot_t(grads[0], ws[k][0])
        for d in range(1, nz):
            acc = acc + dot_t(grads[d], ws[k][d])
        split_store(sc, k, acc, own, other)


def second_up_kernel(count, sc, own, rec, v2, tot, par, up, sums):
    start_sums(sums)
    for h in range(2):
        center, inv = norm_rows(tot[h, 0:1], tot[h, 1:2], count)
        hat = (v2[h] - center) * inv
        slope = gelu_both(hat * par[h, 2:3] + par[h, 3:4])[1]
        u = (own[h] + rec[h].astype(F32)) * slope
        up[h] = u
        add_sums(sums, h, u, u * hat)


def conv_back_kernel(
    count, images, sc, up2, v2, tot2, tot2b, par, diag, own, rec, tot1, cg, up1, sums, pad
):
    rows = HW * images
    center2, inv2 = norm_rows(tot2[0, 0:1], tot2[0, 1:2], count)
    factor = inv2 * par[0, 2:3]
    mean_d, mean_x = tot2b[0, 0:1] / count, tot2b[0, 1:2] / count
    zero_border(pad, images)

    def fill(i, carry):
        at = pl.ds(pl.multiple_of(i * rows, rows), rows)
        hat = (v2[0, at] - center2) * inv2
        g = (factor * (up2[0, at] - mean_d - hat * mean_x)).astype(BF)
        cg[0, at] = g
        pad[pl.ds(i + 1, 1), images : images + rows] = g[None]
        return carry

    lax.fori_loop(0, HW, fill, 0)
    center, inv = norm_rows(tot1[0, 0:1], tot1[0, 1:2], count)
    sums[...] = jnp.zeros_like(sums)

    def taps(i, carry):
        at = pl.ds(pl.multiple_of(i * rows, rows), rows)
        acc = jnp.zeros((rows, QW), F32)
        for di in range(3):
            line = pad[pl.ds(i + 2 - di, 1)][0]
            for dj in range(3):
                start = (2 - dj) * images
                acc = acc + dot_t(line[start : start + rows], diag[0, di * 3 + dj])
        hat = (own[0, at] + rec[0, at].astype(F32) - center) * inv
        u = acc * gelu_both(hat * par[0, 0:1] + par[0, 1:2])[1]
        up1[0, at] = u
        add_sums(sums, 0, u, u * hat)
        return carry

    lax.fori_loop(0, HW, taps, 0)


def first_grad_kernel(count, sc, up1, own, rec, tot, tot_b, par, out):
    for h in range(2):
        center, inv = norm_rows(tot[h, 0:1], tot[h, 1:2], count)
        hat = (own[h] + rec[h].astype(F32) - center) * inv
        g = (inv * par[h, 0:1]) * (up1[h] - tot_b[h, 0:1] / count - hat * (tot_b[h, 1:2] / count))
        out[h] = g.astype(BF)


def input_grad_kernel(sc, own, rec, up, *refs):
    ws, (out, quarters) = refs[:NQ], refs[NQ:]
    fill_quarters(sc, own, rec, quarters)
    acc = up[0]
    for k in range(NQ):
        acc = acc + dot_t(quarter(sc, quarters, k), ws[k][0])
    out[...] = acc.astype(BF)


def reduce_wgrad_kernel(nz, sc, own, rec, *refs):
    xs, outs, quarters = refs[:nz], refs[nz : nz + NQ], refs[nz + NQ]
    fill_quarters(sc, own, rec, quarters)
    grads = jnp.concatenate([quarter(sc, quarters, k) for k in range(NQ)], axis=1)
    for d in range(nz):
        g = dot_rows(xs[d][...], grads)
        for k in range(NQ):
            outs[k][d] = g[:, k * QW : (k + 1) * QW].astype(BF)


def expand_wgrad_kernel(nz, sc, own, rec, eg, *refs):
    outs, quarters = refs[:NQ], refs[NQ]
    fill_quarters(sc, own, rec, quarters)
    width = eg.shape[2]
    grads = jnp.concatenate([eg[d] for d in range(nz)], axis=1)
    for k in range(NQ):
        g = dot_rows(quarter(sc, quarters, k), grads)
        for d in range(nz):
            outs[k][d] = g[:, d * width : (d + 1) * width].astype(BF)


def conv_wgrad_kernel(images, sc, act, cg, out, pad):
    rows = HW * images
    zero_border(pad, images)
    for i in range(HW):
        pad[i + 1, images : images + rows] = act[0, i * rows : (i + 1) * rows]
    grad = cg[0]
    group_row = lax.broadcasted_iota(jnp.int32, (QW, QW), 0) // GW
    group_col = lax.broadcasted_iota(jnp.int32, (QW, QW), 1) // GW
    keep = group_row == group_col
    for di in range(3):
        for dj in range(3):
            window = pad[di : di + HW, dj * images : dj * images + rows].reshape(HW * rows, QW)
            full = jnp.where(keep, dot_rows(window, grad), 0.0)
            out[0, di * 3 + dj] = jnp.sum(full.reshape(QW // GW, GW, QW), axis=0)


def place_kernel(sc, *refs):
    refs[-1][...] = refs[0][...].reshape(refs[-1].shape)


def adam_step(weight, gradient, momentum, variance, learn_rate, decay_rate):
    momentum_new = moment_decay * momentum + (1.0 - moment_decay) * gradient
    variance_new = moment_decay * variance + (1.0 - moment_decay) * gradient * gradient
    correction = 1.0 - moment_decay**STEP
    direction = momentum_new / correction / (jnp.sqrt(variance_new / correction) + adam_eps)
    weight_new = weight - learn_rate * (direction + decay_rate * weight)
    return (weight_new, momentum_new, variance_new, weight_new.astype(BF))


def shards(
    source,
    offsets,
    cotangent,
    reduce_weight,
    reduce_first,
    reduce_second,
    group_weight,
    group_first,
    group_second,
    expand_weight,
    expand_first,
    expand_second,
    mid_norms,
    mid_first,
    mid_second,
    out_norms,
    out_first,
    out_second,
):
    nd, ng = lax.axis_size("dp"), lax.axis_size("group")
    nz = ng // 2
    gi = lax.axis_index("group")
    z, core = gi // 2, gi % 2
    p = lax.axis_index("dp") % NQ
    sc = jnp.stack([p, core, z]).astype(jnp.int32)
    n = source.shape[0]
    images = n // nz
    rows = SPOTS * images
    step = HW * images
    cb = source.shape[3]
    mb = group_weight.shape[3]
    zh = nz // 2
    count = float(SPOTS * n * nd)

    def over_z(value, d):
        pairs = [(2 * a + c, 2 * ((a + d) % nz) + c) for a in range(nz) for c in range(2)]
        return lax.ppermute(value, "group", pairs)

    def over_core(value):
        return lax.ppermute(value, "group", [(a, a ^ 1) for a in range(ng)])

    def over_dp(value, k):
        return lax.ppermute(value, "dp", [(a, a ^ k) for a in range(nd)])

    def everywhere(value):
        k = 1
        while k < nd:
            value = value + over_dp(value, k)
            k *= 2
        k = 2
        while k < ng:
            value = value + lax.ppermute(value, "group", [(a, a ^ k) for a in range(ng)])
            k *= 2
        return value

    col_starts = [((p % 2) * zh + j) * 2 * mb + (p // 2) * mb for j in range(zh)]
    reduce_piece = jnp.concatenate(
        [lax.dynamic_slice_in_dim(reduce_weight, s, mb, 1) for s in col_starts], axis=1
    ).astype(BF)
    expand_piece = (
        lax.dynamic_slice(
            expand_weight.reshape(nz, 2, mb, cb),
            ((p % 2) * zh, p // 2, 0, 0),
            (zh, 1, mb, cb),
        )
        .reshape(QW, cb)
        .astype(BF)
    )

    def spread_weight(piece):
        mine = jnp.stack([piece] + [over_z(piece, d) for d in range(1, nz)])
        return [mine] + [over_dp(mine, k) for k in range(1, NQ)]

    reduce_q = spread_weight(reduce_piece)
    taps_rows = 9 * GW
    pack = jnp.concatenate(
        [group_weight.reshape(taps_rows, mb), mid_norms, out_norms.reshape(-1, mb)], axis=0
    )
    packs = [pack] + [over_z(pack, d) for d in range(1, nz)]
    by_z = jnp.zeros((nz,) + pack.shape, F32)
    for d in range(nz):
        by_z = lax.dynamic_update_slice(by_z, packs[d][None], ((z + nz - d) % nz, 0, 0))
    half = by_z.transpose(1, 0, 2).reshape(pack.shape[0], 2, QW)
    mid_par = half[taps_rows : taps_rows + 4].transpose(1, 0, 2)
    out_par = jnp.stack([v[taps_rows + 4 :].reshape(2, cb) for v in packs])
    conv_low = half[:taps_rows].astype(BF).reshape(9, 1, GW, 2, QW).transpose(3, 0, 1, 2, 4)
    own_group = (jnp.arange(QW) // GW)[None, :] == jnp.arange(QW // GW)[:, None]
    diag = jnp.where(own_group[:, None, :], conv_low, jnp.zeros((), BF)).reshape(2, 9, QW, QW)

    src = source.transpose(1, 2, 0, 3)
    pixels = []
    lane = 128 if cb % 128 == 0 else cb
    for d in range(nz):
        crop = call(
            crop_kernel,
            "crop",
            (cb // lane,),
            [
                pl.BlockSpec(
                    (SRC, SRC, images, lane), lambda i, s, d=d: (0, 0, (s[2] + d) % nz, i)
                ),
                pl.BlockSpec((images, 2), lambda i, s, d=d: ((s[2] + d) % nz, 0)),
            ],
            pl.BlockSpec((SPOTS, images, lane), lambda i, s: (0, 0, i)),
            sds((SPOTS, images, cb), BF),
        )(sc, src, offsets)
        crop = crop.reshape(rows, cb)
        pixels.append(over_z(crop, d) if d else crop)
    cot = cotangent.transpose(1, 2, 0, 3).reshape(SPOTS, n, cb)
    cots = []
    for d in range(nz):
        piece = lax.dynamic_slice_in_dim(cot, ((z + d) % nz) * images, images, 1)
        piece = piece.reshape(rows, cb)
        cots.append(over_z(piece, d) if d else piece)
    expand_q = spread_weight(expand_piece)

    grid = (HW,)
    block2 = pl.BlockSpec((2, step, QW), lambda i, s: (0, i, 0))
    blockz = pl.BlockSpec((nz, step, cb), lambda i, s: (0, i, 0))
    rowc = pl.BlockSpec((step, cb), lambda i, s: (i, 0))
    sum2, sumz = whole((2, 2, QW)), whole((nz, 2, cb))
    par2 = whole((2, 4, QW))
    wr, we = whole((nz, cb, QW)), whole((nz, QW, cb))
    half_f, half_b = sds((2, rows, QW), F32), sds((2, rows, QW), BF)
    sum2_s, sumz_s = sds((2, 2, QW), F32), sds((nz, 2, cb), F32)
    per_h = pl.BlockSpec((1, rows, QW), lambda i, s: (i, 0, 0))
    sum_h = pl.BlockSpec((1, 2, QW), lambda i, s: (i, 0, 0))
    par_h = pl.BlockSpec((1, 4, QW), lambda i, s: (i, 0, 0))
    diag_h = pl.BlockSpec((1, 9, QW, QW), lambda i, s: (i, 0, 0, 0))
    pad_s = pltpu.VMEM((SRC, SRC * images, QW), BF)
    quarters_s = pltpu.VMEM((NQ, step, QW), BF)
    big = 2 * rows * MID * MID

    own1, oth1 = call(
        functools.partial(reduce_kernel, nz),
        "reduce",
        grid,
        [rowc] * nz + [wr] * NQ,
        [block2, block2],
        [half_f, half_b],
        flops=big,
    )(sc, *pixels, *reduce_q)
    rec1 = over_core(oth1)
    tot1 = everywhere(
        call(first_sums_kernel, "first_sums", grid, [block2, block2], sum2, sum2_s)(sc, own1, rec1)
    )
    act, v2, sums2 = call(
        functools.partial(conv_kernel, count, images),
        "conv",
        (2,),
        [per_h, per_h, sum_h, par_h, diag_h],
        [per_h, per_h, sum_h],
        [half_b, half_f, sum2_s],
        [pad_s],
        flops=big,
    )(sc, own1, rec1, tot1, mid_par, diag)
    tot2 = everywhere(sums2)
    sa = call(
        functools.partial(second_act_kernel, count),
        "second_act",
        grid,
        [block2, sum2, par2],
        block2,
        half_b,
    )(sc, v2, tot2, mid_par)
    sa_rec = over_core(sa)
    e, sums3 = call(
        functools.partial(expand_kernel, nz),
        "expand",
        grid,
        [block2, block2] + [we] * NQ,
        [blockz, sumz],
        [sds((nz, rows, cb), F32), sumz_s],
        [quarters_s],
        flops=big,
    )(sc, sa, sa_rec, *expand_q)
    tot3 = everywhere(sums3)
    res = call(
        functools.partial(out_kernel, nz, count),
        "out",
        grid,
        [blockz, sumz, whole((nz, 2, cb))] + [rowc] * (2 * nz),
        [rowc] * nz + [blockz, sumz],
        [sds((rows, cb), BF)] * nz + [sds((nz, rows, cb), F32), sumz_s],
    )(sc, e, tot3, out_par, *pixels, *cots)
    outs, up3, sums3b = res[:nz], res[nz], res[nz + 1]
    tot3b = everywhere(sums3b)

    def place(blocks):
        shape = sds((SPOTS, n, cb), BF)
        result = None
        for d in range(nz):
            spec = pl.BlockSpec((SPOTS, images, cb), lambda i, s, d=d: (0, (s[2] + d) % nz, 0))
            inputs = [blocks[d]]
            in_specs = [whole((rows, cb))]
            aliases = {}
            if result is not None:
                inputs.append(result)
                in_specs.append(pl.BlockSpec(memory_space=pl.ANY))
                aliases = {2: 0}
            result = call(place_kernel, "place", (1,), in_specs, spec, shape, aliases=aliases)(
                sc, *inputs
            )
        return result.reshape(HW, HW, n, cb).transpose(2, 0, 1, 3)

    output = place([over_z(outs[d], -d) if d else outs[0] for d in range(nz)])

    eg, own2, oth2 = call(
        functools.partial(expand_back_kernel, nz, count),
        "expand_back",
        grid,
        [blockz, blockz, sumz, sumz, whole((nz, 2, cb))] + [we] * NQ,
        [blockz, block2, block2],
        [sds((nz, rows, cb), BF), half_f, half_b],
        flops=big,
    )(sc, e, up3, tot3, tot3b, out_par, *expand_q)
    rec2 = over_core(oth2)
    up2, sums2b = call(
        functools.partial(second_up_kernel, count),
        "second_up",
        grid,
        [block2, block2, block2, sum2, par2],
        [block2, sum2],
        [half_f, sum2_s],
    )(sc, own2, rec2, v2, tot2, mid_par)
    tot2b = everywhere(sums2b)
    cg, up1, sums1b = call(
        functools.partial(conv_back_kernel, count, images),
        "conv_back",
        (2,),
        [per_h, per_h, sum_h, sum_h, par_h, diag_h, per_h, per_h, sum_h],
        [per_h, per_h, sum_h],
        [half_b, half_f, sum2_s],
        [pad_s],
        flops=big,
    )(sc, up2, v2, tot2, tot2b, mid_par, diag, own1, rec1, tot1)
    tot1b = everywhere(sums1b)
    fg = call(
        functools.partial(first_grad_kernel, count),
        "first_grad",
        grid,
        [block2, block2, block2, sum2, sum2, par2],
        block2,
        half_b,
    )(sc, up1, own1, rec1, tot1, tot1b, mid_par)
    fg_rec = over_core(fg)
    input_blocks = [None] * nz
    for d in list(range(1, nz)) + [0]:
        block = call(
            input_grad_kernel,
            "input_grad",
            grid,
            [
                block2,
                block2,
                pl.BlockSpec((1, step, cb), lambda i, s, d=d: (d, i, 0)),
            ]
            + [pl.BlockSpec((1, cb, QW), lambda i, s, d=d: (d, 0, 0))] * NQ,
            rowc,
            sds((rows, cb), BF),
            [quarters_s],
            flops=big // nz,
        )(sc, fg, fg_rec, up3, *reduce_q)
        input_blocks[d] = over_z(block, -d) if d else block
    input_grad = place(input_blocks)

    full2 = whole((2, rows, QW))
    quarters_full = pltpu.VMEM((NQ, rows, QW), BF)
    expand_parts = call(
        functools.partial(expand_wgrad_kernel, nz),
        "expand_wgrad",
        (1,),
        [full2, full2, whole((nz, rows, cb))],
        [we] * NQ,
        [sds((nz, QW, cb), BF)] * NQ,
        [quarters_full],
        flops=big,
    )(sc, sa, sa_rec, eg)
    reduce_parts = call(
        functools.partial(reduce_wgrad_kernel, nz),
        "reduce_wgrad",
        (1,),
        [full2, full2] + [whole((rows, cb))] * nz,
        [wr] * NQ,
        [sds((nz, cb, QW), BF)] * NQ,
        [quarters_full],
        flops=big,
    )(sc, fg, fg_rec, *pixels)
    conv_part = call(
        functools.partial(conv_wgrad_kernel, images),
        "conv_wgrad",
        (2,),
        [per_h, per_h],
        pl.BlockSpec((1, 9, GW, QW), lambda i, s: (i, 0, 0, 0)),
        sds((2, 9, GW, QW), F32),
        [pad_s],
        flops=big,
    )(sc, act, cg)

    def low_sum(mine, others):
        total = mine.astype(F32)
        for value in others:
            total = total + value.astype(F32)
        return total

    def home(parts):
        total = low_sum(parts[0], [over_dp(parts[k], k) for k in range(1, NQ)])
        low = total.astype(BF)
        total = low_sum(total[0], [over_z(low[d], -d) for d in range(1, nz)])
        k = NQ
        while k < nd:
            total = low_sum(total, [over_dp(total.astype(BF), k)])
            k *= 2
        low = total.astype(BF)
        pieces = [low] + [over_dp(low, k) for k in range(1, NQ)]
        result = []
        for q in range(NQ):
            k = p ^ q
            value = pieces[NQ - 1]
            for j in range(NQ - 1):
                value = jnp.where(k == j, pieces[j], value)
            result.append(value.astype(F32))
        return result

    blocks = [(a, c, 2 * c + a // zh, (a % zh) * mb) for a in range(nz) for c in range(2)]
    expand_home = home(expand_parts)
    expand_wgrad = jnp.concatenate([expand_home[q][s : s + mb] for _, _, q, s in blocks], axis=0)
    reduce_home = home(reduce_parts)
    reduce_wgrad = jnp.concatenate([reduce_home[q][:, s : s + mb] for _, _, q, s in blocks], axis=1)

    conv_all = conv_part.transpose(1, 2, 0, 3).reshape(taps_rows, nz, mb).transpose(1, 0, 2)
    conv_low_part = conv_all.astype(BF)

    def conv_at(d):
        return lax.dynamic_index_in_dim(conv_low_part, (z + d) % nz, 0, keepdims=False)

    conv_total = low_sum(conv_at(0), [over_z(conv_at(d), d) for d in range(1, nz)])
    k = 1
    while k < nd:
        low = conv_total.astype(BF)
        conv_total = low_sum(low, [over_dp(low, k)])
        k *= 2
    group_wgrad = conv_total.reshape(group_weight.shape)

    def my_mid(total):
        lanes = lax.dynamic_slice_in_dim(total.transpose(1, 0, 2).reshape(2, 2 * QW), z * mb, mb, 1)
        return [lanes[1], lanes[0]]

    mid_grads = jnp.stack(my_mid(tot1b) + my_mid(tot2b))
    mine3 = lax.dynamic_index_in_dim(tot3b, z, 0, keepdims=False)
    out_grads = jnp.stack([mine3[1], mine3[0]])

    local_sq = jnp.zeros((), F32)
    for grad_item in (reduce_wgrad, group_wgrad, expand_wgrad, mid_grads, out_grads):
        local_sq = local_sq + jnp.sum(grad_item * grad_item)
    total_sq = jnp.broadcast_to(local_sq, (8, 128))
    k = 1
    while k < ng:
        total_sq = total_sq + lax.ppermute(total_sq, "group", [(a, a ^ k) for a in range(ng)])
        k *= 2
    grad_norm = jnp.sqrt(total_sq[0, 0])
    clip_scale = jnp.minimum(1.0, clip_norm / (grad_norm + 1e-06))
    reduce_out = adam_step(
        reduce_weight,
        reduce_wgrad * clip_scale,
        reduce_first,
        reduce_second,
        1.0 / jnp.sqrt(1.0 * CIN),
        0.1,
    )
    group_out = adam_step(
        group_weight,
        group_wgrad * clip_scale,
        group_first,
        group_second,
        1.0 / jnp.sqrt(9.0 * GW),
        0.1,
    )
    expand_out = adam_step(
        expand_weight,
        expand_wgrad * clip_scale,
        expand_first,
        expand_second,
        1.0 / jnp.sqrt(1.0 * MID),
        0.1,
    )
    mid_out = adam_step(mid_norms, mid_grads * clip_scale, mid_first, mid_second, 0.5, 0.0)
    out_out = adam_step(out_norms, out_grads * clip_scale, out_first, out_second, 0.5, 0.0)
    return (
        output,
        input_grad,
        grad_norm,
        *reduce_out,
        *group_out,
        *expand_out,
        *mid_out,
        *out_out,
    )


def solution(mesh):
    images = P("dp", None, None, "group")
    rows, cols = P("group", None), P(None, "group")
    kernel = P(None, None, None, "group")
    in_specs = (
        (images, P("dp", None), images) + (rows,) * 3 + (kernel,) * 3 + (cols,) * 3 + (cols,) * 6
    )
    out_specs = (images, images, P()) + (rows,) * 4 + (kernel,) * 4 + (cols,) * 4 + (cols,) * 8
    return jax.shard_map(shards, mesh=mesh, in_specs=in_specs, out_specs=out_specs, check_vma=False)
```

```python
import functools

import jax
import jax.numpy as jnp
from jax import lax
from jax.experimental import pallas as pl
from jax.experimental.pallas import tpu as pltpu
from jax.sharding import PartitionSpec as P

CIN = 2048
GW = 32
HW = 7
STEP = 10
MID = 1024
SRC = 9
NQ = 4
QW = MID // NQ
SPOTS = HW * HW

norm_eps = 1e-05
adam_eps = 1e-08
clip_norm = 1.0
moment_decay = 0.5

GELU_K = 0.7978845608028654
GELU_C = 0.044715
BF = jnp.bfloat16
F32 = jnp.float32


def dot(a, b):
    return jnp.dot(a, b, preferred_element_type=F32)


def dot_t(a, b):
    return lax.dot_general(a, b, (((1,), (1,)), ((), ())), preferred_element_type=F32)


def dot_rows(a, b):
    return lax.dot_general(a, b, (((0,), (0,)), ((), ())), preferred_element_type=F32)


def gelu(u):
    t = jnp.tanh(u * (GELU_K * GELU_C * (u * u) + GELU_K))
    return u * (0.5 * t + 0.5)


def gelu_both(u):
    u2 = u * u
    part = 0.5 * jnp.tanh(u * (GELU_K * GELU_C * u2 + GELU_K)) + 0.5
    bend = u * (6.0 * GELU_K * GELU_C * u2 + 2.0 * GELU_K)
    return u * part, part * (bend * (1.0 - part) + 1.0)


def norm_rows(total, squares, count):
    center = total / count
    spread = squares / count - center * center
    return center, lax.rsqrt(spread + norm_eps)


VMEM = pl.BlockSpec(memory_space=pltpu.VMEM)
SMEM = pl.BlockSpec(memory_space=pltpu.SMEM)
ANY = pl.BlockSpec(memory_space=pl.ANY)


def call(body, name, out_shape, *inputs, scratch=(), limit=8, specs=None, deps=(), **more):
    used, unused = len(inputs), len(deps)

    def inner(*refs):
        body(*refs[:used], *refs[used + unused :])

    return pl.pallas_call(
        inner,
        in_specs=(specs or [SMEM] + [VMEM] * (used - 1)) + [ANY] * unused,
        out_specs=more.pop("out_specs", jax.tree.map(lambda _: VMEM, out_shape)),
        out_shape=out_shape,
        scratch_shapes=list(scratch),
        compiler_params=pltpu.CompilerParams(vmem_limit_bytes=limit << 20),
        cost_estimate=pl.CostEstimate(flops=1024, bytes_accessed=1024, transcendentals=0),
        name=name,
        **more,
    )(*inputs, *deps)


def sds(shape, dtype):
    return jax.ShapeDtypeStruct(shape, dtype)


def tiles(rows, body, carry):
    size = 32 if rows % 32 == 0 else 16

    def step(i, c):
        return body(pl.ds(pl.multiple_of(i * size, size), size), c)

    return lax.fori_loop(0, rows // size, step, carry, unroll=7)


def fold(x):
    return jnp.sum(x.reshape(x.shape[0] // 8, 8, x.shape[1]), axis=0)


def no_sums(width):
    return (jnp.zeros((8, width), F32), jnp.zeros((8, width), F32))


def put_sums(sums, index, pair):
    rows = jnp.concatenate([jnp.sum(v, axis=0, keepdims=True) for v in pair], axis=0)
    sums[pl.ds(index, 1)] = rows[None]


def own_at(sc, h):
    return 2 * sc[1] + h


def other_at(sc, h):
    return 2 * (1 - sc[1]) + h


def source_at(sc, nz, d):
    return lax.rem(sc[2] + (nz - d), nz)


def lanes_of(refs):
    return jnp.concatenate([r[...] for r in refs], axis=1)


def four(sc, own, rec):
    return [own.at[0], own.at[1], rec.at[0], rec.at[1]]


def four_at(sc):
    return [own_at(sc, 0), own_at(sc, 1), other_at(sc, 0), other_at(sc, 1)]


def split3(x):
    high = x.astype(BF)
    rest = x - high.astype(F32)
    middle = rest.astype(BF)
    return high, middle, (rest - middle.astype(F32)).astype(BF)


def tap_spot(t, mb):
    parts = QW // mb
    each = -(-9 // parts)
    return (t % each) * 8, t // each * mb


def tap_lines(mb):
    lines = -(-9 // (QW // mb)) * 8
    return lines + lines % 16


def join_taps(cells, mb):
    each = tap_lines(mb) // 8
    empty = jnp.zeros((8, mb), F32)
    grid = [[empty] * (QW // mb) for _ in range(each)]
    for t, cell in enumerate(cells):
        line, lane = tap_spot(t, mb)
        grid[line // 8][lane // mb] = cell
    rows = [jnp.concatenate(row, axis=1) for row in grid]
    return jnp.concatenate(rows, axis=0).astype(BF)


def bundle_kernel(sc, reduce_piece, expand_piece, taps, norms, out):
    cb, mb = reduce_piece.shape[0], norms.shape[1]
    at = pl.ds(pl.multiple_of(sc[0] * 8, 8), 8)
    tail = cb + tap_lines(mb)
    out[:cb] = reduce_piece[...]
    out[cb:tail] = join_taps([taps[t, at] for t in range(9)], mb)
    parts = [v.astype(F32) for v in split3(norms[...])]
    empty = jnp.zeros((8, mb), F32)
    grid = [[empty] * (QW // mb) for _ in range(2)]
    for t, part in enumerate(parts):
        grid[t * mb // QW][t * mb % QW // mb] = part
    rows = [jnp.concatenate(row, axis=1) for row in grid]
    out[tail : tail + 16] = jnp.concatenate(rows, axis=0).astype(BF)
    for t in range(QW // cb):
        out[tail + 16 :, t * cb : (t + 1) * cb] = expand_piece[t * cb : (t + 1) * cb]


def stack_kernel(lines, *refs):
    reduce_part, expand_part = refs[-2:]
    cb = expand_part.shape[2]
    for d, ref in enumerate(refs[:-2]):
        reduce_part[0, d] = ref[:lines]
        expand_part[0, d] = ref[lines:]


def pair_kernel(a, b, out):
    out[0] = a[0]
    out[1] = b[0]


def spread_kernel(nz, sc, *refs):
    (a0, a1, a2), (b0, b2, b1) = refs[:3], refs[3:6]
    reduce_w, expand_w, diag, mid_par, out_par, taps, norms = refs[6:]
    firsts = [a0.at[0], a1.at[0], a2.at[0], a2.at[1]]
    seconds = [b0.at[0], b1.at[0], b2.at[0], b1.at[1]]
    cb, mb = reduce_w.shape[2], norms.shape[2]
    tail = cb + tap_lines(mb)
    for d in range(nz):
        zs = source_at(sc, nz, d)
        for k in range(NQ):
            q = sc[0] ^ k
            reduce_w[q, d] = firsts[k][d, :cb]
            for t in range(QW // cb):
                expand_w[q, d, t * cb : (t + 1) * cb] = seconds[k][d, :, t * cb : (t + 1) * cb]
            block = firsts[k][d, cb:tail].astype(F32)
            at = pl.ds(pl.multiple_of(q * 8, 8), 8)
            for t in range(9):
                line, lane = tap_spot(t, mb)
                taps[zs, t, at] = block[line : line + 8, lane : lane + mb]
        block = firsts[0][d, tail : tail + 16].astype(F32)
        total = jnp.zeros((8, mb), F32)
        for t in range(3):
            line, lane = t * mb // QW * 8, t * mb % QW
            total = total + block[line : line + 8, lane : lane + mb]
        norms[zs] = total
    keep = group_mask()
    half = nz // 2
    for h in range(2):
        mine = range(h * half, (h + 1) * half)
        mid_par[h] = jnp.concatenate([norms[v][:4] for v in mine], axis=1)
        for t in range(9):
            cell = jnp.concatenate([taps[v, t] for v in mine], axis=1)
            full = jnp.concatenate([cell] * (QW // GW), axis=0)
            diag[h, t] = jnp.where(keep, full, 0.0).astype(BF)
    per = cb // mb
    for v in range(nz):
        lines = norms[v]
        out_par[v] = jnp.concatenate(
            [
                jnp.concatenate([lines[4 + r * per + j : 5 + r * per + j] for j in range(per)], axis=1)
                for r in range(2)
            ],
            axis=0,
        )


def group_mask():
    group_row = lax.broadcasted_iota(jnp.int32, (QW, QW), 0) // GW
    group_col = lax.broadcasted_iota(jnp.int32, (QW, QW), 1) // GW
    return group_row == group_col


def cut_kernel(nz, d, sc, cot, out, sem):
    images = out.shape[1]
    start = pl.multiple_of(lax.rem(sc[2] + d, nz) * images, images)
    copy = pltpu.make_async_copy(cot.at[:, pl.ds(start, images)], out, sem)
    copy.start()
    copy.wait()


def pick_kernel(k, sc, parts, out):
    out[...] = parts[sc[0] ^ k]


def pick_both_kernel(nz, k, sc, parts, taps, out):
    q, cb = sc[0] ^ k, parts.shape[2]
    for d in range(nz):
        out[d, :cb] = parts[q, d]
        out[d, cb:] = taps[q, source_at(sc, nz, d)]


def total_kernel(*refs):
    total = refs[0][...].astype(F32)
    for ref in refs[1:-1]:
        total = total + ref[...].astype(F32)
    refs[-1][...] = total.astype(refs[-1].dtype)


def home_kernel(nz, sc, *refs):
    parts, outs = refs[:NQ], refs[NQ:]
    for d in range(nz):
        total = parts[0][d].astype(F32)
        for k in range(1, NQ):
            total = total + parts[k][d].astype(F32)
        outs[d][...] = total.astype(outs[d].dtype)


def pick3(masks, values):
    return masks[0] * values[0] + masks[1] * values[1] + masks[2] * values[2]


def crop_kernel(nz, d, sc, src, off, out):
    images, lanes = out.shape[1:]
    start = pl.multiple_of(lax.rem(sc[2] + d, nz) * images, images)
    at = pl.ds(start, images)
    row = jnp.broadcast_to(off[at, 0:1], (images, 128))
    col = jnp.broadcast_to(off[at, 1:2], (images, 128))
    row_masks = [(row == a).astype(F32).astype(BF) for a in range(3)]
    col_masks = [(col == a).astype(F32).astype(BF) for a in range(3)]
    for base in range(0, lanes, 128):
        span = slice(base, base + 128)
        lines = []
        for i in range(SRC):
            cells = [src[i, j, at, span] for j in range(SRC)]
            lines.append([pick3(col_masks, cells[j : j + 3]) for j in range(HW)])
            if i >= 2:
                for j in range(HW):
                    cell = pick3(row_masks, [line[j] for line in lines[i - 2 : i + 1]])
                    out[(i - 2) * HW + j, :, span] = cell


def reduce_kernel(nz, sc, *refs):
    xs, (w, own, other) = refs[:nz], refs[nz:]
    x = lanes_of(xs)
    for h in range(2):
        own[h] = dot(x, w[own_at(sc, h)].reshape(x.shape[1], QW))
        other[h] = dot(x, w[other_at(sc, h)].reshape(x.shape[1], QW)).astype(BF)


def first_sums_kernel(sc, own, rec, sums):
    for h in range(2):

        def body(at, c):
            v = own[h, at] + rec[h, at].astype(F32)
            return c[0] + fold(v), c[1] + fold(v * v)

        put_sums(sums, h, tiles(own.shape[1], body, no_sums(QW)))


def zero_border(pad, images):
    span = pad.shape[1]
    pad[0] = jnp.zeros_like(pad[0])
    pad[SRC - 1] = jnp.zeros_like(pad[0])
    edge = jnp.zeros((HW, images, pad.shape[2]), pad.dtype)
    pad[1 : HW + 1, 0:images] = edge
    pad[1 : HW + 1, span - images : span] = edge


def each_cell(images, body, carry):
    def line(i, c):
        for j in range(HW):
            at = pl.ds(pl.multiple_of((i * HW + j) * images, images), images)
            c = body(i, j, at, c)
        return c

    return lax.fori_loop(0, HW, line, carry)


def conv_kernel(count, images, sc, own, rec, tot, par, diag, act, v2, sums, pad):
    rows = HW * images
    zero_border(pad, images)
    for h in range(2):
        center, inv = norm_rows(tot[h, 0:1], tot[h, 1:2], count)
        gain, shift = par[h, 0:1], par[h, 1:2]

        def fill(i, j, at, c):
            v = own[h, at] + rec[h, at].astype(F32)
            a = gelu((v - center) * inv * gain + shift).astype(BF)
            act[h, at] = a
            pad[i + 1, (j + 1) * images : (j + 2) * images] = a
            return c

        each_cell(images, fill, 0)

        def taps(i, c):
            acc = jnp.zeros((rows, QW), F32)
            for di in range(3):
                line = pad.at[i + di]
                for dj in range(3):
                    acc = acc + dot(line[dj * images : dj * images + rows], diag[h, di * 3 + dj])
            v2[h, pl.ds(pl.multiple_of(i * rows, rows), rows)] = acc
            return c[0] + fold(acc), c[1] + fold(acc * acc)

        put_sums(sums, h, lax.fori_loop(0, HW, taps, no_sums(QW)))


def second_act_kernel(count, sc, v2, tot, par, out):
    for h in range(2):
        center, inv = norm_rows(tot[h, 0:1], tot[h, 1:2], count)
        gain, shift = par[h, 2:3], par[h, 3:4]

        def body(at, c):
            out[h, at] = gelu((v2[h, at] - center) * inv * gain + shift).astype(BF)
            return c

        tiles(v2.shape[1], body, 0)


def expand_kernel(nz, sc, own, rec, w, e, sums):
    x = lanes_of(four(sc, own, rec))
    for d in range(nz):
        e[d] = dot(x, jnp.concatenate([w[k, d] for k in four_at(sc)], axis=0))

        def body(at, c):
            v = e[d, at]
            return c[0] + fold(v), c[1] + fold(v * v)

        put_sums(sums, source_at(sc, nz, d), tiles(e.shape[1], body, no_sums(e.shape[2])))


def up_kernel(nz, count, sc, e, tot, par, *refs):
    xs, cots = refs[:nz], refs[nz : 2 * nz]
    outs, (up, sums) = refs[2 * nz : 3 * nz], refs[3 * nz :]
    for d in range(nz):
        zs = source_at(sc, nz, d)
        t = tot[zs]
        center, inv = norm_rows(t[0:1], t[1:2], count)
        gain, shift = par[zs, 0:1], par[zs, 1:2]

        def body(at, c):
            hat = (e[d, at] - center) * inv
            value, slope = gelu_both(hat * gain + shift + xs[d][at].astype(F32))
            outs[d][at] = value.astype(BF)
            u = cots[d][at].astype(F32) * slope
            up[d, at] = u
            return c[0] + fold(u), c[1] + fold(u * hat)

        put_sums(sums, zs, tiles(e.shape[1], body, no_sums(e.shape[2])))


def add_kernel(a, b, out):
    out[...] = a[...] + b[...]


def pass_kernel(value, out):
    out[...] = value[...]


def expand_back_kernel(nz, count, sc, e, up, tot, tot_b, par, w, eg, own, other):
    for d in range(nz):
        zs = source_at(sc, nz, d)
        t, b = tot[zs], tot_b[zs]
        center, inv = norm_rows(t[0:1], t[1:2], count)
        factor, mean_d, mean_x = inv * par[zs, 0:1], b[0:1] / count, b[1:2] / count

        def body(at, c):
            hat = (e[d, at] - center) * inv
            eg[d, at] = (factor * (up[d, at] - mean_d - hat * mean_x)).astype(BF)
            return c

        tiles(e.shape[1], body, 0)
    grads = lanes_of([eg.at[d] for d in range(nz)])
    for h in range(2):
        for index, out in ((own_at(sc, h), own), (other_at(sc, h), other)):
            out[h] = dot_t(grads, lanes_of([w.at[index, d] for d in range(nz)])).astype(out.dtype)


def second_up_kernel(count, sc, own, rec, v2, tot, par, up, sums):
    for h in range(2):
        center, inv = norm_rows(tot[h, 0:1], tot[h, 1:2], count)
        gain, shift = par[h, 2:3], par[h, 3:4]

        def body(at, c):
            hat = (v2[h, at] - center) * inv
            u = (own[h, at] + rec[h, at].astype(F32)) * gelu_both(hat * gain + shift)[1]
            up[h, at] = u
            return c[0] + fold(u), c[1] + fold(u * hat)

        put_sums(sums, h, tiles(v2.shape[1], body, no_sums(QW)))


def conv_back_kernel(
    count, images, sc, up2, v2, tot2, tot2b, par, diag, own, rec, tot1, cg, up1, sums, pad, temp
):
    rows = HW * images
    zero_border(pad, images)
    for h in range(2):
        center2, inv2 = norm_rows(tot2[h, 0:1], tot2[h, 1:2], count)
        factor = inv2 * par[h, 2:3]
        mean_d, mean_x = tot2b[h, 0:1] / count, tot2b[h, 1:2] / count

        def fill(i, j, at, c):
            hat = (v2[h, at] - center2) * inv2
            g = (factor * (up2[h, at] - mean_d - hat * mean_x)).astype(BF)
            cg[h, at] = g
            pad[i + 1, (j + 1) * images : (j + 2) * images] = g
            return c

        each_cell(images, fill, 0)
        center, inv = norm_rows(tot1[h, 0:1], tot1[h, 1:2], count)
        gain, shift = par[h, 0:1], par[h, 1:2]

        def taps(i, c):
            acc = jnp.zeros((rows, QW), F32)
            for di in range(3):
                line = pad.at[i + 2 - di]
                for dj in range(3):
                    start = (2 - dj) * images
                    acc = acc + dot_t(line[start : start + rows], diag[h, di * 3 + dj])
            temp[...] = acc
            for j in range(HW):
                at = pl.ds(pl.multiple_of(i * rows + j * images, images), images)
                hat = (own[h, at] + rec[h, at].astype(F32) - center) * inv
                u = temp[j * images : (j + 1) * images] * gelu_both(hat * gain + shift)[1]
                up1[h, at] = u
                c = (c[0] + fold(u), c[1] + fold(u * hat))
            return c

        put_sums(sums, h, lax.fori_loop(0, HW, taps, no_sums(QW)))


def first_grad_kernel(count, sc, up1, own, rec, tot, tot_b, par, out):
    for h in range(2):
        center, inv = norm_rows(tot[h, 0:1], tot[h, 1:2], count)
        factor = inv * par[h, 0:1]
        mean_d, mean_x = tot_b[h, 0:1] / count, tot_b[h, 1:2] / count

        def body(at, c):
            hat = (own[h, at] + rec[h, at].astype(F32) - center) * inv
            out[h, at] = (factor * (up1[h, at] - mean_d - hat * mean_x)).astype(BF)
            return c

        tiles(up1.shape[1], body, 0)


def input_grad_kernel(d, sc, own, rec, up, w, out):
    weights = lanes_of([w.at[k, d] for k in four_at(sc)])
    out[...] = (up[d] + dot_t(lanes_of(four(sc, own, rec)), weights)).astype(BF)


def reduce_wgrad_kernel(nz, sc, own, rec, *refs):
    xs, out = refs[:nz], refs[nz]
    grads = lanes_of(four(sc, own, rec))
    for d in range(nz):
        g = dot_rows(xs[d][...], grads).astype(BF)
        for j, k in enumerate(four_at(sc)):
            out[k, d] = g[:, j * QW : (j + 1) * QW]


def expand_wgrad_kernel(nz, sc, own, rec, eg, out):
    width = eg.shape[2]
    grads = lanes_of([eg.at[d] for d in range(nz)])
    for ref, k in zip(four(sc, own, rec), four_at(sc)):
        g = dot_rows(ref[...], grads).astype(BF)
        for d in range(nz):
            out[k, d] = g[:, d * width : (d + 1) * width]


def conv_wgrad_kernel(images, mb, sc, act, cg, out, pad):
    rows = HW * images
    keep = group_mask()
    zero_border(pad, images)
    for h in range(2):
        for i in range(HW):
            pad[i + 1, images : images + rows] = act[h, i * rows : (i + 1) * rows]
        grad = cg[h]
        cells = []
        for di in range(3):
            for dj in range(3):
                window = pad[di : di + HW, dj * images : dj * images + rows]
                full = dot_rows(window.reshape(HW * rows, QW), grad)
                full = jnp.where(keep, full, 0.0)
                cells.append(jnp.sum(full.reshape(QW // GW, GW, QW), axis=0))
        for q in range(NQ):
            for a in range(QW // mb):
                pieces = [c[q * 8 : q * 8 + 8, a * mb : (a + 1) * mb] for c in cells]
                out[q, h * (QW // mb) + a] = join_taps(pieces, mb)


def square_sum(x):
    return jnp.sum(x.reshape(x.shape[0] // 8, 8, x.shape[1]), axis=0)


def lane_fold(x):
    return sum(x[:, j : j + 128] for j in range(0, x.shape[1], 128)) if x.shape[1] > 128 else x


def expand_home_kernel(nz, sc, *refs):
    parts, (grad, squares, whole) = refs[:NQ], refs[NQ:]
    rows = grad.shape[0] // (2 * nz)
    half = nz // 2
    for k in range(NQ):
        whole[sc[0] ^ k] = parts[k][...]
    total = jnp.zeros((8, 128), F32)
    for q in range(NQ):
        for a in range(half):
            g = whole[q, a * rows : (a + 1) * rows].astype(F32)
            start = (((q % 2) * half + a) * 2 + q // 2) * rows
            grad[start : start + rows] = g
            total = total + lane_fold(square_sum(g * g))
    squares[...] = total


def reduce_home_kernel(nz, sc, *refs):
    parts, (mid, out, before) = refs[:NQ], refs[NQ : NQ + 3]
    grad, taps, squares, whole = refs[NQ + 3 :]
    cb, mb = grad.shape[0], taps.shape[2]
    half = nz // 2
    for k in range(NQ):
        whole[sc[0] ^ k] = parts[k][...]
    total = before[...]
    for q in range(NQ):
        for a in range(half):
            start = (((q % 2) * half + a) * 2 + q // 2) * mb
            grad[:, start : start + mb] = whole[q, :cb, a * mb : (a + 1) * mb].astype(F32)
        block = whole[q, cb:].astype(F32)
        for t in range(9):
            line, lane = tap_spot(t, mb)
            taps[t, q * 8 : (q + 1) * 8] = block[line : line + 8, lane : lane + mb]
        full = whole[q].astype(F32)
        total = total + lane_fold(square_sum(full * full))
    extra = jnp.sum(mid[...] * mid[...]) + jnp.sum(out[...] * out[...])
    first = lax.broadcasted_iota(jnp.int32, (8, 128), 0) + lax.broadcasted_iota(
        jnp.int32, (8, 128), 1
    )
    total = total + jnp.where(first == 0, extra, 0.0)
    squares[...] = jnp.broadcast_to(jnp.sum(total, keepdims=True), (8, 128))


def place_kernel(nz, d, sc, block, *refs):
    out, sem = refs[-2:]
    images = block.shape[1]
    start = pl.multiple_of(lax.rem(sc[2] + d, nz) * images, images)
    copy = pltpu.make_async_copy(block, out.at[:, pl.ds(start, images)], sem)
    copy.start()
    copy.wait()


def adam_step(weight, gradient, momentum, variance, learn_rate, decay_rate):
    momentum_new = moment_decay * momentum + (1.0 - moment_decay) * gradient
    variance_new = moment_decay * variance + (1.0 - moment_decay) * gradient * gradient
    correction = 1.0 - moment_decay**STEP
    direction = momentum_new / correction / (jnp.sqrt(variance_new / correction) + adam_eps)
    weight_new = weight - learn_rate * (direction + decay_rate * weight)
    return (weight_new, momentum_new, variance_new, weight_new.astype(BF))


def shards(
    source,
    offsets,
    cotangent,
    reduce_weight,
    reduce_first,
    reduce_second,
    group_weight,
    group_first,
    group_second,
    expand_weight,
    expand_first,
    expand_second,
    mid_norms,
    mid_first,
    mid_second,
    out_norms,
    out_first,
    out_second,
):
    nd, ng = lax.axis_size("dp"), lax.axis_size("group")
    nz = ng // 2
    gi = lax.axis_index("group")
    z, core = gi // 2, gi % 2
    p = lax.axis_index("dp") % NQ
    sc = jnp.stack([p, core, z]).astype(jnp.int32)
    n = source.shape[0]
    images = n // nz
    rows = SPOTS * images
    cb = source.shape[3]
    mb = group_weight.shape[3]
    zh = nz // 2
    count = float(SPOTS * n * nd)

    def over_z(value, d):
        pairs = [(2 * a + c, 2 * ((a + d) % nz) + c) for a in range(nz) for c in range(2)]
        return lax.ppermute(value, "group", pairs)

    def over_core(value):
        return lax.ppermute(value, "group", [(a, a ^ 1) for a in range(ng)])

    def over_dp(value, k):
        return lax.ppermute(value, "dp", [(a, a ^ k) for a in range(nd)])

    def over_all_dp(value, *pins):
        k = 1
        while k < nd:
            other = over_dp(value, k)
            k *= 2
            if k < nd or not pins:
                value = value + other
            else:
                value = call(
                    add_kernel,
                    "add",
                    sds(value.shape, F32),
                    value,
                    other,
                    specs=[VMEM] * 2,
                    deps=pins,
                )
        return value

    def over_all_z(value):
        k = 2
        while k < ng:
            value = value + lax.ppermute(value, "group", [(a, a ^ k) for a in range(ng)])
            k *= 2
        return value

    def everywhere(value, *pins):
        return over_all_z(over_all_dp(value, *pins))

    src = source.transpose(1, 2, 0, 3)
    crops = []
    order = [1] + list(range(2, nz))[::-1] + [0]
    for d in order:
        crop = call(
            functools.partial(crop_kernel, nz, d),
            "crop",
            sds((SPOTS, images, cb), BF),
            sc,
            src,
            offsets,
            deps=crops[-1:],
        ).reshape(rows, cb)
        crops.append(crop)
    pixels = [over_z(crops[order.index(d)], d) if d else crops[-1] for d in range(nz)]

    col_starts = [((p % 2) * zh + j) * 2 * mb + (p // 2) * mb for j in range(zh)]
    reduce_piece = jnp.concatenate(
        [lax.dynamic_slice_in_dim(reduce_weight, s, mb, 1) for s in col_starts], axis=1
    ).astype(BF)
    expand_piece = (
        lax.dynamic_slice(
            expand_weight.reshape(nz, 2, mb, cb),
            ((p % 2) * zh, p // 2, 0, 0),
            (zh, 1, mb, cb),
        )
        .reshape(QW, cb)
        .astype(BF)
    )

    pack = jnp.concatenate([mid_norms, out_norms.reshape(-1, mb)], axis=0)
    bundle = call(
        bundle_kernel,
        "bundle",
        sds((2 * cb + tap_lines(mb) + 16, QW), BF),
        sc,
        reduce_piece,
        expand_piece,
        group_weight.reshape(9, GW, mb),
        pack,
        deps=crops[:1],
    )
    bundles = [bundle] + [over_z(bundle, d) for d in range(1, nz)]

    lines = cb + tap_lines(mb) + 16
    first_w, second_w = call(
        functools.partial(stack_kernel, lines),
        "stack",
        [sds((1, nz, lines, QW), BF), sds((1, nz, cb, QW), BF)],
        *bundles,
        specs=[VMEM] * nz,
        deps=[crops[-1], pixels[1]],
    )

    def pair(a, b):
        shape = sds((2,) + a.shape[1:], BF)
        return call(pair_kernel, "pair", shape, a, b, specs=[VMEM] * 2, deps=[pixels[-1]])

    first_x, second_y = over_dp(first_w, 1), over_dp(second_w, 2)
    first_y, second_x = (
        over_dp(pair(first_w, first_x), 2),
        over_dp(pair(second_w, second_y), 1),
    )
    reduce_q, expand_q, diag, mid_par, out_par = call(
        functools.partial(spread_kernel, nz),
        "spread",
        [
            sds((NQ, nz, cb, QW), BF),
            sds((NQ, nz, QW, cb), BF),
            sds((2, 9, QW, QW), BF),
            sds((2, 4, QW), F32),
            sds((nz, 2, cb), F32),
        ],
        sc,
        first_w,
        first_x,
        first_y,
        second_w,
        second_y,
        second_x,
        scratch=[pltpu.VMEM((nz, 9, GW, mb), F32), pltpu.VMEM((nz, 8, mb), F32)],
    )

    cot = cotangent.transpose(1, 2, 0, 3).reshape(SPOTS, n, cb)

    def cut(d, *deps):
        piece = call(
            functools.partial(cut_kernel, nz, d),
            "cut",
            sds((SPOTS, images, cb), BF),
            sc,
            cot,
            specs=[SMEM, ANY],
            scratch=[pltpu.SemaphoreType.DMA],
            deps=deps,
        ).reshape(rows, cb)
        return piece

    def turn(d):
        return 0 if d == 1 else (1 if d == nz - 1 else 2)

    half_f, half_b = sds((2, rows, QW), F32), sds((2, rows, QW), BF)
    sum2_s, sumz_s = sds((2, 2, QW), F32), sds((nz, 2, cb), F32)
    pad_s = pltpu.VMEM((SRC, SRC * images, QW), BF)

    own1, oth1 = call(
        functools.partial(reduce_kernel, nz),
        "reduce",
        [half_f, half_b],
        sc,
        *pixels,
        reduce_q,
        limit=16,
        deps=[diag, mid_par, out_par, expand_q],
    )
    rec1 = over_core(oth1)
    turns = [[d for d in range(1, nz) if turn(d) == t] for t in range(3)]
    cots = [cut(0, diag)] + [None] * (nz - 1)

    def send_cots(t, *deps):
        pieces = [cut(d, *deps) for d in turns[t]]
        for d, piece in zip(turns[t], pieces):
            cots[d] = over_z(piece, d)
        return pieces, [cots[d] for d in turns[t]]

    sent, pins = send_cots(0, oth1)
    sums1 = call(first_sums_kernel, "first_sums", sum2_s, sc, own1, rec1, deps=sent)
    tot1 = everywhere(sums1, *pins)
    sent, pins = send_cots(1, tot1)
    act, v2, sums2 = call(
        functools.partial(conv_kernel, count, images),
        "conv",
        [half_b, half_f, sum2_s],
        sc,
        own1,
        rec1,
        tot1,
        mid_par,
        diag,
        scratch=[pad_s],
        deps=sent,
    )
    tot2 = everywhere(sums2, *pins)
    sent, pins = send_cots(2, tot2)
    sa = call(
        functools.partial(second_act_kernel, count),
        "second_act",
        half_b,
        sc,
        v2,
        tot2,
        mid_par,
        deps=sent,
    )
    sa_rec = over_core(sa)
    e, sums3 = call(
        functools.partial(expand_kernel, nz),
        "expand",
        [sds((nz, rows, cb), F32), sumz_s],
        sc,
        sa,
        sa_rec,
        expand_q,
        limit=12,
    )
    tot3 = everywhere(sums3)
    res = call(
        functools.partial(up_kernel, nz, count),
        "up",
        [sds((rows, cb), BF)] * nz + [sds((nz, rows, cb), F32), sumz_s],
        sc,
        e,
        tot3,
        out_par,
        *pixels,
        *cots,
    )
    values, up3, sums3b = res[:nz], res[nz], res[nz + 1]
    part3b = over_all_z(sums3b)
    tot3b = over_all_dp(part3b)
    outs = list(values)

    def later(value, *deps):
        return call(
            pass_kernel, "pass", sds(value.shape, value.dtype), value, specs=[VMEM], deps=deps
        )

    def place(blocks, *deps):
        result = None
        for d in range(nz):
            extra = () if result is None else (result,)
            result = call(
                functools.partial(place_kernel, nz, d),
                "place",
                sds((SPOTS, n, cb), BF),
                sc,
                blocks[d].reshape(SPOTS, images, cb),
                *extra,
                specs=[SMEM, VMEM] + [ANY] * len(extra),
                out_specs=ANY,
                scratch=[pltpu.SemaphoreType.DMA],
                input_output_aliases={2: 0} if extra else {},
                deps=deps,
            )
        return result.reshape(HW, HW, n, cb).transpose(2, 0, 1, 3)

    def send_outs(t, *deps):
        pieces = [later(values[d], *deps) for d in turns[t]]
        for d, piece in zip(turns[t], pieces):
            outs[d] = over_z(piece, -d)
        return pieces, [outs[d] for d in turns[t]]

    sent, pins = send_outs(0, part3b)
    eg, own2, oth2 = call(
        functools.partial(expand_back_kernel, nz, count),
        "expand_back",
        [sds((nz, rows, cb), BF), half_f, half_b],
        sc,
        e,
        up3,
        tot3,
        tot3b,
        out_par,
        expand_q,
        deps=sent,
    )
    rec2 = over_core(oth2)
    up2, sums2b = call(
        functools.partial(second_up_kernel, count),
        "second_up",
        [half_f, sum2_s],
        sc,
        own2,
        rec2,
        v2,
        tot2,
        mid_par,
    )
    mid2b = over_all_dp(sums2b, *pins)
    tot2b = over_all_z(mid2b)
    sent, pins = send_outs(1, tot2b)
    cg, up1, sums1b = call(
        functools.partial(conv_back_kernel, count, images),
        "conv_back",
        [half_b, half_f, sum2_s],
        sc,
        up2,
        v2,
        tot2,
        tot2b,
        mid_par,
        diag,
        own1,
        rec1,
        tot1,
        scratch=[pad_s, pltpu.VMEM((HW * images, QW), F32)],
        deps=sent,
    )
    tot1b = everywhere(sums1b, *pins)
    sent, _ = send_outs(2, tot1b)
    fg = call(
        functools.partial(first_grad_kernel, count),
        "first_grad",
        half_b,
        sc,
        up1,
        own1,
        rec1,
        tot1,
        tot1b,
        mid_par,
        deps=sent,
    )
    fg_rec = over_core(fg)
    def input_block(d, *deps):
        return call(
            functools.partial(input_grad_kernel, d),
            "input_grad",
            sds((rows, cb), BF),
            sc,
            fg,
            fg_rec,
            up3,
            reduce_q,
            deps=deps,
        )

    expand_parts = call(
        functools.partial(expand_wgrad_kernel, nz),
        "expand_wgrad",
        sds((NQ, nz, QW, cb), BF),
        sc,
        sa,
        sa_rec,
        eg,
        limit=12,
    )
    first = input_block(2)
    conv_parts = call(
        functools.partial(conv_wgrad_kernel, images, mb),
        "conv_wgrad",
        sds((NQ, nz, tap_lines(mb), QW), BF),
        sc,
        act,
        cg,
        scratch=[pad_s],
        deps=[first],
    )
    reduce_parts = call(
        functools.partial(reduce_wgrad_kernel, nz),
        "reduce_wgrad",
        sds((NQ, nz, cb, QW), BF),
        sc,
        fg,
        fg_rec,
        *pixels,
        limit=12,
        deps=[conv_parts],
    )
    reduce_picks = [
        call(
            functools.partial(pick_both_kernel, nz, k),
            "pick_both",
            sds((nz, cb + tap_lines(mb), QW), BF),
            sc,
            reduce_parts,
            conv_parts,
            deps=[outs[d] for d in turns[2]],
        )
        for k in range(NQ)
    ]
    input_blocks = {2: first}
    last = reduce_picks[-1]
    for d in [d for d in range(1, nz) if d != 2] + [0]:
        last = input_block(d, last)
        input_blocks[d] = last
    input_moved = [over_z(input_blocks[d], -d) if d else input_blocks[0] for d in range(nz)]

    def low_sum(mine, others):
        total = mine.astype(F32)
        for value in others:
            total = total + value.astype(F32)
        return total

    def picks(parts, *deps):
        return [
            call(
                functools.partial(pick_kernel, k),
                "pick",
                sds(parts.shape[1:], BF),
                sc,
                parts,
                deps=deps,
            )
            for k in range(NQ)
        ]

    def home(parts, deps, pins):
        shape = parts[0].shape[1:]
        pieces = call(
            functools.partial(home_kernel, nz),
            "home",
            [sds(shape, F32)] + [sds(shape, BF)] * (nz - 1),
            sc,
            parts[0],
            *[over_dp(parts[k], k) for k in range(1, NQ)],
            deps=deps,
        )
        low = call(
            total_kernel,
            "total",
            sds(shape, BF),
            pieces[0],
            *[over_z(pieces[d], -d) for d in range(1, nz)],
            specs=[VMEM] * nz,
            deps=pins,
        )
        k = NQ
        while k < nd:
            low = low_sum(low, [over_dp(low, k)]).astype(BF)
            k *= 2
        return [low] + [over_dp(low, k) for k in range(1, NQ)]

    expand_pieces = home(picks(expand_parts, mid2b), [last], [])
    expand_wgrad, squares = call(
        functools.partial(expand_home_kernel, nz),
        "expand_home",
        [sds((MID, cb), F32), sds((8, 128), F32)],
        sc,
        *expand_pieces,
        scratch=[pltpu.VMEM((NQ, QW, cb), BF)],
    )
    reduce_pieces = home(
        reduce_picks,
        [input_moved[2], last, squares],
        [input_moved[d] for d in range(1, nz) if d not in (2, nz - 1)],
    )
    input_grad = place(input_moved)
    output = place(outs, last)

    def my_mid(total):
        lanes = lax.dynamic_slice_in_dim(total.transpose(1, 0, 2).reshape(2, 2 * QW), z * mb, mb, 1)
        return [lanes[1], lanes[0]]

    mid_grads = jnp.stack(my_mid(tot1b) + my_mid(tot2b))
    mine3 = lax.dynamic_index_in_dim(tot3b, z, 0, keepdims=False)
    out_grads = jnp.stack([mine3[1], mine3[0]])

    reduce_wgrad, tap_grad, total_sq = call(
        functools.partial(reduce_home_kernel, nz),
        "reduce_home",
        [sds((cb, MID), F32), sds((9, GW, mb), F32), sds((8, 128), F32)],
        sc,
        *reduce_pieces,
        mid_grads,
        out_grads,
        squares,
        scratch=[pltpu.VMEM((NQ, cb + tap_lines(mb), QW), BF)],
    )
    group_wgrad = tap_grad.reshape(group_weight.shape)
    k = 1
    while k < ng:
        total_sq = total_sq + lax.ppermute(total_sq, "group", [(a, a ^ k) for a in range(ng)])
        k *= 2
    grad_norm = jnp.sqrt(total_sq[0, 0])
    clip_scale = jnp.minimum(1.0, clip_norm / (grad_norm + 1e-06))
    reduce_out = adam_step(
        reduce_weight,
        reduce_wgrad * clip_scale,
        reduce_first,
        reduce_second,
        1.0 / jnp.sqrt(1.0 * CIN),
        0.1,
    )
    group_out = adam_step(
        group_weight,
        group_wgrad * clip_scale,
        group_first,
        group_second,
        1.0 / jnp.sqrt(9.0 * GW),
        0.1,
    )
    expand_out = adam_step(
        expand_weight,
        expand_wgrad * clip_scale,
        expand_first,
        expand_second,
        1.0 / jnp.sqrt(1.0 * MID),
        0.1,
    )
    mid_out = adam_step(mid_norms, mid_grads * clip_scale, mid_first, mid_second, 0.5, 0.0)
    out_out = adam_step(out_norms, out_grads * clip_scale, out_first, out_second, 0.5, 0.0)
    return (
        output,
        input_grad,
        grad_norm,
        *reduce_out,
        *group_out,
        *expand_out,
        *mid_out,
        *out_out,
    )


def solution(mesh):
    images = P("dp", None, None, "group")
    rows, cols = P("group", None), P(None, "group")
    kernel = P(None, None, None, "group")
    in_specs = (
        (images, P("dp", None), images) + (rows,) * 3 + (kernel,) * 3 + (cols,) * 3 + (cols,) * 6
    )
    out_specs = (images, images, P()) + (rows,) * 4 + (kernel,) * 4 + (cols,) * 4 + (cols,) * 8
    return jax.shard_map(shards, mesh=mesh, in_specs=in_specs, out_specs=out_specs, check_vma=False)
```

```python
import functools

import jax
import jax.numpy as jnp
from jax import lax
from jax.experimental import pallas as pl
from jax.experimental.pallas import tpu as pltpu
from jax.sharding import PartitionSpec as P

CIN = 2048
GW = 32
HW = 7
STEP = 10
MID = 1024
SRC = 9
NQ = 4
QW = MID // NQ
SPOTS = HW * HW

norm_eps = 1e-05
adam_eps = 1e-08
clip_norm = 1.0
moment_decay = 0.5

GELU_K = 0.7978845608028654
GELU_C = 0.044715
BF = jnp.bfloat16
F32 = jnp.float32


def dot(a, b):
    return jnp.dot(a, b, preferred_element_type=F32)


def dot_t(a, b):
    return lax.dot_general(a, b, (((1,), (1,)), ((), ())), preferred_element_type=F32)


def dot_rows(a, b):
    return lax.dot_general(a, b, (((0,), (0,)), ((), ())), preferred_element_type=F32)


def gelu(u):
    t = jnp.tanh(u * (GELU_K * GELU_C * (u * u) + GELU_K))
    return u * (0.5 * t + 0.5)


def gelu_both(u):
    u2 = u * u
    part = 0.5 * jnp.tanh(u * (GELU_K * GELU_C * u2 + GELU_K)) + 0.5
    bend = u * (6.0 * GELU_K * GELU_C * u2 + 2.0 * GELU_K)
    return u * part, part * (bend * (1.0 - part) + 1.0)


def norm_rows(total, squares, count):
    center = total / count
    spread = squares / count - center * center
    return center, lax.rsqrt(spread + norm_eps)


VMEM = pl.BlockSpec(memory_space=pltpu.VMEM)
SMEM = pl.BlockSpec(memory_space=pltpu.SMEM)
ANY = pl.BlockSpec(memory_space=pl.ANY)


def call(body, name, out_shape, *inputs, scratch=(), limit=8, specs=None, deps=(), **more):
    used, unused = len(inputs), len(deps)

    def inner(*refs):
        body(*refs[:used], *refs[used + unused :])

    return pl.pallas_call(
        inner,
        in_specs=(specs or [SMEM] + [VMEM] * (used - 1)) + [ANY] * unused,
        out_specs=more.pop("out_specs", jax.tree.map(lambda _: VMEM, out_shape)),
        out_shape=out_shape,
        scratch_shapes=list(scratch),
        compiler_params=pltpu.CompilerParams(vmem_limit_bytes=limit << 20),
        cost_estimate=pl.CostEstimate(flops=1024, bytes_accessed=1024, transcendentals=0),
        name=name,
        **more,
    )(*inputs, *deps)


def sds(shape, dtype):
    return jax.ShapeDtypeStruct(shape, dtype)


def tiles(rows, body, carry):
    size = 32 if rows % 32 == 0 else 16

    def step(i, c):
        return body(pl.ds(pl.multiple_of(i * size, size), size), c)

    trips = rows // size
    unroll = max(u for u in range(1, 9) if trips % u == 0)
    return lax.fori_loop(0, trips, step, carry, unroll=unroll)


def fold(x):
    return jnp.sum(x.reshape(x.shape[0] // 8, 8, x.shape[1]), axis=0)


def no_sums(width):
    return (jnp.zeros((8, width), F32), jnp.zeros((8, width), F32))


def put_sums(sums, index, pair):
    rows = jnp.concatenate([jnp.sum(v, axis=0, keepdims=True) for v in pair], axis=0)
    sums[pl.ds(index, 1)] = rows[None]


def own_at(sc, h):
    return 2 * sc[1] + h


def other_at(sc, h):
    return 2 * (1 - sc[1]) + h


def source_at(sc, nz, d):
    return lax.rem(sc[2] + (nz - d), nz)


def lanes_of(refs):
    return jnp.concatenate([r[...] for r in refs], axis=1)


def four(sc, own, rec):
    return [own.at[0], own.at[1], rec.at[0], rec.at[1]]


def four_at(sc):
    return [own_at(sc, 0), own_at(sc, 1), other_at(sc, 0), other_at(sc, 1)]


def split3(x):
    high = x.astype(BF)
    rest = x - high.astype(F32)
    middle = rest.astype(BF)
    return high, middle, (rest - middle.astype(F32)).astype(BF)


def tap_spot(t, mb):
    parts = QW // mb
    each = -(-9 // parts)
    return (t % each) * 8, t // each * mb


def tap_lines(mb):
    lines = -(-9 // (QW // mb)) * 8
    return lines + lines % 16


def join_taps(cells, mb):
    each = tap_lines(mb) // 8
    empty = jnp.zeros((8, mb), F32)
    grid = [[empty] * (QW // mb) for _ in range(each)]
    for t, cell in enumerate(cells):
        line, lane = tap_spot(t, mb)
        grid[line // 8][lane // mb] = cell
    rows = [jnp.concatenate(row, axis=1) for row in grid]
    return jnp.concatenate(rows, axis=0).astype(BF)


def bundle_kernel(sc, reduce_piece, expand_piece, taps, norms, out):
    cb, mb = reduce_piece.shape[0], norms.shape[1]
    at = pl.ds(pl.multiple_of(sc[0] * 8, 8), 8)
    tail = cb + tap_lines(mb)
    out[:cb] = reduce_piece[...]
    out[cb:tail] = join_taps([taps[t, at] for t in range(9)], mb)
    parts = [v.astype(F32) for v in split3(norms[...])]
    empty = jnp.zeros((8, mb), F32)
    grid = [[empty] * (QW // mb) for _ in range(2)]
    for t, part in enumerate(parts):
        grid[t * mb // QW][t * mb % QW // mb] = part
    rows = [jnp.concatenate(row, axis=1) for row in grid]
    out[tail : tail + 16] = jnp.concatenate(rows, axis=0).astype(BF)
    for t in range(QW // cb):
        out[tail + 16 :, t * cb : (t + 1) * cb] = expand_piece[t * cb : (t + 1) * cb]


def stack_kernel(lines, *refs):
    reduce_part, expand_part = refs[-2:]
    for d, ref in enumerate(refs[:-2]):
        reduce_part[0, d] = ref[:lines]
        expand_part[0, d] = ref[lines:]


def pair_kernel(a, b, out):
    out[0] = a[...].reshape(out.shape[1:])
    out[1] = b[...].reshape(out.shape[1:])


def spread_kernel(nz, sc, *refs):
    (a0, a1, a2), (b0, b2, b1) = refs[:3], refs[3:6]
    reduce_w, expand_w, diag, mid_par, out_par, taps, norms = refs[6:]
    firsts = [a0.at[0], a1.at[0], a2.at[0], a2.at[1]]
    seconds = [b0.at[0], b1.at[0], b2.at[0], b1.at[1]]
    cb, mb = reduce_w.shape[2], norms.shape[2]
    tail = cb + tap_lines(mb)
    for d in range(nz):
        zs = source_at(sc, nz, d)
        for k in range(NQ):
            q = sc[0] ^ k
            reduce_w[q, d] = firsts[k][d, :cb]
            for t in range(QW // cb):
                expand_w[q, d, t * cb : (t + 1) * cb] = seconds[k][d, :, t * cb : (t + 1) * cb]
            block = firsts[k][d, cb:tail].astype(F32)
            at = pl.ds(pl.multiple_of(q * 8, 8), 8)
            for t in range(9):
                line, lane = tap_spot(t, mb)
                taps[zs, t, at] = block[line : line + 8, lane : lane + mb]
        block = firsts[0][d, tail : tail + 16].astype(F32)
        total = jnp.zeros((8, mb), F32)
        for t in range(3):
            line, lane = t * mb // QW * 8, t * mb % QW
            total = total + block[line : line + 8, lane : lane + mb]
        norms[zs] = total
    keep = group_mask()
    half = nz // 2
    for h in range(2):
        mine = range(h * half, (h + 1) * half)
        mid_par[h] = jnp.concatenate([norms[v][:4] for v in mine], axis=1)
        for t in range(9):
            cell = jnp.concatenate([taps[v, t] for v in mine], axis=1)
            full = jnp.concatenate([cell] * (QW // GW), axis=0)
            diag[h, t] = jnp.where(keep, full, 0.0).astype(BF)
    per = cb // mb
    for v in range(nz):
        lines = norms[v]
        out_par[v] = jnp.concatenate(
            [
                jnp.concatenate([lines[4 + r * per + j : 5 + r * per + j] for j in range(per)], axis=1)
                for r in range(2)
            ],
            axis=0,
        )


def group_mask():
    group_row = lax.broadcasted_iota(jnp.int32, (QW, QW), 0) // GW
    group_col = lax.broadcasted_iota(jnp.int32, (QW, QW), 1) // GW
    return group_row == group_col


def cut_kernel(nz, d, low, sc, cot, out, sem):
    spots, images = out.shape[:2]
    start = pl.multiple_of(lax.rem(sc[2] + d, nz) * images, images)
    copy = pltpu.make_async_copy(cot.at[low : low + spots, pl.ds(start, images)], out, sem)
    copy.start()
    copy.wait()


def pick_kernel(nz, k, sc, parts, *refs):
    q, out = sc[0] ^ k, refs[-1]
    cb = parts.shape[2]
    for d in range(nz):
        out[d, :cb] = parts[q, d]
        for taps in refs[:-1]:
            out[d, cb:] = taps[q, source_at(sc, nz, d)]


def total_kernel(*refs):
    total = refs[0][...].astype(F32)
    for ref in refs[1:-1]:
        total = total + ref[...].astype(F32)
    refs[-1][...] = total.astype(refs[-1].dtype)


def home_kernel(nz, sc, *refs):
    parts, outs = refs[:NQ], refs[NQ:]
    for d in range(nz):
        total = parts[0][d].astype(F32)
        for k in range(1, NQ):
            total = total + parts[k][d].astype(F32)
        outs[d][...] = total.astype(outs[d].dtype)


def pick3(masks, values):
    return masks[0] * values[0] + masks[1] * values[1] + masks[2] * values[2]


def crop_kernel(nz, d, sc, src, off, out):
    images, lanes = out.shape[1:]
    start = pl.multiple_of(lax.rem(sc[2] + d, nz) * images, images)
    at = pl.ds(start, images)
    row = jnp.broadcast_to(off[at, 0:1], (images, 128))
    col = jnp.broadcast_to(off[at, 1:2], (images, 128))
    row_masks = [(row == a).astype(F32).astype(BF) for a in range(3)]
    col_masks = [(col == a).astype(F32).astype(BF) for a in range(3)]
    for base in range(0, lanes, 128):
        span = slice(base, base + 128)
        lines = []
        for i in range(SRC):
            cells = [src[i, j, at, span] for j in range(SRC)]
            lines.append([pick3(col_masks, cells[j : j + 3]) for j in range(HW)])
            if i >= 2:
                for j in range(HW):
                    cell = pick3(row_masks, [line[j] for line in lines[i - 2 : i + 1]])
                    out[(i - 2) * HW + j, :, span] = cell


def reduce_kernel(nz, sc, *refs):
    xs, (w, own, other) = refs[:nz], refs[nz:]
    x = lanes_of(xs)
    for h in range(2):
        own[h] = dot(x, w[own_at(sc, h)].reshape(x.shape[1], QW))
        other[h] = dot(x, w[other_at(sc, h)].reshape(x.shape[1], QW)).astype(BF)


def first_sums_kernel(sc, own, rec, sums):
    for h in range(2):

        def body(at, c):
            v = own[h, at] + rec[h, at].astype(F32)
            return c[0] + fold(v), c[1] + fold(v * v)

        put_sums(sums, h, tiles(own.shape[1], body, no_sums(QW)))


def zero_border(pad, images):
    span = pad.shape[1]
    pad[0] = jnp.zeros_like(pad[0])
    pad[SRC - 1] = jnp.zeros_like(pad[0])
    edge = jnp.zeros((HW, images, pad.shape[2]), pad.dtype)
    pad[1 : HW + 1, 0:images] = edge
    pad[1 : HW + 1, span - images : span] = edge


def each_cell(images, body, carry):
    def line(i, c):
        for j in range(HW):
            at = pl.ds(pl.multiple_of((i * HW + j) * images, images), images)
            c = body(i, j, at, c)
        return c

    return lax.fori_loop(0, HW, line, carry)


def conv_kernel(count, images, sc, own, rec, tot, par, diag, act, v2, sums, pad):
    rows = HW * images
    zero_border(pad, images)
    for h in range(2):
        center, inv = norm_rows(tot[h, 0:1], tot[h, 1:2], count)
        gain, shift = par[h, 0:1], par[h, 1:2]

        def fill(i, j, at, c):
            v = own[h, at] + rec[h, at].astype(F32)
            a = gelu((v - center) * inv * gain + shift).astype(BF)
            act[h, at] = a
            pad[i + 1, (j + 1) * images : (j + 2) * images] = a
            return c

        each_cell(images, fill, 0)

        def taps(i, c):
            acc = jnp.zeros((rows, QW), F32)
            for di in range(3):
                line = pad.at[i + di]
                for dj in range(3):
                    acc = acc + dot(line[dj * images : dj * images + rows], diag[h, di * 3 + dj])
            v2[h, pl.ds(pl.multiple_of(i * rows, rows), rows)] = acc
            return c[0] + fold(acc), c[1] + fold(acc * acc)

        put_sums(sums, h, lax.fori_loop(0, HW, taps, no_sums(QW)))


def second_act_kernel(count, sc, v2, tot, par, out):
    for h in range(2):
        center, inv = norm_rows(tot[h, 0:1], tot[h, 1:2], count)
        gain, shift = par[h, 2:3], par[h, 3:4]

        def body(at, c):
            out[h, at] = gelu((v2[h, at] - center) * inv * gain + shift).astype(BF)
            return c

        tiles(v2.shape[1], body, 0)


def expand_kernel(nz, sc, own, rec, w, e, sums):
    x = lanes_of(four(sc, own, rec))
    for d in range(nz):
        e[d] = dot(x, jnp.concatenate([w[k, d] for k in four_at(sc)], axis=0))

        def body(at, c):
            v = e[d, at]
            return c[0] + fold(v), c[1] + fold(v * v)

        put_sums(sums, source_at(sc, nz, d), tiles(e.shape[1], body, no_sums(e.shape[2])))


def up_kernel(nz, count, pieces, earlier, sc, e, tot, par, *refs):
    many = len(pieces)
    xs, refs = refs[:many], refs[many:]
    cots, refs = refs[: sum(pieces.values())], refs[sum(pieces.values()) + 2 * earlier :]
    outs, (up, sums) = refs[:many], refs[many:]
    used = 0
    for j, d in enumerate(pieces):
        zs = source_at(sc, nz, d)
        t = tot[zs]
        center, inv = norm_rows(t[0:1], t[1:2], count)
        gain, shift = par[zs, 0:1], par[zs, 1:2]
        base = 0
        pair = no_sums(e.shape[2])
        for cot in cots[used : used + pieces[d]]:

            def body(local, c):
                size = local.size
                at = pl.ds(pl.multiple_of(local.start + base, size), size)
                hat = (e[d, at] - center) * inv
                value, slope = gelu_both(hat * gain + shift + xs[j][at].astype(F32))
                outs[j][at] = value.astype(BF)
                u = cot[local].astype(F32) * slope
                up[d, at] = u
                return c[0] + fold(u), c[1] + fold(u * hat)

            pair = tiles(cot.shape[0], body, pair)
            base += cot.shape[0]
        used += pieces[d]
        put_sums(sums, zs, pair)


def add_kernel(a, b, out):
    out[...] = a[...] + b[...]


def pass_kernel(low, value, out):
    out[...] = value[low : low + out.shape[0]]


def expand_back_kernel(nz, count, sc, e, up, tot, tot_b, par, w, eg, own, other):
    for d in range(nz):
        zs = source_at(sc, nz, d)
        t, b = tot[zs], tot_b[zs]
        center, inv = norm_rows(t[0:1], t[1:2], count)
        factor, mean_d, mean_x = inv * par[zs, 0:1], b[0:1] / count, b[1:2] / count

        def body(at, c):
            hat = (e[d, at] - center) * inv
            eg[d, at] = (factor * (up[d, at] - mean_d - hat * mean_x)).astype(BF)
            return c

        tiles(e.shape[1], body, 0)
    grads = lanes_of([eg.at[d] for d in range(nz)])
    for h in range(2):
        for index, out in ((own_at(sc, h), own), (other_at(sc, h), other)):
            out[h] = dot_t(grads, lanes_of([w.at[index, d] for d in range(nz)])).astype(out.dtype)


def second_up_kernel(count, sc, own, rec, v2, tot, par, up, sums):
    for h in range(2):
        center, inv = norm_rows(tot[h, 0:1], tot[h, 1:2], count)
        gain, shift = par[h, 2:3], par[h, 3:4]

        def body(at, c):
            hat = (v2[h, at] - center) * inv
            u = (own[h, at] + rec[h, at].astype(F32)) * gelu_both(hat * gain + shift)[1]
            up[h, at] = u
            return c[0] + fold(u), c[1] + fold(u * hat)

        put_sums(sums, h, tiles(v2.shape[1], body, no_sums(QW)))


def conv_back_kernel(
    count, images, sc, up2, v2, tot2, tot2b, par, diag, own, rec, tot1, cg, up1, sums, pad, temp
):
    rows = HW * images
    zero_border(pad, images)
    for h in range(2):
        center2, inv2 = norm_rows(tot2[h, 0:1], tot2[h, 1:2], count)
        factor = inv2 * par[h, 2:3]
        mean_d, mean_x = tot2b[h, 0:1] / count, tot2b[h, 1:2] / count

        def fill(i, j, at, c):
            hat = (v2[h, at] - center2) * inv2
            g = (factor * (up2[h, at] - mean_d - hat * mean_x)).astype(BF)
            cg[h, at] = g
            pad[i + 1, (j + 1) * images : (j + 2) * images] = g
            return c

        each_cell(images, fill, 0)
        center, inv = norm_rows(tot1[h, 0:1], tot1[h, 1:2], count)
        gain, shift = par[h, 0:1], par[h, 1:2]

        def taps(i, c):
            acc = jnp.zeros((rows, QW), F32)
            for di in range(3):
                line = pad.at[i + 2 - di]
                for dj in range(3):
                    start = (2 - dj) * images
                    acc = acc + dot_t(line[start : start + rows], diag[h, di * 3 + dj])
            temp[...] = acc
            for j in range(HW):
                at = pl.ds(pl.multiple_of(i * rows + j * images, images), images)
                hat = (own[h, at] + rec[h, at].astype(F32) - center) * inv
                u = temp[j * images : (j + 1) * images] * gelu_both(hat * gain + shift)[1]
                up1[h, at] = u
                c = (c[0] + fold(u), c[1] + fold(u * hat))
            return c

        put_sums(sums, h, lax.fori_loop(0, HW, taps, no_sums(QW)))


def first_grad_kernel(count, sc, up1, own, rec, tot, tot_b, par, out):
    for h in range(2):
        center, inv = norm_rows(tot[h, 0:1], tot[h, 1:2], count)
        factor = inv * par[h, 0:1]
        mean_d, mean_x = tot_b[h, 0:1] / count, tot_b[h, 1:2] / count

        def body(at, c):
            hat = (own[h, at] + rec[h, at].astype(F32) - center) * inv
            out[h, at] = (factor * (up1[h, at] - mean_d - hat * mean_x)).astype(BF)
            return c

        tiles(up1.shape[1], body, 0)


def input_grad_kernel(d, sc, own, rec, up, w, out):
    weights = lanes_of([w.at[k, d] for k in four_at(sc)])
    out[...] = (up[d] + dot_t(lanes_of(four(sc, own, rec)), weights)).astype(BF)


def reduce_wgrad_kernel(nz, sc, own, rec, *refs):
    xs, out = refs[:nz], refs[nz]
    grads = lanes_of(four(sc, own, rec))
    for d in range(nz):
        g = dot_rows(xs[d][...], grads).astype(BF)
        for j, k in enumerate(four_at(sc)):
            out[k, d] = g[:, j * QW : (j + 1) * QW]


def expand_wgrad_kernel(nz, sc, own, rec, eg, out):
    width = eg.shape[2]
    grads = lanes_of([eg.at[d] for d in range(nz)])
    for ref, k in zip(four(sc, own, rec), four_at(sc)):
        g = dot_rows(ref[...], grads).astype(BF)
        for d in range(nz):
            out[k, d] = g[:, d * width : (d + 1) * width]


def conv_wgrad_kernel(images, mb, sc, act, cg, out, pad):
    rows = HW * images
    keep = group_mask()
    zero_border(pad, images)
    for h in range(2):
        for i in range(HW):
            pad[i + 1, images : images + rows] = act[h, i * rows : (i + 1) * rows]
        grad = cg[h]
        cells = []
        for di in range(3):
            for dj in range(3):
                window = pad[di : di + HW, dj * images : dj * images + rows]
                full = dot_rows(window.reshape(HW * rows, QW), grad)
                full = jnp.where(keep, full, 0.0)
                cells.append(jnp.sum(full.reshape(QW // GW, GW, QW), axis=0))
        for q in range(NQ):
            for a in range(QW // mb):
                pieces = [c[q * 8 : q * 8 + 8, a * mb : (a + 1) * mb] for c in cells]
                out[q, h * (QW // mb) + a] = join_taps(pieces, mb)


def square_sum(x):
    return jnp.sum(x.reshape(x.shape[0] // 8, 8, x.shape[1]), axis=0)


def lane_fold(x):
    return sum(x[:, j : j + 128] for j in range(0, x.shape[1], 128)) if x.shape[1] > 128 else x


def grads_kernel(nz, sc, *refs):
    firsts, seconds, (mid, out) = refs[:NQ], refs[NQ : 2 * NQ], refs[2 * NQ : 2 * NQ + 2]
    expand, reduce, taps, squares, first, second = refs[2 * NQ + 2 :]
    cb, mb = reduce.shape[0], taps.shape[2]
    half = nz // 2
    for k in range(NQ):
        first[sc[0] ^ k] = firsts[k][...]
        second[sc[0] ^ k] = seconds[k][...]
    total = jnp.zeros((8, 128), F32)
    for q in range(NQ):
        for a in range(half):
            start = (((q % 2) * half + a) * 2 + q // 2) * mb
            piece = second[q, a * mb : (a + 1) * mb].astype(F32)
            expand[start : start + mb] = piece
            total = total + lane_fold(square_sum(piece * piece))
            piece = first[q, :cb, a * mb : (a + 1) * mb]
            reduce[:, start : start + mb] = piece.astype(F32)
        block = first[q, cb:].astype(F32)
        for t in range(9):
            line, lane = tap_spot(t, mb)
            taps[t, q * 8 : (q + 1) * 8] = block[line : line + 8, lane : lane + mb]
        full = first[q].astype(F32)
        total = total + lane_fold(square_sum(full * full))
    extra = jnp.sum(mid[...] * mid[...]) + jnp.sum(out[...] * out[...])
    corner = lax.broadcasted_iota(jnp.int32, (8, 128), 0) + lax.broadcasted_iota(
        jnp.int32, (8, 128), 1
    )
    total = total + jnp.where(corner == 0, extra, 0.0)
    squares[...] = jnp.broadcast_to(jnp.sum(total, keepdims=True), (8, 128))


def place_kernel(nz, d, low, sc, block, *refs):
    out, token, sem = refs[-3:]
    token[...] = jnp.zeros_like(token)
    spots, images = block.shape[:2]
    start = pl.multiple_of(lax.rem(sc[2] + d, nz) * images, images)
    copy = pltpu.make_async_copy(block, out.at[low : low + spots, pl.ds(start, images)], sem)
    copy.start()
    copy.wait()


def adam_step(weight, gradient, momentum, variance, learn_rate, decay_rate):
    momentum_new = moment_decay * momentum + (1.0 - moment_decay) * gradient
    variance_new = moment_decay * variance + (1.0 - moment_decay) * gradient * gradient
    correction = 1.0 - moment_decay**STEP
    direction = momentum_new / correction / (jnp.sqrt(variance_new / correction) + adam_eps)
    weight_new = weight - learn_rate * (direction + decay_rate * weight)
    return (weight_new, momentum_new, variance_new, weight_new.astype(BF))


def shards(
    source,
    offsets,
    cotangent,
    reduce_weight,
    reduce_first,
    reduce_second,
    group_weight,
    group_first,
    group_second,
    expand_weight,
    expand_first,
    expand_second,
    mid_norms,
    mid_first,
    mid_second,
    out_norms,
    out_first,
    out_second,
):
    nd, ng = lax.axis_size("dp"), lax.axis_size("group")
    nz = ng // 2
    gi = lax.axis_index("group")
    z, core = gi // 2, gi % 2
    p = lax.axis_index("dp") % NQ
    sc = jnp.stack([p, core, z]).astype(jnp.int32)
    n = source.shape[0]
    images = n // nz
    rows = SPOTS * images
    cb = source.shape[3]
    mb = group_weight.shape[3]
    zh = nz // 2
    count = float(SPOTS * n * nd)

    def over_z(value, d):
        pairs = [(2 * a + c, 2 * ((a + d) % nz) + c) for a in range(nz) for c in range(2)]
        return lax.ppermute(value, "group", pairs)

    def over_core(value):
        return lax.ppermute(value, "group", [(a, a ^ 1) for a in range(ng)])

    def over_dp(value, k):
        return lax.ppermute(value, "dp", [(a, a ^ k) for a in range(nd)])

    def over_all_dp(value, *pins):
        k = 1
        while k < nd:
            other = over_dp(value, k)
            k *= 2
            if k < nd or not pins:
                value = value + other
            else:
                value = call(
                    add_kernel,
                    "add",
                    sds(value.shape, F32),
                    value,
                    other,
                    specs=[VMEM] * 2,
                    deps=pins,
                )
        return value

    def over_all_z(value):
        k = 2
        while k < ng:
            value = value + lax.ppermute(value, "group", [(a, a ^ k) for a in range(ng)])
            k *= 2
        return value

    def everywhere(value, *pins):
        return over_all_z(over_all_dp(value, *pins))

    src = source.transpose(1, 2, 0, 3)
    crops = []
    order = [1] + list(range(2, nz))[::-1] + [0]
    for d in order:
        crop = call(
            functools.partial(crop_kernel, nz, d),
            "crop",
            sds((SPOTS, images, cb), BF),
            sc,
            src,
            offsets,
            deps=crops[-1:],
        ).reshape(rows, cb)
        crops.append(crop)
    pixels = [over_z(crops[order.index(d)], d) if d else crops[-1] for d in range(nz)]

    col_starts = [((p % 2) * zh + j) * 2 * mb + (p // 2) * mb for j in range(zh)]
    reduce_piece = jnp.concatenate(
        [lax.dynamic_slice_in_dim(reduce_weight, s, mb, 1) for s in col_starts], axis=1
    ).astype(BF)
    expand_piece = (
        lax.dynamic_slice(
            expand_weight.reshape(nz, 2, mb, cb),
            ((p % 2) * zh, p // 2, 0, 0),
            (zh, 1, mb, cb),
        )
        .reshape(QW, cb)
        .astype(BF)
    )

    pack = jnp.concatenate([mid_norms, out_norms.reshape(-1, mb)], axis=0)
    bundle = call(
        bundle_kernel,
        "bundle",
        sds((2 * cb + tap_lines(mb) + 16, QW), BF),
        sc,
        reduce_piece,
        expand_piece,
        group_weight.reshape(9, GW, mb),
        pack,
        deps=crops[:1],
    )

    lines = cb + tap_lines(mb) + 16
    parts = [sds((1, nz, lines, QW), BF), sds((1, nz, cb, QW), BF)]

    def pair(a, b, shape, *deps):
        return call(pair_kernel, "pair", sds((2,) + shape, BF), a, b, specs=[VMEM] * 2, deps=deps)

    first_w, second_w = call(
        functools.partial(stack_kernel, lines),
        "stack",
        parts,
        bundle,
        *[over_z(bundle, d) for d in range(1, nz)],
        specs=[VMEM] * nz,
        deps=[crops[-1], pixels[1]],
    )

    first_x, second_y = over_dp(first_w, 1), over_dp(second_w, 2)
    first_y, second_x = (
        over_dp(pair(first_w, first_x, first_w.shape[1:], pixels[-1]), 2),
        over_dp(pair(second_w, second_y, second_w.shape[1:], pixels[-1]), 1),
    )
    reduce_q, expand_q, diag, mid_par, out_par = call(
        functools.partial(spread_kernel, nz),
        "spread",
        [
            sds((NQ, nz, cb, QW), BF),
            sds((NQ, nz, QW, cb), BF),
            sds((2, 9, QW, QW), BF),
            sds((2, 4, QW), F32),
            sds((nz, 2, cb), F32),
        ],
        sc,
        first_w,
        first_x,
        first_y,
        second_w,
        second_y,
        second_x,
        scratch=[pltpu.VMEM((nz, 9, GW, mb), F32), pltpu.VMEM((nz, 8, mb), F32)],
    )

    cot = cotangent.transpose(1, 2, 0, 3).reshape(SPOTS, n, cb)

    def cut(d, low, high, *deps):
        return call(
            functools.partial(cut_kernel, nz, d, low),
            "cut",
            sds((high - low, images, cb), BF),
            sc,
            cot,
            specs=[SMEM, ANY],
            scratch=[pltpu.SemaphoreType.DMA],
            deps=deps,
        ).reshape((high - low) * images, cb)

    def turn(d):
        return 0 if d == 1 else (1 if d == nz - 1 else 2)

    half_f, half_b = sds((2, rows, QW), F32), sds((2, rows, QW), BF)
    sum2_s, sumz_s = sds((2, 2, QW), F32), sds((nz, 2, cb), F32)
    pad_s = pltpu.VMEM((SRC, SRC * images, QW), BF)

    own1, oth1 = call(
        functools.partial(reduce_kernel, nz),
        "reduce",
        [half_f, half_b],
        sc,
        *pixels,
        reduce_q,
        limit=16,
        deps=[diag, mid_par, out_par, expand_q],
    )
    rec1 = over_core(oth1)
    turns = [[d for d in range(1, nz) if turn(d) == t] for t in range(3)]
    split = SPOTS // 2
    cot_turns = [
        [(d, 0, SPOTS) for d in turns[0]],
        [(d, 0, SPOTS) for d in turns[1]],
        [(d, 0, split) for d in turns[2]],
        [(d, split, SPOTS) for d in turns[2]],
    ]
    cots = {0: [cut(0, 0, SPOTS, diag)]}

    def send_cots(t, *deps):
        pieces = [cut(*spot, *deps) for spot in cot_turns[t]]
        moved = [over_z(piece, spot[0]) for spot, piece in zip(cot_turns[t], pieces)]
        for spot, piece in zip(cot_turns[t], moved):
            cots.setdefault(spot[0], []).append(piece)
        return pieces, moved

    sent, pins = send_cots(0, oth1)
    sums1 = call(first_sums_kernel, "first_sums", sum2_s, sc, own1, rec1, deps=sent)
    tot1 = everywhere(sums1, *pins)
    sent, pins = send_cots(1, tot1)
    act, v2, sums2 = call(
        functools.partial(conv_kernel, count, images),
        "conv",
        [half_b, half_f, sum2_s],
        sc,
        own1,
        rec1,
        tot1,
        mid_par,
        diag,
        scratch=[pad_s],
        deps=sent,
    )
    tot2 = everywhere(sums2, *pins)
    sent, pins = send_cots(2, tot2)
    sent_more, last_cots = send_cots(3, tot2)
    sa = call(
        functools.partial(second_act_kernel, count),
        "second_act",
        half_b,
        sc,
        v2,
        tot2,
        mid_par,
        deps=sent + sent_more,
    )
    sa_rec = over_core(sa)
    e, sums3 = call(
        functools.partial(expand_kernel, nz),
        "expand",
        [sds((nz, rows, cb), F32), sumz_s],
        sc,
        sa,
        sa_rec,
        expand_q,
        limit=12,
    )
    tot3 = everywhere(sums3, *pins)
    def upward(ds, *earlier, deps=()):
        many = len(ds)
        pieces = {d: len(cots[d]) for d in ds}
        at = 4 + many + sum(pieces.values())
        res = call(
            functools.partial(up_kernel, nz, count, pieces, len(earlier) // 2),
            "up",
            [sds((rows, cb), BF)] * many + [sds((nz, rows, cb), F32), sumz_s],
            sc,
            e,
            tot3,
            out_par,
            *[pixels[d] for d in ds],
            *[piece for d in ds for piece in cots[d]],
            *earlier,
            input_output_aliases={at: many, at + 1: many + 1} if earlier else {},
            deps=deps,
        )
        return dict(zip(ds, res[:many])), res[many], res[many + 1]

    early, up3, sums3b = upward(turns[0], deps=last_cots)
    values, up3, sums3b = upward([d for d in range(nz) if d not in turns[0]], up3, sums3b)
    values.update(early)
    outs = [(0, 0, values[0])]

    def send_outs(t, *deps):
        pieces, moved = [], []
        for d, low, high in cot_turns[t]:
            piece = values[d]
            if deps:
                piece = call(
                    functools.partial(pass_kernel, low * images),
                    "pass",
                    sds(((high - low) * images, cb), BF),
                    piece,
                    specs=[VMEM],
                    deps=deps,
                )
            pieces.append(piece)
            moved.append(over_z(piece, -d))
            outs.append((d, low, moved[-1]))
        return pieces, moved

    sent, pins = send_outs(0)
    tot3b = everywhere(sums3b, *pins)

    def place(pieces, result=None, *deps):
        for d, low, piece in pieces:
            extra = () if result is None else (result,)
            result, token = call(
                functools.partial(place_kernel, nz, d, low),
                "place",
                [sds((SPOTS, n, cb), BF), sds((8, 128), F32)],
                sc,
                piece.reshape(-1, images, cb),
                *extra,
                specs=[SMEM, VMEM] + [ANY] * len(extra),
                out_specs=[ANY, VMEM],
                scratch=[pltpu.SemaphoreType.DMA],
                input_output_aliases={2: 0} if extra else {},
                deps=deps,
            )
        return result, token

    def to_images(result):
        return result.reshape(HW, HW, n, cb).transpose(2, 0, 1, 3)

    sent, pins = send_outs(1, tot3b)
    eg, own2, oth2 = call(
        functools.partial(expand_back_kernel, nz, count),
        "expand_back",
        [sds((nz, rows, cb), BF), half_f, half_b],
        sc,
        e,
        up3,
        tot3,
        tot3b,
        out_par,
        expand_q,
        deps=sent,
    )
    expand_parts = call(
        functools.partial(expand_wgrad_kernel, nz),
        "expand_wgrad",
        sds((NQ, nz, QW, cb), BF),
        sc,
        sa,
        sa_rec,
        eg,
        limit=12,
    )

    def pick(k, parts, *more, deps=()):
        return call(
            functools.partial(pick_kernel, nz, k),
            "pick",
            sds((nz, parts.shape[2] + sum(v.shape[2] for v in more), parts.shape[3]), BF),
            sc,
            parts,
            *more,
            deps=deps,
        )

    def gather_home(picks, deps=()):
        shape = picks[0].shape[1:]
        return call(
            functools.partial(home_kernel, nz),
            "home",
            [sds(shape, F32)] + [sds(shape, BF)] * (nz - 1),
            sc,
            picks[0],
            *[over_dp(picks[k], k) for k in range(1, NQ)],
            deps=deps,
        )

    def total_of(pieces, deps=()):
        low = call(
            total_kernel,
            "total",
            sds(pieces[0].shape, BF),
            pieces[0],
            *[over_z(pieces[d], -d) for d in range(1, nz)],
            specs=[VMEM] * nz,
            deps=deps,
        )
        k = NQ
        while k < nd:
            low = (low.astype(F32) + over_dp(low, k).astype(F32)).astype(BF)
            k *= 2
        return low

    def to_all_dp(low):
        return [low] + [over_dp(low, k) for k in range(1, NQ)]

    rec2 = over_core(oth2)
    up2, sums2b = call(
        functools.partial(second_up_kernel, count),
        "second_up",
        [half_f, sum2_s],
        sc,
        own2,
        rec2,
        v2,
        tot2,
        mid_par,
        deps=[expand_parts],
    )
    mid2b = over_all_dp(sums2b, *pins)
    tot2b = over_all_z(mid2b)
    sent, pins = send_outs(2, tot2b)
    expand_picks = [pick(k, expand_parts, deps=[mid2b]) for k in range(NQ)]
    expand_pieces = gather_home(expand_picks)
    pins.append(expand_pieces[0])
    cg, up1, sums1b = call(
        functools.partial(conv_back_kernel, count, images),
        "conv_back",
        [half_b, half_f, sum2_s],
        sc,
        up2,
        v2,
        tot2,
        tot2b,
        mid_par,
        diag,
        own1,
        rec1,
        tot1,
        scratch=[pad_s, pltpu.VMEM((HW * images, QW), F32)],
        deps=sent,
    )
    tot1b = everywhere(sums1b, *pins)
    fg = call(
        functools.partial(first_grad_kernel, count),
        "first_grad",
        half_b,
        sc,
        up1,
        own1,
        rec1,
        tot1,
        tot1b,
        mid_par,
    )
    fg_rec = over_core(fg)
    def input_block(d, *deps):
        return call(
            functools.partial(input_grad_kernel, d),
            "input_grad",
            sds((rows, cb), BF),
            sc,
            fg,
            fg_rec,
            up3,
            reduce_q,
            deps=deps,
        )

    first = input_block(2)
    reduce_parts = call(
        functools.partial(reduce_wgrad_kernel, nz),
        "reduce_wgrad",
        sds((NQ, nz, cb, QW), BF),
        sc,
        fg,
        fg_rec,
        *pixels,
        limit=12,
        deps=[first],
    )
    conv_parts = call(
        functools.partial(conv_wgrad_kernel, images, mb),
        "conv_wgrad",
        sds((NQ, nz, tap_lines(mb), QW), BF),
        sc,
        act,
        cg,
        scratch=[pad_s],
        deps=[reduce_parts],
    )
    expand_low = total_of(expand_pieces, [conv_parts])
    _, pins = send_outs(3, expand_low)

    def later(value, *deps):
        shape = sds(value.shape, value.dtype)
        body = functools.partial(pass_kernel, 0)
        return call(body, "pass", shape, value, specs=[VMEM], deps=deps)

    reduce_picks = [
        pick(k, reduce_parts, conv_parts, deps=[expand_low]) for k in range(NQ)
    ]
    final = nz - 1
    input_blocks = {2: later(first, expand_low)}
    last = reduce_picks[1]
    for d in list(range(3, nz)) + [1, 0]:
        last = input_block(d, last)
        input_blocks[d] = last
    output, token = place(outs)
    pieces = gather_home(reduce_picks, [last, token])

    expand_home = to_all_dp(later(expand_low, pieces[0]))
    moved = [(0, 0, input_blocks[0])]
    moved += [(d, 0, over_z(input_blocks[d], -d)) for d in range(2, final)]
    placed, token = place(moved)
    reduce_low = total_of(pieces, [token])
    reduce_home = to_all_dp(reduce_low)
    second = later(input_blocks[1], reduce_low)
    second_moved = over_z(second, -1)
    placed, _ = place([(1, 0, second_moved)], placed)

    def my_mid(total):
        lanes = lax.dynamic_slice_in_dim(total.transpose(1, 0, 2).reshape(2, 2 * QW), z * mb, mb, 1)
        return [lanes[1], lanes[0]]

    mid_grads = jnp.stack(my_mid(tot1b) + my_mid(tot2b))
    mine3 = lax.dynamic_index_in_dim(tot3b, z, 0, keepdims=False)
    out_grads = jnp.stack([mine3[1], mine3[0]])

    expand_wgrad, reduce_wgrad, tap_grad, total_sq = call(
        functools.partial(grads_kernel, nz),
        "grads",
        [
            sds((MID, cb), F32),
            sds((cb, MID), F32),
            sds((9, GW, mb), F32),
            sds((8, 128), F32),
        ],
        sc,
        *reduce_home,
        *expand_home,
        mid_grads,
        out_grads,
        scratch=[
            pltpu.VMEM((NQ, cb + tap_lines(mb), QW), BF),
            pltpu.VMEM((NQ, QW, cb), BF),
        ],
        deps=[second],
    )
    group_wgrad = tap_grad.reshape(group_weight.shape)
    total_sq = call(
        add_kernel,
        "add",
        sds((8, 128), F32),
        total_sq,
        over_core(total_sq),
        specs=[VMEM] * 2,
        deps=[second_moved],
    )
    total_sq = over_all_z(total_sq)
    moved = over_z(later(input_blocks[final], total_sq), -final)
    input_grad, _ = place([(final, 0, moved)], placed)
    grad_norm = jnp.sqrt(total_sq[0, 0])
    clip_scale = jnp.minimum(1.0, clip_norm / (grad_norm + 1e-06))
    reduce_out = adam_step(
        reduce_weight,
        reduce_wgrad * clip_scale,
        reduce_first,
        reduce_second,
        1.0 / jnp.sqrt(1.0 * CIN),
        0.1,
    )
    group_out = adam_step(
        group_weight,
        group_wgrad * clip_scale,
        group_first,
        group_second,
        1.0 / jnp.sqrt(9.0 * GW),
        0.1,
    )
    expand_out = adam_step(
        expand_weight,
        expand_wgrad * clip_scale,
        expand_first,
        expand_second,
        1.0 / jnp.sqrt(1.0 * MID),
        0.1,
    )
    mid_out = adam_step(mid_norms, mid_grads * clip_scale, mid_first, mid_second, 0.5, 0.0)
    out_out = adam_step(out_norms, out_grads * clip_scale, out_first, out_second, 0.5, 0.0)
    return (
        to_images(output),
        to_images(input_grad),
        grad_norm,
        *reduce_out,
        *group_out,
        *expand_out,
        *mid_out,
        *out_out,
    )


def solution(mesh):
    images = P("dp", None, None, "group")
    rows, cols = P("group", None), P(None, "group")
    kernel = P(None, None, None, "group")
    in_specs = (
        (images, P("dp", None), images) + (rows,) * 3 + (kernel,) * 3 + (cols,) * 3 + (cols,) * 6
    )
    out_specs = (images, images, P()) + (rows,) * 4 + (kernel,) * 4 + (cols,) * 4 + (cols,) * 8
    return jax.shard_map(shards, mesh=mesh, in_specs=in_specs, out_specs=out_specs, check_vma=False)
```

```python
import functools

import jax
import jax.numpy as jnp
from jax import lax
from jax.experimental import pallas as pl
from jax.experimental.pallas import tpu as pltpu
from jax.sharding import PartitionSpec as P

CIN = 2048
GW = 32
HW = 7
STEP = 10
MID = 1024
SRC = 9
NQ = 4
QW = MID // NQ
SPOTS = HW * HW

norm_eps = 1e-05
adam_eps = 1e-08
clip_norm = 1.0
moment_decay = 0.5

GELU_K = 0.7978845608028654
GELU_C = 0.044715
BF = jnp.bfloat16
F32 = jnp.float32


def dot(a, b):
    return jnp.dot(a, b, preferred_element_type=F32)


def dot_t(a, b):
    return lax.dot_general(a, b, (((1,), (1,)), ((), ())), preferred_element_type=F32)


def dot_rows(a, b):
    return lax.dot_general(a, b, (((0,), (0,)), ((), ())), preferred_element_type=F32)


def gelu(u):
    t = jnp.tanh(u * (GELU_K * GELU_C * (u * u) + GELU_K))
    return u * (0.5 * t + 0.5)


def gelu_both(u):
    u2 = u * u
    part = 0.5 * jnp.tanh(u * (GELU_K * GELU_C * u2 + GELU_K)) + 0.5
    bend = u * (6.0 * GELU_K * GELU_C * u2 + 2.0 * GELU_K)
    return u * part, part * (bend * (1.0 - part) + 1.0)


def norm_rows(total, squares, count):
    center = total / count
    spread = squares / count - center * center
    return center, lax.rsqrt(spread + norm_eps)


VMEM = pl.BlockSpec(memory_space=pltpu.VMEM)
SMEM = pl.BlockSpec(memory_space=pltpu.SMEM)
ANY = pl.BlockSpec(memory_space=pl.ANY)


def call(body, name, out_shape, *inputs, scratch=(), limit=8, specs=None, deps=(), **more):
    used, unused = len(inputs), len(deps)

    def inner(*refs):
        body(*refs[:used], *refs[used + unused :])

    return pl.pallas_call(
        inner,
        in_specs=(specs or [SMEM] + [VMEM] * (used - 1)) + [ANY] * unused,
        out_specs=more.pop("out_specs", jax.tree.map(lambda _: VMEM, out_shape)),
        out_shape=out_shape,
        scratch_shapes=list(scratch),
        compiler_params=pltpu.CompilerParams(vmem_limit_bytes=limit << 20),
        cost_estimate=pl.CostEstimate(flops=1024, bytes_accessed=1024, transcendentals=0),
        name=name,
        **more,
    )(*inputs, *deps)


def sds(shape, dtype):
    return jax.ShapeDtypeStruct(shape, dtype)


def tiles(rows, body, carry):
    size = 32 if rows % 32 == 0 else 16

    def step(i, c):
        return body(pl.ds(pl.multiple_of(i * size, size), size), c)

    trips = rows // size
    unroll = max(u for u in range(1, 9) if trips % u == 0)
    return lax.fori_loop(0, trips, step, carry, unroll=unroll)


def fold(x):
    return jnp.sum(x.reshape(x.shape[0] // 8, 8, x.shape[1]), axis=0)


def no_sums(width):
    return (jnp.zeros((8, width), F32), jnp.zeros((8, width), F32))


def put_sums(sums, index, pair):
    rows = jnp.concatenate([jnp.sum(v, axis=0, keepdims=True) for v in pair], axis=0)
    sums[pl.ds(index, 1)] = rows[None]


def own_at(sc, h):
    return 2 * sc[1] + h


def other_at(sc, h):
    return 2 * (1 - sc[1]) + h


def source_at(sc, nz, d):
    return lax.rem(sc[2] + (nz - d), nz)


def lanes_of(refs):
    return jnp.concatenate([r[...] for r in refs], axis=1)


def four(sc, own, rec):
    return [own.at[0], own.at[1], rec.at[0], rec.at[1]]


def four_at(sc):
    return [own_at(sc, 0), own_at(sc, 1), other_at(sc, 0), other_at(sc, 1)]


def split3(x):
    high = x.astype(BF)
    rest = x - high.astype(F32)
    middle = rest.astype(BF)
    return high, middle, (rest - middle.astype(F32)).astype(BF)


def tap_spot(t, mb):
    parts = QW // mb
    each = -(-9 // parts)
    return (t % each) * 8, t // each * mb


def tap_lines(mb):
    lines = -(-9 // (QW // mb)) * 8
    return lines + lines % 16


def join_taps(cells, mb):
    each = tap_lines(mb) // 8
    empty = jnp.zeros((8, mb), F32)
    grid = [[empty] * (QW // mb) for _ in range(each)]
    for t, cell in enumerate(cells):
        line, lane = tap_spot(t, mb)
        grid[line // 8][lane // mb] = cell
    rows = [jnp.concatenate(row, axis=1) for row in grid]
    return jnp.concatenate(rows, axis=0).astype(BF)


def bundle_kernel(sc, reduce_piece, expand_piece, taps, norms, out):
    cb, mb = reduce_piece.shape[0], norms.shape[1]
    at = pl.ds(pl.multiple_of(sc[0] * 8, 8), 8)
    tail = cb + tap_lines(mb)
    out[:cb] = reduce_piece[...]
    out[cb:tail] = join_taps([taps[t, at] for t in range(9)], mb)
    parts = [v.astype(F32) for v in split3(norms[...])]
    empty = jnp.zeros((8, mb), F32)
    grid = [[empty] * (QW // mb) for _ in range(2)]
    for t, part in enumerate(parts):
        grid[t * mb // QW][t * mb % QW // mb] = part
    rows = [jnp.concatenate(row, axis=1) for row in grid]
    out[tail : tail + 16] = jnp.concatenate(rows, axis=0).astype(BF)
    for t in range(QW // cb):
        out[tail + 16 :, t * cb : (t + 1) * cb] = expand_piece[t * cb : (t + 1) * cb]


def stack_kernel(lines, *refs):
    reduce_part, expand_part = refs[-2:]
    for d, ref in enumerate(refs[:-2]):
        reduce_part[0, d] = ref[:lines]
        expand_part[0, d] = ref[lines:]


def pair_kernel(a, b, out):
    out[0] = a[...].reshape(out.shape[1:])
    out[1] = b[...].reshape(out.shape[1:])


def spread_kernel(nz, sc, *refs):
    (a0, a1, a2), (b0, b2, b1) = refs[:3], refs[3:6]
    reduce_w, expand_w, diag, mid_par, out_par, taps, norms = refs[6:]
    firsts = [a0.at[0], a1.at[0], a2.at[0], a2.at[1]]
    seconds = [b0.at[0], b1.at[0], b2.at[0], b1.at[1]]
    cb, mb = reduce_w.shape[2], norms.shape[2]
    tail = cb + tap_lines(mb)
    for d in range(nz):
        zs = source_at(sc, nz, d)
        for k in range(NQ):
            q = sc[0] ^ k
            reduce_w[q, d] = firsts[k][d, :cb]
            for t in range(QW // cb):
                expand_w[q, d, t * cb : (t + 1) * cb] = seconds[k][d, :, t * cb : (t + 1) * cb]
            block = firsts[k][d, cb:tail].astype(F32)
            at = pl.ds(pl.multiple_of(q * 8, 8), 8)
            for t in range(9):
                line, lane = tap_spot(t, mb)
                taps[zs, t, at] = block[line : line + 8, lane : lane + mb]
        block = firsts[0][d, tail : tail + 16].astype(F32)
        total = jnp.zeros((8, mb), F32)
        for t in range(3):
            line, lane = t * mb // QW * 8, t * mb % QW
            total = total + block[line : line + 8, lane : lane + mb]
        norms[zs] = total
    keep = group_mask()
    half = nz // 2
    for h in range(2):
        mine = range(h * half, (h + 1) * half)
        mid_par[h] = jnp.concatenate([norms[v][:4] for v in mine], axis=1)
        for t in range(9):
            cell = jnp.concatenate([taps[v, t] for v in mine], axis=1)
            full = jnp.concatenate([cell] * (QW // GW), axis=0)
            diag[h, t] = jnp.where(keep, full, 0.0).astype(BF)
    per = cb // mb
    for v in range(nz):
        lines = norms[v]
        out_par[v] = jnp.concatenate(
            [
                jnp.concatenate([lines[4 + r * per + j : 5 + r * per + j] for j in range(per)], axis=1)
                for r in range(2)
            ],
            axis=0,
        )


def group_mask():
    group_row = lax.broadcasted_iota(jnp.int32, (QW, QW), 0) // GW
    group_col = lax.broadcasted_iota(jnp.int32, (QW, QW), 1) // GW
    return group_row == group_col


def cut_kernel(nz, d, low, sc, cot, out, sem):
    spots, images = out.shape[:2]
    start = pl.multiple_of(lax.rem(sc[2] + d, nz) * images, images)
    copy = pltpu.make_async_copy(cot.at[low : low + spots, pl.ds(start, images)], out, sem)
    copy.start()
    copy.wait()


def pick_kernel(nz, k, sc, parts, *refs):
    q, out = sc[0] ^ k, refs[-1]
    cb = parts.shape[2]
    for d in range(nz):
        out[d, :cb] = parts[q, d]
        for taps in refs[:-1]:
            out[d, cb:] = taps[q, source_at(sc, nz, d)]


def total_kernel(*refs):
    total = refs[0][...].astype(F32)
    for ref in refs[1:-1]:
        total = total + ref[...].astype(F32)
    refs[-1][...] = total.astype(refs[-1].dtype)


def home_kernel(nz, sc, *refs):
    parts, outs = refs[:NQ], refs[NQ:]
    for d in range(nz):
        total = parts[0][d].astype(F32)
        for k in range(1, NQ):
            total = total + parts[k][d].astype(F32)
        outs[d][...] = total.astype(outs[d].dtype)


def pick3(masks, values):
    return masks[0] * values[0] + masks[1] * values[1] + masks[2] * values[2]


def crop_kernel(nz, d, sc, src, off, out):
    images, lanes = out.shape[1:]
    start = pl.multiple_of(lax.rem(sc[2] + d, nz) * images, images)
    at = pl.ds(start, images)
    row = jnp.broadcast_to(off[at, 0:1], (images, 128))
    col = jnp.broadcast_to(off[at, 1:2], (images, 128))
    row_masks = [(row == a).astype(F32).astype(BF) for a in range(3)]
    col_masks = [(col == a).astype(F32).astype(BF) for a in range(3)]
    for base in range(0, lanes, 128):
        span = slice(base, base + 128)
        lines = []
        for i in range(SRC):
            cells = [src[i, j, at, span] for j in range(SRC)]
            lines.append([pick3(col_masks, cells[j : j + 3]) for j in range(HW)])
            if i >= 2:
                for j in range(HW):
                    cell = pick3(row_masks, [line[j] for line in lines[i - 2 : i + 1]])
                    out[(i - 2) * HW + j, :, span] = cell


def reduce_kernel(nz, sc, *refs):
    xs, (w, own, other) = refs[:nz], refs[nz:]
    x = lanes_of(xs)
    for h in range(2):
        own[h] = dot(x, w[own_at(sc, h)].reshape(x.shape[1], QW))
        other[h] = dot(x, w[other_at(sc, h)].reshape(x.shape[1], QW)).astype(BF)


def first_sums_kernel(sc, own, rec, sums):
    for h in range(2):

        def body(at, c):
            v = own[h, at] + rec[h, at].astype(F32)
            return c[0] + fold(v), c[1] + fold(v * v)

        put_sums(sums, h, tiles(own.shape[1], body, no_sums(QW)))


def zero_border(pad, images):
    span = pad.shape[1]
    pad[0] = jnp.zeros_like(pad[0])
    pad[SRC - 1] = jnp.zeros_like(pad[0])
    edge = jnp.zeros((HW, images, pad.shape[2]), pad.dtype)
    pad[1 : HW + 1, 0:images] = edge
    pad[1 : HW + 1, span - images : span] = edge


def each_cell(images, body, carry):
    def line(i, c):
        for j in range(HW):
            at = pl.ds(pl.multiple_of((i * HW + j) * images, images), images)
            c = body(i, j, at, c)
        return c

    return lax.fori_loop(0, HW, line, carry)


def conv_kernel(count, images, sc, own, rec, tot, par, diag, act, v2, sums, pad):
    rows = HW * images
    zero_border(pad, images)
    for h in range(2):
        center, inv = norm_rows(tot[h, 0:1], tot[h, 1:2], count)
        gain, shift = par[h, 0:1], par[h, 1:2]

        def fill(i, j, at, c):
            v = own[h, at] + rec[h, at].astype(F32)
            a = gelu((v - center) * inv * gain + shift).astype(BF)
            act[h, at] = a
            pad[i + 1, (j + 1) * images : (j + 2) * images] = a
            return c

        each_cell(images, fill, 0)

        def taps(i, c):
            acc = jnp.zeros((rows, QW), F32)
            for di in range(3):
                line = pad.at[i + di]
                for dj in range(3):
                    acc = acc + dot(line[dj * images : dj * images + rows], diag[h, di * 3 + dj])
            v2[h, pl.ds(pl.multiple_of(i * rows, rows), rows)] = acc
            return c[0] + fold(acc), c[1] + fold(acc * acc)

        put_sums(sums, h, lax.fori_loop(0, HW, taps, no_sums(QW)))


def second_act_kernel(count, sc, v2, tot, par, out):
    for h in range(2):
        center, inv = norm_rows(tot[h, 0:1], tot[h, 1:2], count)
        gain, shift = par[h, 2:3], par[h, 3:4]

        def body(at, c):
            out[h, at] = gelu((v2[h, at] - center) * inv * gain + shift).astype(BF)
            return c

        tiles(v2.shape[1], body, 0)


def expand_kernel(nz, sc, own, rec, w, e, sums):
    x = lanes_of(four(sc, own, rec))
    for d in range(nz):
        e[d] = dot(x, jnp.concatenate([w[k, d] for k in four_at(sc)], axis=0))

        def body(at, c):
            v = e[d, at]
            return c[0] + fold(v), c[1] + fold(v * v)

        put_sums(sums, source_at(sc, nz, d), tiles(e.shape[1], body, no_sums(e.shape[2])))


def up_kernel(nz, count, pieces, earlier, sc, e, tot, par, *refs):
    many = len(pieces)
    xs, refs = refs[:many], refs[many:]
    cots, refs = refs[: sum(pieces.values())], refs[sum(pieces.values()) + 2 * earlier :]
    outs, (up, sums) = refs[:many], refs[many:]
    used = 0
    for j, d in enumerate(pieces):
        zs = source_at(sc, nz, d)
        t = tot[zs]
        center, inv = norm_rows(t[0:1], t[1:2], count)
        gain, shift = par[zs, 0:1], par[zs, 1:2]
        base = 0
        pair = no_sums(e.shape[2])
        for cot in cots[used : used + pieces[d]]:

            def body(local, c):
                size = local.size
                at = pl.ds(pl.multiple_of(local.start + base, size), size)
                hat = (e[d, at] - center) * inv
                value, slope = gelu_both(hat * gain + shift + xs[j][at].astype(F32))
                outs[j][at] = value.astype(BF)
                u = cot[local].astype(F32) * slope
                up[d, at] = u
                return c[0] + fold(u), c[1] + fold(u * hat)

            pair = tiles(cot.shape[0], body, pair)
            base += cot.shape[0]
        used += pieces[d]
        put_sums(sums, zs, pair)


def add_kernel(a, b, out):
    out[...] = a[...] + b[...]


def pass_kernel(low, value, out):
    out[...] = value[low : low + out.shape[0]]


def expand_back_kernel(nz, count, sc, e, up, tot, tot_b, par, w, eg, own, other):
    for d in range(nz):
        zs = source_at(sc, nz, d)
        t, b = tot[zs], tot_b[zs]
        center, inv = norm_rows(t[0:1], t[1:2], count)
        factor, mean_d, mean_x = inv * par[zs, 0:1], b[0:1] / count, b[1:2] / count

        def body(at, c):
            hat = (e[d, at] - center) * inv
            eg[d, at] = (factor * (up[d, at] - mean_d - hat * mean_x)).astype(BF)
            return c

        tiles(e.shape[1], body, 0)
    grads = lanes_of([eg.at[d] for d in range(nz)])
    for h in range(2):
        for index, out in ((own_at(sc, h), own), (other_at(sc, h), other)):
            out[h] = dot_t(grads, lanes_of([w.at[index, d] for d in range(nz)])).astype(out.dtype)


def second_up_kernel(count, sc, own, rec, v2, tot, par, up, sums):
    for h in range(2):
        center, inv = norm_rows(tot[h, 0:1], tot[h, 1:2], count)
        gain, shift = par[h, 2:3], par[h, 3:4]

        def body(at, c):
            hat = (v2[h, at] - center) * inv
            u = (own[h, at] + rec[h, at].astype(F32)) * gelu_both(hat * gain + shift)[1]
            up[h, at] = u
            return c[0] + fold(u), c[1] + fold(u * hat)

        put_sums(sums, h, tiles(v2.shape[1], body, no_sums(QW)))


def conv_back_kernel(
    count, images, sc, up2, v2, tot2, tot2b, par, diag, own, rec, tot1, cg, up1, sums, pad, temp
):
    rows = HW * images
    zero_border(pad, images)
    for h in range(2):
        center2, inv2 = norm_rows(tot2[h, 0:1], tot2[h, 1:2], count)
        factor = inv2 * par[h, 2:3]
        mean_d, mean_x = tot2b[h, 0:1] / count, tot2b[h, 1:2] / count

        def fill(i, j, at, c):
            hat = (v2[h, at] - center2) * inv2
            g = (factor * (up2[h, at] - mean_d - hat * mean_x)).astype(BF)
            cg[h, at] = g
            pad[i + 1, (j + 1) * images : (j + 2) * images] = g
            return c

        each_cell(images, fill, 0)
        center, inv = norm_rows(tot1[h, 0:1], tot1[h, 1:2], count)
        gain, shift = par[h, 0:1], par[h, 1:2]

        def taps(i, c):
            acc = jnp.zeros((rows, QW), F32)
            for di in range(3):
                line = pad.at[i + 2 - di]
                for dj in range(3):
                    start = (2 - dj) * images
                    acc = acc + dot_t(line[start : start + rows], diag[h, di * 3 + dj])
            temp[...] = acc
            for j in range(HW):
                at = pl.ds(pl.multiple_of(i * rows + j * images, images), images)
                hat = (own[h, at] + rec[h, at].astype(F32) - center) * inv
                u = temp[j * images : (j + 1) * images] * gelu_both(hat * gain + shift)[1]
                up1[h, at] = u
                c = (c[0] + fold(u), c[1] + fold(u * hat))
            return c

        put_sums(sums, h, lax.fori_loop(0, HW, taps, no_sums(QW)))


def first_grad_kernel(count, sc, up1, own, rec, tot, tot_b, par, out):
    for h in range(2):
        center, inv = norm_rows(tot[h, 0:1], tot[h, 1:2], count)
        factor = inv * par[h, 0:1]
        mean_d, mean_x = tot_b[h, 0:1] / count, tot_b[h, 1:2] / count

        def body(at, c):
            hat = (own[h, at] + rec[h, at].astype(F32) - center) * inv
            out[h, at] = (factor * (up1[h, at] - mean_d - hat * mean_x)).astype(BF)
            return c

        tiles(up1.shape[1], body, 0)


def input_grad_kernel(d, sc, own, rec, up, w, out):
    weights = lanes_of([w.at[k, d] for k in four_at(sc)])
    out[...] = (up[d] + dot_t(lanes_of(four(sc, own, rec)), weights)).astype(BF)


def reduce_wgrad_kernel(nz, sc, own, rec, *refs):
    xs, out = refs[:nz], refs[nz]
    grads = lanes_of(four(sc, own, rec))
    for d in range(nz):
        g = dot_rows(xs[d][...], grads).astype(BF)
        for j, k in enumerate(four_at(sc)):
            out[k, d] = g[:, j * QW : (j + 1) * QW]


def expand_wgrad_kernel(nz, sc, own, rec, eg, out):
    width = eg.shape[2]
    grads = lanes_of([eg.at[d] for d in range(nz)])
    for ref, k in zip(four(sc, own, rec), four_at(sc)):
        g = dot_rows(ref[...], grads).astype(BF)
        for d in range(nz):
            out[k, d] = g[:, d * width : (d + 1) * width]


def conv_wgrad_kernel(images, mb, sc, act, cg, out, pad):
    rows = HW * images
    keep = group_mask()
    zero_border(pad, images)
    for h in range(2):
        for i in range(HW):
            pad[i + 1, images : images + rows] = act[h, i * rows : (i + 1) * rows]
        grad = cg[h]
        cells = []
        for di in range(3):
            for dj in range(3):
                window = pad[di : di + HW, dj * images : dj * images + rows]
                full = dot_rows(window.reshape(HW * rows, QW), grad)
                full = jnp.where(keep, full, 0.0)
                cells.append(jnp.sum(full.reshape(QW // GW, GW, QW), axis=0))
        for q in range(NQ):
            for a in range(QW // mb):
                pieces = [c[q * 8 : q * 8 + 8, a * mb : (a + 1) * mb] for c in cells]
                out[q, h * (QW // mb) + a] = join_taps(pieces, mb)


def square_sum(x):
    return jnp.sum(x.reshape(x.shape[0] // 8, 8, x.shape[1]), axis=0)


def lane_fold(x):
    return sum(x[:, j : j + 128] for j in range(0, x.shape[1], 128)) if x.shape[1] > 128 else x


def grads_kernel(nz, sc, *refs):
    firsts, seconds, (mid, out) = refs[:NQ], refs[NQ : 2 * NQ], refs[2 * NQ : 2 * NQ + 2]
    expand, reduce, taps, squares, first, second = refs[2 * NQ + 2 :]
    cb, mb = reduce.shape[0], taps.shape[2]
    half = nz // 2
    for k in range(NQ):
        first[sc[0] ^ k] = firsts[k][...]
        second[sc[0] ^ k] = seconds[k][...]
    total = jnp.zeros((8, 128), F32)
    for q in range(NQ):
        for a in range(half):
            start = (((q % 2) * half + a) * 2 + q // 2) * mb
            piece = second[q, a * mb : (a + 1) * mb].astype(F32)
            expand[start : start + mb] = piece
            total = total + lane_fold(square_sum(piece * piece))
            piece = first[q, :cb, a * mb : (a + 1) * mb]
            reduce[:, start : start + mb] = piece.astype(F32)
        block = first[q, cb:].astype(F32)
        for t in range(9):
            line, lane = tap_spot(t, mb)
            taps[t, q * 8 : (q + 1) * 8] = block[line : line + 8, lane : lane + mb]
        full = first[q].astype(F32)
        total = total + lane_fold(square_sum(full * full))
    extra = jnp.sum(mid[...] * mid[...]) + jnp.sum(out[...] * out[...])
    corner = lax.broadcasted_iota(jnp.int32, (8, 128), 0) + lax.broadcasted_iota(
        jnp.int32, (8, 128), 1
    )
    total = total + jnp.where(corner == 0, extra, 0.0)
    squares[...] = jnp.broadcast_to(jnp.sum(total, keepdims=True), (8, 128))


def place_kernel(nz, d, low, sc, block, *refs):
    out, token, sem = refs[-3:]
    token[...] = jnp.zeros_like(token)
    spots, images = block.shape[:2]
    start = pl.multiple_of(lax.rem(sc[2] + d, nz) * images, images)
    copy = pltpu.make_async_copy(block, out.at[low : low + spots, pl.ds(start, images)], sem)
    copy.start()
    copy.wait()


def adam_step(weight, gradient, momentum, variance, learn_rate, decay_rate):
    momentum_new = moment_decay * momentum + (1.0 - moment_decay) * gradient
    variance_new = moment_decay * variance + (1.0 - moment_decay) * gradient * gradient
    correction = 1.0 - moment_decay**STEP
    direction = momentum_new / correction / (jnp.sqrt(variance_new / correction) + adam_eps)
    weight_new = weight - learn_rate * (direction + decay_rate * weight)
    return (weight_new, momentum_new, variance_new, weight_new.astype(BF))


def shards(
    source,
    offsets,
    cotangent,
    reduce_weight,
    reduce_first,
    reduce_second,
    group_weight,
    group_first,
    group_second,
    expand_weight,
    expand_first,
    expand_second,
    mid_norms,
    mid_first,
    mid_second,
    out_norms,
    out_first,
    out_second,
):
    nd, ng = lax.axis_size("dp"), lax.axis_size("group")
    nz = ng // 2
    gi = lax.axis_index("group")
    z, core = gi // 2, gi % 2
    p = lax.axis_index("dp") % NQ
    sc = jnp.stack([p, core, z]).astype(jnp.int32)
    n = source.shape[0]
    images = n // nz
    rows = SPOTS * images
    cb = source.shape[3]
    mb = group_weight.shape[3]
    zh = nz // 2
    count = float(SPOTS * n * nd)

    def over_z(value, d):
        pairs = [(2 * a + c, 2 * ((a + d) % nz) + c) for a in range(nz) for c in range(2)]
        return lax.ppermute(value, "group", pairs)

    def over_core(value):
        return lax.ppermute(value, "group", [(a, a ^ 1) for a in range(ng)])

    def over_dp(value, k):
        return lax.ppermute(value, "dp", [(a, a ^ k) for a in range(nd)])

    def pinned_add(a, b, pins):
        shape = sds(a.shape, F32)
        return call(add_kernel, "add", shape, a, b, specs=[VMEM] * 2, deps=pins)

    def over_all_dp(value, *pins):
        k = 1
        while k < nd:
            other = over_dp(value, k)
            k *= 2
            if k < nd or not pins:
                value = value + other
            else:
                value = pinned_add(value, other, pins)
        return value

    def over_all_z(value, *pins):
        k = 2
        while k < ng:
            other = lax.ppermute(value, "group", [(a, a ^ k) for a in range(ng)])
            k *= 2
            if k < ng or not pins:
                value = value + other
            else:
                value = pinned_add(value, other, pins)
        return value

    def everywhere(value, *pins):
        return over_all_z(over_all_dp(value), *pins)

    src = source.transpose(1, 2, 0, 3)
    crops = []
    order = [1] + list(range(2, nz))[::-1] + [0]
    for d in order:
        crop = call(
            functools.partial(crop_kernel, nz, d),
            "crop",
            sds((SPOTS, images, cb), BF),
            sc,
            src,
            offsets,
            deps=crops[-1:],
        ).reshape(rows, cb)
        crops.append(crop)
    pixels = [over_z(crops[order.index(d)], d) if d else crops[-1] for d in range(nz)]

    col_starts = [((p % 2) * zh + j) * 2 * mb + (p // 2) * mb for j in range(zh)]
    reduce_piece = jnp.concatenate(
        [lax.dynamic_slice_in_dim(reduce_weight, s, mb, 1) for s in col_starts], axis=1
    ).astype(BF)
    expand_piece = (
        lax.dynamic_slice(
            expand_weight.reshape(nz, 2, mb, cb),
            ((p % 2) * zh, p // 2, 0, 0),
            (zh, 1, mb, cb),
        )
        .reshape(QW, cb)
        .astype(BF)
    )

    pack = jnp.concatenate([mid_norms, out_norms.reshape(-1, mb)], axis=0)
    bundle = call(
        bundle_kernel,
        "bundle",
        sds((2 * cb + tap_lines(mb) + 16, QW), BF),
        sc,
        reduce_piece,
        expand_piece,
        group_weight.reshape(9, GW, mb),
        pack,
        deps=crops[:1],
    )

    lines = cb + tap_lines(mb) + 16
    parts = [sds((1, nz, lines, QW), BF), sds((1, nz, cb, QW), BF)]

    def pair(a, b, shape, *deps):
        return call(pair_kernel, "pair", sds((2,) + shape, BF), a, b, specs=[VMEM] * 2, deps=deps)

    first_w, second_w = call(
        functools.partial(stack_kernel, lines),
        "stack",
        parts,
        bundle,
        *[over_z(bundle, d) for d in range(1, nz)],
        specs=[VMEM] * nz,
        deps=[crops[-1], pixels[1]],
    )

    first_x, second_y = over_dp(first_w, 1), over_dp(second_w, 2)
    first_y, second_x = (
        over_dp(pair(first_w, first_x, first_w.shape[1:], pixels[-1]), 2),
        over_dp(pair(second_w, second_y, second_w.shape[1:], pixels[-1]), 1),
    )
    reduce_q, expand_q, diag, mid_par, out_par = call(
        functools.partial(spread_kernel, nz),
        "spread",
        [
            sds((NQ, nz, cb, QW), BF),
            sds((NQ, nz, QW, cb), BF),
            sds((2, 9, QW, QW), BF),
            sds((2, 4, QW), F32),
            sds((nz, 2, cb), F32),
        ],
        sc,
        first_w,
        first_x,
        first_y,
        second_w,
        second_y,
        second_x,
        scratch=[pltpu.VMEM((nz, 9, GW, mb), F32), pltpu.VMEM((nz, 8, mb), F32)],
    )

    cot = cotangent.transpose(1, 2, 0, 3).reshape(SPOTS, n, cb)

    def cut(d, low, high, *deps):
        return call(
            functools.partial(cut_kernel, nz, d, low),
            "cut",
            sds((high - low, images, cb), BF),
            sc,
            cot,
            specs=[SMEM, ANY],
            scratch=[pltpu.SemaphoreType.DMA],
            deps=deps,
        ).reshape((high - low) * images, cb)

    def turn(d):
        return 0 if d == 1 else (1 if d == nz - 1 else 2)

    half_f, half_b = sds((2, rows, QW), F32), sds((2, rows, QW), BF)
    sum2_s, sumz_s = sds((2, 2, QW), F32), sds((nz, 2, cb), F32)
    pad_s = pltpu.VMEM((SRC, SRC * images, QW), BF)

    own1, oth1 = call(
        functools.partial(reduce_kernel, nz),
        "reduce",
        [half_f, half_b],
        sc,
        *pixels,
        reduce_q,
        limit=16,
        deps=[diag, mid_par, out_par, expand_q],
    )
    rec1 = over_core(oth1)
    turns = [[d for d in range(1, nz) if turn(d) == t] for t in range(3)]
    split = SPOTS // 2
    cot_turns = [
        [(d, 0, SPOTS) for d in turns[0]],
        [(d, 0, SPOTS) for d in turns[1]],
        [(d, 0, split) for d in turns[2]],
        [(d, split, SPOTS) for d in turns[2]],
    ]
    cots = {0: [cut(0, 0, SPOTS, diag)]}

    def send_cots(t, *deps):
        pieces = [cut(*spot, *deps) for spot in cot_turns[t]]
        moved = [over_z(piece, spot[0]) for spot, piece in zip(cot_turns[t], pieces)]
        for spot, piece in zip(cot_turns[t], moved):
            cots.setdefault(spot[0], []).append(piece)
        return pieces, moved

    sent, pins = send_cots(0, oth1)
    sums1 = call(first_sums_kernel, "first_sums", sum2_s, sc, own1, rec1, deps=sent)
    tot1 = everywhere(sums1, *pins)
    sent, pins = send_cots(1, tot1)
    act, v2, sums2 = call(
        functools.partial(conv_kernel, count, images),
        "conv",
        [half_b, half_f, sum2_s],
        sc,
        own1,
        rec1,
        tot1,
        mid_par,
        diag,
        scratch=[pad_s],
        deps=sent,
    )
    tot2 = everywhere(sums2, *pins)
    sent, pins = send_cots(2, tot2)
    sent_more, last_cots = send_cots(3, tot2)
    sa = call(
        functools.partial(second_act_kernel, count),
        "second_act",
        half_b,
        sc,
        v2,
        tot2,
        mid_par,
        deps=sent + sent_more,
    )
    sa_rec = over_core(sa)
    e, sums3 = call(
        functools.partial(expand_kernel, nz),
        "expand",
        [sds((nz, rows, cb), F32), sumz_s],
        sc,
        sa,
        sa_rec,
        expand_q,
        limit=12,
    )
    tot3 = everywhere(sums3, *pins)
    def upward(ds, *earlier, deps=()):
        many = len(ds)
        pieces = {d: len(cots[d]) for d in ds}
        at = 4 + many + sum(pieces.values())
        res = call(
            functools.partial(up_kernel, nz, count, pieces, len(earlier) // 2),
            "up",
            [sds((rows, cb), BF)] * many + [sds((nz, rows, cb), F32), sumz_s],
            sc,
            e,
            tot3,
            out_par,
            *[pixels[d] for d in ds],
            *[piece for d in ds for piece in cots[d]],
            *earlier,
            input_output_aliases={at: many, at + 1: many + 1} if earlier else {},
            deps=deps,
        )
        return dict(zip(ds, res[:many])), res[many], res[many + 1]

    early, up3, sums3b = upward(turns[0], deps=last_cots)
    values, up3, sums3b = upward([d for d in range(nz) if d not in turns[0]], up3, sums3b)
    values.update(early)
    outs = [(0, 0, values[0])]

    def send_outs(t, *deps):
        pieces, moved = [], []
        for d, low, high in cot_turns[t]:
            piece = values[d]
            if deps:
                piece = call(
                    functools.partial(pass_kernel, low * images),
                    "pass",
                    sds(((high - low) * images, cb), BF),
                    piece,
                    specs=[VMEM],
                    deps=deps,
                )
            pieces.append(piece)
            moved.append(over_z(piece, -d))
            outs.append((d, low, moved[-1]))
        return pieces, moved

    sent, pins = send_outs(0)
    tot3b = everywhere(sums3b, *pins)

    def place(pieces, result=None, *deps):
        for d, low, piece in pieces:
            extra = () if result is None else (result,)
            result, token = call(
                functools.partial(place_kernel, nz, d, low),
                "place",
                [sds((SPOTS, n, cb), BF), sds((8, 128), F32)],
                sc,
                piece.reshape(-1, images, cb),
                *extra,
                specs=[SMEM, VMEM] + [ANY] * len(extra),
                out_specs=[ANY, VMEM],
                scratch=[pltpu.SemaphoreType.DMA],
                input_output_aliases={2: 0} if extra else {},
                deps=deps,
            )
        return result, token

    def to_images(result):
        return result.reshape(HW, HW, n, cb).transpose(2, 0, 1, 3)

    sent, pins = send_outs(1, tot3b)
    eg, own2, oth2 = call(
        functools.partial(expand_back_kernel, nz, count),
        "expand_back",
        [sds((nz, rows, cb), BF), half_f, half_b],
        sc,
        e,
        up3,
        tot3,
        tot3b,
        out_par,
        expand_q,
        deps=sent,
    )
    expand_parts = call(
        functools.partial(expand_wgrad_kernel, nz),
        "expand_wgrad",
        sds((NQ, nz, QW, cb), BF),
        sc,
        sa,
        sa_rec,
        eg,
        limit=12,
    )

    def pick(k, parts, *more, deps=()):
        return call(
            functools.partial(pick_kernel, nz, k),
            "pick",
            sds((nz, parts.shape[2] + sum(v.shape[2] for v in more), parts.shape[3]), BF),
            sc,
            parts,
            *more,
            deps=deps,
        )

    def gather_home(picks, deps=()):
        shape = picks[0].shape[1:]
        return call(
            functools.partial(home_kernel, nz),
            "home",
            [sds(shape, F32)] + [sds(shape, BF)] * (nz - 1),
            sc,
            picks[0],
            *[over_dp(picks[k], k) for k in range(1, NQ)],
            deps=deps,
        )

    def total_of(pieces, deps=()):
        low = call(
            total_kernel,
            "total",
            sds(pieces[0].shape, BF),
            pieces[0],
            *[over_z(pieces[d], -d) for d in range(1, nz)],
            specs=[VMEM] * nz,
            deps=deps,
        )
        k = NQ
        while k < nd:
            low = (low.astype(F32) + over_dp(low, k).astype(F32)).astype(BF)
            k *= 2
        return low

    def to_all_dp(low):
        return [low] + [over_dp(low, k) for k in range(1, NQ)]

    rec2 = over_core(oth2)
    up2, sums2b = call(
        functools.partial(second_up_kernel, count),
        "second_up",
        [half_f, sum2_s],
        sc,
        own2,
        rec2,
        v2,
        tot2,
        mid_par,
        deps=[expand_parts],
    )
    mid2b = over_all_dp(sums2b)
    tot2b = over_all_z(mid2b, *pins)
    sent, pins = send_outs(2, tot2b)
    expand_picks = [pick(k, expand_parts, deps=[mid2b]) for k in range(NQ)]
    cg, up1, sums1b = call(
        functools.partial(conv_back_kernel, count, images),
        "conv_back",
        [half_b, half_f, sum2_s],
        sc,
        up2,
        v2,
        tot2,
        tot2b,
        mid_par,
        diag,
        own1,
        rec1,
        tot1,
        scratch=[pad_s, pltpu.VMEM((HW * images, QW), F32)],
        deps=sent,
    )
    expand_pieces = gather_home(expand_picks, [sums1b])
    expand_low = total_of(expand_pieces)
    tot1b = over_all_z(over_all_dp(sums1b, expand_pieces[0]), *pins, expand_low)
    fg = call(
        functools.partial(first_grad_kernel, count),
        "first_grad",
        half_b,
        sc,
        up1,
        own1,
        rec1,
        tot1,
        tot1b,
        mid_par,
    )
    fg_rec = over_core(fg)
    def input_block(d, *deps):
        return call(
            functools.partial(input_grad_kernel, d),
            "input_grad",
            sds((rows, cb), BF),
            sc,
            fg,
            fg_rec,
            up3,
            reduce_q,
            deps=deps,
        )

    first = input_block(2)
    reduce_parts = call(
        functools.partial(reduce_wgrad_kernel, nz),
        "reduce_wgrad",
        sds((NQ, nz, cb, QW), BF),
        sc,
        fg,
        fg_rec,
        *pixels,
        limit=12,
        deps=[first],
    )
    conv_parts = call(
        functools.partial(conv_wgrad_kernel, images, mb),
        "conv_wgrad",
        sds((NQ, nz, tap_lines(mb), QW), BF),
        sc,
        act,
        cg,
        scratch=[pad_s],
        deps=[reduce_parts],
    )
    _, pins = send_outs(3, tot1b)

    def later(value, *deps):
        shape = sds(value.shape, value.dtype)
        body = functools.partial(pass_kernel, 0)
        return call(body, "pass", shape, value, specs=[VMEM], deps=deps)

    expand_home = to_all_dp(expand_low)
    reduce_picks = [
        pick(k, reduce_parts, conv_parts, deps=expand_home[1:]) for k in range(NQ)
    ]
    final = nz - 1
    input_blocks = {2: first}
    last = reduce_picks[1]
    for d in list(range(3, nz)) + [1, 0]:
        last = input_block(d, last)
        input_blocks[d] = last
    output, token = place([v for v in outs if v[1] == 0])
    pieces = gather_home(reduce_picks, [last, token])
    output, _ = place([v for v in outs if v[1] > 0], output)
    moved = [(0, 0, input_blocks[0])]
    moved += [(d, 0, over_z(input_blocks[d], -d)) for d in range(2, final)]
    placed, token = place(moved)
    reduce_low = total_of(pieces, [token] + pins)
    reduce_home = to_all_dp(reduce_low)
    second = later(input_blocks[1], reduce_low)
    second_moved = over_z(second, -1)
    placed, _ = place([(1, 0, second_moved)], placed)

    def my_mid(total):
        lanes = lax.dynamic_slice_in_dim(total.transpose(1, 0, 2).reshape(2, 2 * QW), z * mb, mb, 1)
        return [lanes[1], lanes[0]]

    mid_grads = jnp.stack(my_mid(tot1b) + my_mid(tot2b))
    mine3 = lax.dynamic_index_in_dim(tot3b, z, 0, keepdims=False)
    out_grads = jnp.stack([mine3[1], mine3[0]])

    expand_wgrad, reduce_wgrad, tap_grad, total_sq = call(
        functools.partial(grads_kernel, nz),
        "grads",
        [
            sds((MID, cb), F32),
            sds((cb, MID), F32),
            sds((9, GW, mb), F32),
            sds((8, 128), F32),
        ],
        sc,
        *reduce_home,
        *expand_home,
        mid_grads,
        out_grads,
        scratch=[
            pltpu.VMEM((NQ, cb + tap_lines(mb), QW), BF),
            pltpu.VMEM((NQ, QW, cb), BF),
        ],
        deps=[second],
    )
    group_wgrad = tap_grad.reshape(group_weight.shape)
    total_sq = over_all_z(total_sq + over_core(total_sq), second_moved)
    moved = over_z(later(input_blocks[final], second_moved), -final)
    input_grad, _ = place([(final, 0, moved)], placed)
    grad_norm = jnp.sqrt(total_sq[0, 0])
    clip_scale = jnp.minimum(1.0, clip_norm / (grad_norm + 1e-06))
    reduce_out = adam_step(
        reduce_weight,
        reduce_wgrad * clip_scale,
        reduce_first,
        reduce_second,
        1.0 / jnp.sqrt(1.0 * CIN),
        0.1,
    )
    group_out = adam_step(
        group_weight,
        group_wgrad * clip_scale,
        group_first,
        group_second,
        1.0 / jnp.sqrt(9.0 * GW),
        0.1,
    )
    expand_out = adam_step(
        expand_weight,
        expand_wgrad * clip_scale,
        expand_first,
        expand_second,
        1.0 / jnp.sqrt(1.0 * MID),
        0.1,
    )
    mid_out = adam_step(mid_norms, mid_grads * clip_scale, mid_first, mid_second, 0.5, 0.0)
    out_out = adam_step(out_norms, out_grads * clip_scale, out_first, out_second, 0.5, 0.0)
    return (
        to_images(output),
        to_images(input_grad),
        grad_norm,
        *reduce_out,
        *group_out,
        *expand_out,
        *mid_out,
        *out_out,
    )


def solution(mesh):
    images = P("dp", None, None, "group")
    rows, cols = P("group", None), P(None, "group")
    kernel = P(None, None, None, "group")
    in_specs = (
        (images, P("dp", None), images) + (rows,) * 3 + (kernel,) * 3 + (cols,) * 3 + (cols,) * 6
    )
    out_specs = (images, images, P()) + (rows,) * 4 + (kernel,) * 4 + (cols,) * 4 + (cols,) * 8
    return jax.shard_map(shards, mesh=mesh, in_specs=in_specs, out_specs=out_specs, check_vma=False)
```

```python
import functools

import jax
import jax.numpy as jnp
from jax import lax
from jax.experimental import pallas as pl
from jax.experimental.pallas import tpu as pltpu
from jax.sharding import PartitionSpec as P

CIN = 2048
GW = 32
HW = 7
STEP = 10
MID = 1024
SRC = 9
NQ = 4
QW = MID // NQ
SPOTS = HW * HW

norm_eps = 1e-05
adam_eps = 1e-08
clip_norm = 1.0
moment_decay = 0.5

GELU_K = 0.7978845608028654
GELU_C = 0.044715
BF = jnp.bfloat16
F32 = jnp.float32


def dot(a, b):
    return jnp.dot(a, b, preferred_element_type=F32)


def dot_t(a, b):
    return lax.dot_general(a, b, (((1,), (1,)), ((), ())), preferred_element_type=F32)


def dot_rows(a, b):
    return lax.dot_general(a, b, (((0,), (0,)), ((), ())), preferred_element_type=F32)


def gelu(u):
    t = jnp.tanh(u * (GELU_K * GELU_C * (u * u) + GELU_K))
    return u * (0.5 * t + 0.5)


def gelu_both(u):
    u2 = u * u
    part = 0.5 * jnp.tanh(u * (GELU_K * GELU_C * u2 + GELU_K)) + 0.5
    bend = u * (6.0 * GELU_K * GELU_C * u2 + 2.0 * GELU_K)
    return u * part, part * (bend * (1.0 - part) + 1.0)


def norm_rows(total, squares, count):
    center = total / count
    spread = squares / count - center * center
    return center, lax.rsqrt(spread + norm_eps)


VMEM = pl.BlockSpec(memory_space=pltpu.VMEM)
SMEM = pl.BlockSpec(memory_space=pltpu.SMEM)
ANY = pl.BlockSpec(memory_space=pl.ANY)


def call(body, name, out_shape, *inputs, scratch=(), limit=8, specs=None, deps=(), **more):
    used, unused = len(inputs), len(deps)

    def inner(*refs):
        body(*refs[:used], *refs[used + unused :])

    return pl.pallas_call(
        inner,
        in_specs=(specs or [SMEM] + [VMEM] * (used - 1)) + [ANY] * unused,
        out_specs=more.pop("out_specs", jax.tree.map(lambda _: VMEM, out_shape)),
        out_shape=out_shape,
        scratch_shapes=list(scratch),
        compiler_params=pltpu.CompilerParams(vmem_limit_bytes=limit << 20),
        cost_estimate=pl.CostEstimate(flops=1024, bytes_accessed=1024, transcendentals=0),
        name=name,
        **more,
    )(*inputs, *deps)


def sds(shape, dtype):
    return jax.ShapeDtypeStruct(shape, dtype)


def tiles(rows, body, carry):
    size = 32 if rows % 32 == 0 else 16

    def step(i, c):
        return body(pl.ds(pl.multiple_of(i * size, size), size), c)

    trips = rows // size
    unroll = max(u for u in range(1, 9) if trips % u == 0)
    return lax.fori_loop(0, trips, step, carry, unroll=unroll)


def fold(x):
    return jnp.sum(x.reshape(x.shape[0] // 8, 8, x.shape[1]), axis=0)


def no_sums(width):
    return (jnp.zeros((8, width), F32), jnp.zeros((8, width), F32))


def put_sums(sums, index, pair):
    rows = jnp.concatenate([jnp.sum(v, axis=0, keepdims=True) for v in pair], axis=0)
    sums[pl.ds(index, 1)] = rows[None]


def own_at(sc, h):
    return 2 * sc[1] + h


def other_at(sc, h):
    return 2 * (1 - sc[1]) + h


def source_at(sc, nz, d):
    return lax.rem(sc[2] + (nz - d), nz)


def lanes_of(refs):
    return jnp.concatenate([r[...] for r in refs], axis=1)


def four(sc, own, rec):
    return [own.at[0], own.at[1], rec.at[0], rec.at[1]]


def four_at(sc):
    return [own_at(sc, 0), own_at(sc, 1), other_at(sc, 0), other_at(sc, 1)]


def split3(x):
    high = x.astype(BF)
    rest = x - high.astype(F32)
    middle = rest.astype(BF)
    return high, middle, (rest - middle.astype(F32)).astype(BF)


def tap_spot(t, mb):
    parts = QW // mb
    each = -(-9 // parts)
    return (t % each) * 8, t // each * mb


def tap_lines(mb):
    lines = -(-9 // (QW // mb)) * 8
    return lines + lines % 16


def join_taps(cells, mb):
    each = tap_lines(mb) // 8
    empty = jnp.zeros((8, mb), F32)
    grid = [[empty] * (QW // mb) for _ in range(each)]
    for t, cell in enumerate(cells):
        line, lane = tap_spot(t, mb)
        grid[line // 8][lane // mb] = cell
    rows = [jnp.concatenate(row, axis=1) for row in grid]
    return jnp.concatenate(rows, axis=0).astype(BF)


def bundle_kernel(sc, reduce_piece, expand_piece, taps, norms, out):
    cb, mb = reduce_piece.shape[0], norms.shape[1]
    at = pl.ds(pl.multiple_of(sc[0] * 8, 8), 8)
    tail = cb + tap_lines(mb)
    out[:cb] = reduce_piece[...]
    out[cb:tail] = join_taps([taps[t, at] for t in range(9)], mb)
    parts = [v.astype(F32) for v in split3(norms[...])]
    empty = jnp.zeros((8, mb), F32)
    grid = [[empty] * (QW // mb) for _ in range(2)]
    for t, part in enumerate(parts):
        grid[t * mb // QW][t * mb % QW // mb] = part
    rows = [jnp.concatenate(row, axis=1) for row in grid]
    out[tail : tail + 16] = jnp.concatenate(rows, axis=0).astype(BF)
    for t in range(QW // cb):
        out[tail + 16 :, t * cb : (t + 1) * cb] = expand_piece[t * cb : (t + 1) * cb]


def stack_kernel(lines, *refs):
    reduce_part, expand_part = refs[-2:]
    for d, ref in enumerate(refs[:-2]):
        reduce_part[0, d] = ref[:lines]
        expand_part[0, d] = ref[lines:]


def pair_kernel(a, b, out):
    out[0] = a[...].reshape(out.shape[1:])
    out[1] = b[...].reshape(out.shape[1:])


def spread_kernel(nz, sc, *refs):
    (a0, a1, a2), (b0, b2, b1) = refs[:3], refs[3:6]
    reduce_w, expand_w, diag, mid_par, out_par, taps, norms = refs[6:]
    firsts = [a0.at[0], a1.at[0], a2.at[0], a2.at[1]]
    seconds = [b0.at[0], b1.at[0], b2.at[0], b1.at[1]]
    cb, mb = reduce_w.shape[2], norms.shape[2]
    tail = cb + tap_lines(mb)
    for d in range(nz):
        zs = source_at(sc, nz, d)
        for k in range(NQ):
            q = sc[0] ^ k
            reduce_w[q, d] = firsts[k][d, :cb]
            for t in range(QW // cb):
                expand_w[q, d, t * cb : (t + 1) * cb] = seconds[k][d, :, t * cb : (t + 1) * cb]
            block = firsts[k][d, cb:tail].astype(F32)
            at = pl.ds(pl.multiple_of(q * 8, 8), 8)
            for t in range(9):
                line, lane = tap_spot(t, mb)
                taps[zs, t, at] = block[line : line + 8, lane : lane + mb]
        block = firsts[0][d, tail : tail + 16].astype(F32)
        total = jnp.zeros((8, mb), F32)
        for t in range(3):
            line, lane = t * mb // QW * 8, t * mb % QW
            total = total + block[line : line + 8, lane : lane + mb]
        norms[zs] = total
    keep = group_mask()
    half = nz // 2
    for h in range(2):
        mine = range(h * half, (h + 1) * half)
        mid_par[h] = jnp.concatenate([norms[v][:4] for v in mine], axis=1)
        for t in range(9):
            cell = jnp.concatenate([taps[v, t] for v in mine], axis=1)
            full = jnp.concatenate([cell] * (QW // GW), axis=0)
            diag[h, t] = jnp.where(keep, full, 0.0).astype(BF)
    per = cb // mb
    for v in range(nz):
        lines = norms[v]
        out_par[v] = jnp.concatenate(
            [
                jnp.concatenate([lines[4 + r * per + j : 5 + r * per + j] for j in range(per)], axis=1)
                for r in range(2)
            ],
            axis=0,
        )


def group_mask():
    group_row = lax.broadcasted_iota(jnp.int32, (QW, QW), 0) // GW
    group_col = lax.broadcasted_iota(jnp.int32, (QW, QW), 1) // GW
    return group_row == group_col


def cut_kernel(nz, d, low, sc, cot, out, sem):
    spots, images = out.shape[:2]
    start = pl.multiple_of(lax.rem(sc[2] + d, nz) * images, images)
    copy = pltpu.make_async_copy(cot.at[low : low + spots, pl.ds(start, images)], out, sem)
    copy.start()
    copy.wait()


def pick_kernel(nz, k, sc, parts, *refs):
    q, out = sc[0] ^ k, refs[-1]
    cb = parts.shape[2]
    for d in range(nz):
        out[d, :cb] = parts[q, d]
        for taps in refs[:-1]:
            out[d, cb:] = taps[q, source_at(sc, nz, d)]


def total_kernel(*refs):
    total = refs[0][...].astype(F32)
    for ref in refs[1:-1]:
        total = total + ref[...].astype(F32)
    refs[-1][...] = total.astype(refs[-1].dtype)


def home_kernel(nz, sc, *refs):
    parts, outs = refs[:NQ], refs[NQ:]
    for d in range(nz):
        total = parts[0][d].astype(F32)
        for k in range(1, NQ):
            total = total + parts[k][d].astype(F32)
        outs[d][...] = total.astype(outs[d].dtype)


def pick3(masks, values):
    return masks[0] * values[0] + masks[1] * values[1] + masks[2] * values[2]


def crop_kernel(nz, d, sc, src, off, out):
    images, lanes = out.shape[1:]
    start = pl.multiple_of(lax.rem(sc[2] + d, nz) * images, images)
    at = pl.ds(start, images)
    row = jnp.broadcast_to(off[at, 0:1], (images, 128))
    col = jnp.broadcast_to(off[at, 1:2], (images, 128))
    row_masks = [(row == a).astype(F32).astype(BF) for a in range(3)]
    col_masks = [(col == a).astype(F32).astype(BF) for a in range(3)]
    for base in range(0, lanes, 128):
        span = slice(base, base + 128)
        lines = []
        for i in range(SRC):
            cells = [src[i, j, at, span] for j in range(SRC)]
            lines.append([pick3(col_masks, cells[j : j + 3]) for j in range(HW)])
            if i >= 2:
                for j in range(HW):
                    cell = pick3(row_masks, [line[j] for line in lines[i - 2 : i + 1]])
                    out[(i - 2) * HW + j, :, span] = cell


def reduce_kernel(nz, sc, *refs):
    xs, (w, own, other) = refs[:nz], refs[nz:]
    x = lanes_of(xs)
    for h in range(2):
        own[h] = dot(x, w[own_at(sc, h)].reshape(x.shape[1], QW))
        other[h] = dot(x, w[other_at(sc, h)].reshape(x.shape[1], QW)).astype(BF)


def first_sums_kernel(sc, own, rec, sums):
    for h in range(2):

        def body(at, c):
            v = own[h, at] + rec[h, at].astype(F32)
            return c[0] + fold(v), c[1] + fold(v * v)

        put_sums(sums, h, tiles(own.shape[1], body, no_sums(QW)))


def zero_border(pad, images):
    span = pad.shape[1]
    pad[0] = jnp.zeros_like(pad[0])
    pad[SRC - 1] = jnp.zeros_like(pad[0])
    edge = jnp.zeros((HW, images, pad.shape[2]), pad.dtype)
    pad[1 : HW + 1, 0:images] = edge
    pad[1 : HW + 1, span - images : span] = edge


def each_cell(images, body, carry):
    def line(i, c):
        for j in range(HW):
            at = pl.ds(pl.multiple_of((i * HW + j) * images, images), images)
            c = body(i, j, at, c)
        return c

    return lax.fori_loop(0, HW, line, carry)


def conv_kernel(count, images, sc, own, rec, tot, par, diag, act, v2, sums, pad):
    rows = HW * images
    zero_border(pad, images)
    for h in range(2):
        center, inv = norm_rows(tot[h, 0:1], tot[h, 1:2], count)
        gain, shift = par[h, 0:1], par[h, 1:2]

        def fill(i, j, at, c):
            v = own[h, at] + rec[h, at].astype(F32)
            a = gelu((v - center) * inv * gain + shift).astype(BF)
            act[h, at] = a
            pad[i + 1, (j + 1) * images : (j + 2) * images] = a
            return c

        each_cell(images, fill, 0)

        def taps(i, c):
            acc = jnp.zeros((rows, QW), F32)
            for di in range(3):
                line = pad.at[i + di]
                for dj in range(3):
                    acc = acc + dot(line[dj * images : dj * images + rows], diag[h, di * 3 + dj])
            v2[h, pl.ds(pl.multiple_of(i * rows, rows), rows)] = acc
            return c[0] + fold(acc), c[1] + fold(acc * acc)

        put_sums(sums, h, lax.fori_loop(0, HW, taps, no_sums(QW)))


def second_act_kernel(count, sc, v2, tot, par, out):
    for h in range(2):
        center, inv = norm_rows(tot[h, 0:1], tot[h, 1:2], count)
        gain, shift = par[h, 2:3], par[h, 3:4]

        def body(at, c):
            out[h, at] = gelu((v2[h, at] - center) * inv * gain + shift).astype(BF)
            return c

        tiles(v2.shape[1], body, 0)


def expand_kernel(nz, sc, own, rec, w, e, sums):
    x = lanes_of(four(sc, own, rec))
    for d in range(nz):
        e[d] = dot(x, jnp.concatenate([w[k, d] for k in four_at(sc)], axis=0))

        def body(at, c):
            v = e[d, at]
            return c[0] + fold(v), c[1] + fold(v * v)

        put_sums(sums, source_at(sc, nz, d), tiles(e.shape[1], body, no_sums(e.shape[2])))


def up_kernel(nz, count, pieces, earlier, sc, e, tot, par, *refs):
    many = len(pieces)
    xs, refs = refs[:many], refs[many:]
    cots, refs = refs[: sum(pieces.values())], refs[sum(pieces.values()) + 2 * earlier :]
    outs, (up, sums) = refs[:many], refs[many:]
    used = 0
    for j, d in enumerate(pieces):
        zs = source_at(sc, nz, d)
        t = tot[zs]
        center, inv = norm_rows(t[0:1], t[1:2], count)
        gain, shift = par[zs, 0:1], par[zs, 1:2]
        base = 0
        pair = no_sums(e.shape[2])
        for cot in cots[used : used + pieces[d]]:

            def body(local, c):
                size = local.size
                at = pl.ds(pl.multiple_of(local.start + base, size), size)
                hat = (e[d, at] - center) * inv
                value, slope = gelu_both(hat * gain + shift + xs[j][at].astype(F32))
                outs[j][at] = value.astype(BF)
                u = cot[local].astype(F32) * slope
                up[d, at] = u
                return c[0] + fold(u), c[1] + fold(u * hat)

            pair = tiles(cot.shape[0], body, pair)
            base += cot.shape[0]
        used += pieces[d]
        put_sums(sums, zs, pair)


def add_kernel(a, b, out):
    out[...] = a[...] + b[...]


def pass_kernel(low, value, out):
    out[...] = value[low : low + out.shape[0]]


def expand_back_kernel(nz, count, sc, e, up, tot, tot_b, par, w, eg, own, other):
    for d in range(nz):
        zs = source_at(sc, nz, d)
        t, b = tot[zs], tot_b[zs]
        center, inv = norm_rows(t[0:1], t[1:2], count)
        factor, mean_d, mean_x = inv * par[zs, 0:1], b[0:1] / count, b[1:2] / count

        def body(at, c):
            hat = (e[d, at] - center) * inv
            eg[d, at] = (factor * (up[d, at] - mean_d - hat * mean_x)).astype(BF)
            return c

        tiles(e.shape[1], body, 0)
    grads = lanes_of([eg.at[d] for d in range(nz)])
    for h in range(2):
        for index, out in ((own_at(sc, h), own), (other_at(sc, h), other)):
            out[h] = dot_t(grads, lanes_of([w.at[index, d] for d in range(nz)])).astype(out.dtype)


def second_up_kernel(count, sc, own, rec, v2, tot, par, up, sums):
    for h in range(2):
        center, inv = norm_rows(tot[h, 0:1], tot[h, 1:2], count)
        gain, shift = par[h, 2:3], par[h, 3:4]

        def body(at, c):
            hat = (v2[h, at] - center) * inv
            u = (own[h, at] + rec[h, at].astype(F32)) * gelu_both(hat * gain + shift)[1]
            up[h, at] = u
            return c[0] + fold(u), c[1] + fold(u * hat)

        put_sums(sums, h, tiles(v2.shape[1], body, no_sums(QW)))


def conv_back_kernel(
    count, images, sc, up2, v2, tot2, tot2b, par, diag, own, rec, tot1, cg, up1, sums, pad, temp
):
    rows = HW * images
    zero_border(pad, images)
    for h in range(2):
        center2, inv2 = norm_rows(tot2[h, 0:1], tot2[h, 1:2], count)
        factor = inv2 * par[h, 2:3]
        mean_d, mean_x = tot2b[h, 0:1] / count, tot2b[h, 1:2] / count

        def fill(i, j, at, c):
            hat = (v2[h, at] - center2) * inv2
            g = (factor * (up2[h, at] - mean_d - hat * mean_x)).astype(BF)
            cg[h, at] = g
            pad[i + 1, (j + 1) * images : (j + 2) * images] = g
            return c

        each_cell(images, fill, 0)
        center, inv = norm_rows(tot1[h, 0:1], tot1[h, 1:2], count)
        gain, shift = par[h, 0:1], par[h, 1:2]

        def taps(i, c):
            acc = jnp.zeros((rows, QW), F32)
            for di in range(3):
                line = pad.at[i + 2 - di]
                for dj in range(3):
                    start = (2 - dj) * images
                    acc = acc + dot_t(line[start : start + rows], diag[h, di * 3 + dj])
            temp[...] = acc
            for j in range(HW):
                at = pl.ds(pl.multiple_of(i * rows + j * images, images), images)
                hat = (own[h, at] + rec[h, at].astype(F32) - center) * inv
                u = temp[j * images : (j + 1) * images] * gelu_both(hat * gain + shift)[1]
                up1[h, at] = u
                c = (c[0] + fold(u), c[1] + fold(u * hat))
            return c

        put_sums(sums, h, lax.fori_loop(0, HW, taps, no_sums(QW)))


def first_grad_kernel(count, sc, up1, own, rec, tot, tot_b, par, out):
    for h in range(2):
        center, inv = norm_rows(tot[h, 0:1], tot[h, 1:2], count)
        factor = inv * par[h, 0:1]
        mean_d, mean_x = tot_b[h, 0:1] / count, tot_b[h, 1:2] / count

        def body(at, c):
            hat = (own[h, at] + rec[h, at].astype(F32) - center) * inv
            out[h, at] = (factor * (up1[h, at] - mean_d - hat * mean_x)).astype(BF)
            return c

        tiles(up1.shape[1], body, 0)


def input_grad_kernel(d, sc, own, rec, up, w, out):
    weights = lanes_of([w.at[k, d] for k in four_at(sc)])
    out[...] = (up[d] + dot_t(lanes_of(four(sc, own, rec)), weights)).astype(BF)


def reduce_wgrad_kernel(nz, sc, own, rec, *refs):
    xs, out = refs[:nz], refs[nz]
    grads = lanes_of(four(sc, own, rec))
    for d in range(nz):
        g = dot_rows(xs[d][...], grads).astype(BF)
        for j, k in enumerate(four_at(sc)):
            out[k, d] = g[:, j * QW : (j + 1) * QW]


def expand_wgrad_kernel(nz, sc, own, rec, eg, out):
    width = eg.shape[2]
    grads = lanes_of([eg.at[d] for d in range(nz)])
    for ref, k in zip(four(sc, own, rec), four_at(sc)):
        g = dot_rows(ref[...], grads).astype(BF)
        for d in range(nz):
            out[k, d] = g[:, d * width : (d + 1) * width]


def conv_wgrad_kernel(images, mb, sc, act, cg, out, pad):
    rows = HW * images
    keep = group_mask()
    zero_border(pad, images)
    for h in range(2):
        for i in range(HW):
            pad[i + 1, images : images + rows] = act[h, i * rows : (i + 1) * rows]
        grad = cg[h]
        cells = []
        for di in range(3):
            for dj in range(3):
                window = pad[di : di + HW, dj * images : dj * images + rows]
                full = dot_rows(window.reshape(HW * rows, QW), grad)
                full = jnp.where(keep, full, 0.0)
                cells.append(jnp.sum(full.reshape(QW // GW, GW, QW), axis=0))
        for q in range(NQ):
            for a in range(QW // mb):
                pieces = [c[q * 8 : q * 8 + 8, a * mb : (a + 1) * mb] for c in cells]
                out[q, h * (QW // mb) + a] = join_taps(pieces, mb)


def square_sum(x):
    return jnp.sum(x.reshape(x.shape[0] // 8, 8, x.shape[1]), axis=0)


def lane_fold(x):
    return sum(x[:, j : j + 128] for j in range(0, x.shape[1], 128)) if x.shape[1] > 128 else x


def grads_kernel(nz, sc, *refs):
    firsts, seconds, (mid, out) = refs[:NQ], refs[NQ : 2 * NQ], refs[2 * NQ : 2 * NQ + 2]
    expand, reduce, taps, squares, first, second = refs[2 * NQ + 2 :]
    cb, mb = reduce.shape[0], taps.shape[2]
    half = nz // 2
    for k in range(NQ):
        first[sc[0] ^ k] = firsts[k][...]
        second[sc[0] ^ k] = seconds[k][...]
    total = jnp.zeros((8, 128), F32)
    for q in range(NQ):
        for a in range(half):
            start = (((q % 2) * half + a) * 2 + q // 2) * mb
            piece = second[q, a * mb : (a + 1) * mb].astype(F32)
            expand[start : start + mb] = piece
            total = total + lane_fold(square_sum(piece * piece))
            piece = first[q, :cb, a * mb : (a + 1) * mb]
            reduce[:, start : start + mb] = piece.astype(F32)
        block = first[q, cb:].astype(F32)
        for t in range(9):
            line, lane = tap_spot(t, mb)
            taps[t, q * 8 : (q + 1) * 8] = block[line : line + 8, lane : lane + mb]
        full = first[q].astype(F32)
        total = total + lane_fold(square_sum(full * full))
    extra = jnp.sum(mid[...] * mid[...]) + jnp.sum(out[...] * out[...])
    corner = lax.broadcasted_iota(jnp.int32, (8, 128), 0) + lax.broadcasted_iota(
        jnp.int32, (8, 128), 1
    )
    total = total + jnp.where(corner == 0, extra, 0.0)
    squares[...] = jnp.broadcast_to(jnp.sum(total, keepdims=True), (8, 128))


def place_kernel(nz, d, low, sc, block, *refs):
    out, token, sem = refs[-3:]
    token[...] = jnp.zeros_like(token)
    spots, images = block.shape[:2]
    start = pl.multiple_of(lax.rem(sc[2] + d, nz) * images, images)
    copy = pltpu.make_async_copy(block, out.at[low : low + spots, pl.ds(start, images)], sem)
    copy.start()
    copy.wait()


def adam_step(weight, gradient, momentum, variance, learn_rate, decay_rate):
    momentum_new = moment_decay * momentum + (1.0 - moment_decay) * gradient
    variance_new = moment_decay * variance + (1.0 - moment_decay) * gradient * gradient
    correction = 1.0 - moment_decay**STEP
    direction = momentum_new / correction / (jnp.sqrt(variance_new / correction) + adam_eps)
    weight_new = weight - learn_rate * (direction + decay_rate * weight)
    return (weight_new, momentum_new, variance_new, weight_new.astype(BF))


def shards(
    source,
    offsets,
    cotangent,
    reduce_weight,
    reduce_first,
    reduce_second,
    group_weight,
    group_first,
    group_second,
    expand_weight,
    expand_first,
    expand_second,
    mid_norms,
    mid_first,
    mid_second,
    out_norms,
    out_first,
    out_second,
):
    nd, ng = lax.axis_size("dp"), lax.axis_size("group")
    nz = ng // 2
    gi = lax.axis_index("group")
    z, core = gi // 2, gi % 2
    p = lax.axis_index("dp") % NQ
    sc = jnp.stack([p, core, z]).astype(jnp.int32)
    n = source.shape[0]
    images = n // nz
    rows = SPOTS * images
    cb = source.shape[3]
    mb = group_weight.shape[3]
    zh = nz // 2
    count = float(SPOTS * n * nd)

    def over_z(value, d):
        pairs = [(2 * a + c, 2 * ((a + d) % nz) + c) for a in range(nz) for c in range(2)]
        return lax.ppermute(value, "group", pairs)

    def over_core(value):
        return lax.ppermute(value, "group", [(a, a ^ 1) for a in range(ng)])

    def over_dp(value, k):
        return lax.ppermute(value, "dp", [(a, a ^ k) for a in range(nd)])

    def pinned_add(a, b, pins):
        shape = sds(a.shape, F32)
        return call(add_kernel, "add", shape, a, b, specs=[VMEM] * 2, deps=pins)

    def over_all_dp(value, *pins):
        k = 1
        while k < nd:
            other = over_dp(value, k)
            k *= 2
            if k < nd or not pins:
                value = value + other
            else:
                value = pinned_add(value, other, pins)
        return value

    def over_all_z(value, *pins):
        k = 2
        while k < ng:
            other = lax.ppermute(value, "group", [(a, a ^ k) for a in range(ng)])
            k *= 2
            if k < ng or not pins:
                value = value + other
            else:
                value = pinned_add(value, other, pins)
        return value

    def everywhere(value, *pins):
        return over_all_z(over_all_dp(value), *pins)

    src = source.transpose(1, 2, 0, 3)
    crops = []
    order = [1] + list(range(2, nz))[::-1] + [0]
    for d in order:
        crop = call(
            functools.partial(crop_kernel, nz, d),
            "crop",
            sds((SPOTS, images, cb), BF),
            sc,
            src,
            offsets,
            deps=crops[-1:],
        ).reshape(rows, cb)
        crops.append(crop)
    pixels = [over_z(crops[order.index(d)], d) if d else crops[-1] for d in range(nz)]

    col_starts = [((p % 2) * zh + j) * 2 * mb + (p // 2) * mb for j in range(zh)]
    reduce_piece = jnp.concatenate(
        [lax.dynamic_slice_in_dim(reduce_weight, s, mb, 1) for s in col_starts], axis=1
    ).astype(BF)
    expand_piece = (
        lax.dynamic_slice(
            expand_weight.reshape(nz, 2, mb, cb),
            ((p % 2) * zh, p // 2, 0, 0),
            (zh, 1, mb, cb),
        )
        .reshape(QW, cb)
        .astype(BF)
    )

    pack = jnp.concatenate([mid_norms, out_norms.reshape(-1, mb)], axis=0)
    bundle = call(
        bundle_kernel,
        "bundle",
        sds((2 * cb + tap_lines(mb) + 16, QW), BF),
        sc,
        reduce_piece,
        expand_piece,
        group_weight.reshape(9, GW, mb),
        pack,
        deps=crops[:1],
    )

    lines = cb + tap_lines(mb) + 16
    parts = [sds((1, nz, lines, QW), BF), sds((1, nz, cb, QW), BF)]

    def pair(a, b, shape, *deps):
        return call(pair_kernel, "pair", sds((2,) + shape, BF), a, b, specs=[VMEM] * 2, deps=deps)

    first_w, second_w = call(
        functools.partial(stack_kernel, lines),
        "stack",
        parts,
        bundle,
        *[over_z(bundle, d) for d in range(1, nz)],
        specs=[VMEM] * nz,
        deps=[crops[-1], pixels[1]],
    )

    first_x, second_y = over_dp(first_w, 1), over_dp(second_w, 2)
    first_y, second_x = (
        over_dp(pair(first_w, first_x, first_w.shape[1:], pixels[-1]), 2),
        over_dp(pair(second_w, second_y, second_w.shape[1:], pixels[-1]), 1),
    )
    reduce_q, expand_q, diag, mid_par, out_par = call(
        functools.partial(spread_kernel, nz),
        "spread",
        [
            sds((NQ, nz, cb, QW), BF),
            sds((NQ, nz, QW, cb), BF),
            sds((2, 9, QW, QW), BF),
            sds((2, 4, QW), F32),
            sds((nz, 2, cb), F32),
        ],
        sc,
        first_w,
        first_x,
        first_y,
        second_w,
        second_y,
        second_x,
        scratch=[pltpu.VMEM((nz, 9, GW, mb), F32), pltpu.VMEM((nz, 8, mb), F32)],
    )

    cot = cotangent.transpose(1, 2, 0, 3).reshape(SPOTS, n, cb)

    def cut(d, low, high, *deps):
        return call(
            functools.partial(cut_kernel, nz, d, low),
            "cut",
            sds((high - low, images, cb), BF),
            sc,
            cot,
            specs=[SMEM, ANY],
            scratch=[pltpu.SemaphoreType.DMA],
            deps=deps,
        ).reshape((high - low) * images, cb)

    def turn(d):
        return 0 if d == 1 else (1 if d == nz - 1 else 2)

    half_f, half_b = sds((2, rows, QW), F32), sds((2, rows, QW), BF)
    sum2_s, sumz_s = sds((2, 2, QW), F32), sds((nz, 2, cb), F32)
    pad_s = pltpu.VMEM((SRC, SRC * images, QW), BF)

    own1, oth1 = call(
        functools.partial(reduce_kernel, nz),
        "reduce",
        [half_f, half_b],
        sc,
        *pixels,
        reduce_q,
        limit=16,
        deps=[diag, mid_par, out_par, expand_q],
    )
    rec1 = over_core(oth1)
    turns = [[d for d in range(1, nz) if turn(d) == t] for t in range(3)]
    split = SPOTS // 2
    out_turns = [
        [(d, 0, SPOTS) for d in turns[0]],
        [(d, 0, SPOTS) for d in turns[1]],
        [(d, 0, split) for d in turns[2]],
        [(d, split, SPOTS) for d in turns[2]],
    ]
    cot_turns = [
        [(d, 0, SPOTS) for d in turns[0]],
        [(d, 0, SPOTS) for d in turns[1]] + [(d, 0, 10) for d in turns[2]],
        [(d, 10, 30) for d in turns[2]],
        [(d, 30, SPOTS) for d in turns[2]],
    ]
    cots = {0: [cut(0, 0, SPOTS, diag)]}

    def send_cots(t, *deps):
        pieces = [cut(*spot, *deps) for spot in cot_turns[t]]
        moved = [over_z(piece, spot[0]) for spot, piece in zip(cot_turns[t], pieces)]
        for spot, piece in zip(cot_turns[t], moved):
            cots.setdefault(spot[0], []).append(piece)
        return pieces, moved

    sent, pins = send_cots(0, oth1)
    sums1 = call(first_sums_kernel, "first_sums", sum2_s, sc, own1, rec1, deps=sent)
    tot1 = everywhere(sums1, *pins)
    sent, pins = send_cots(1, tot1)
    act, v2, sums2 = call(
        functools.partial(conv_kernel, count, images),
        "conv",
        [half_b, half_f, sum2_s],
        sc,
        own1,
        rec1,
        tot1,
        mid_par,
        diag,
        scratch=[pad_s],
        deps=sent,
    )
    tot2 = everywhere(sums2, *pins)
    sent, pins = send_cots(2, tot2)
    sent_more, last_cots = send_cots(3, tot2)
    sa = call(
        functools.partial(second_act_kernel, count),
        "second_act",
        half_b,
        sc,
        v2,
        tot2,
        mid_par,
        deps=sent + sent_more,
    )
    sa_rec = over_core(sa)
    e, sums3 = call(
        functools.partial(expand_kernel, nz),
        "expand",
        [sds((nz, rows, cb), F32), sumz_s],
        sc,
        sa,
        sa_rec,
        expand_q,
        limit=12,
    )
    tot3 = everywhere(sums3, *pins)
    def upward(ds, *earlier, deps=()):
        many = len(ds)
        pieces = {d: len(cots[d]) for d in ds}
        at = 4 + many + sum(pieces.values())
        res = call(
            functools.partial(up_kernel, nz, count, pieces, len(earlier) // 2),
            "up",
            [sds((rows, cb), BF)] * many + [sds((nz, rows, cb), F32), sumz_s],
            sc,
            e,
            tot3,
            out_par,
            *[pixels[d] for d in ds],
            *[piece for d in ds for piece in cots[d]],
            *earlier,
            input_output_aliases={at: many, at + 1: many + 1} if earlier else {},
            deps=deps,
        )
        return dict(zip(ds, res[:many])), res[many], res[many + 1]

    early, up3, sums3b = upward(turns[0], deps=last_cots)
    values, up3, sums3b = upward([d for d in range(nz) if d not in turns[0]], up3, sums3b)
    values.update(early)
    outs = [(0, 0, values[0])]

    def send_outs(t, *deps):
        pieces, moved = [], []
        for d, low, high in out_turns[t]:
            piece = values[d]
            if deps:
                piece = call(
                    functools.partial(pass_kernel, low * images),
                    "pass",
                    sds(((high - low) * images, cb), BF),
                    piece,
                    specs=[VMEM],
                    deps=deps,
                )
            pieces.append(piece)
            moved.append(over_z(piece, -d))
            outs.append((d, low, moved[-1]))
        return pieces, moved

    sent, pins = send_outs(0)
    tot3b = everywhere(sums3b, *pins)

    def place(pieces, result=None, *deps):
        for d, low, piece in pieces:
            extra = () if result is None else (result,)
            result, token = call(
                functools.partial(place_kernel, nz, d, low),
                "place",
                [sds((SPOTS, n, cb), BF), sds((8, 128), F32)],
                sc,
                piece.reshape(-1, images, cb),
                *extra,
                specs=[SMEM, VMEM] + [ANY] * len(extra),
                out_specs=[ANY, VMEM],
                scratch=[pltpu.SemaphoreType.DMA],
                input_output_aliases={2: 0} if extra else {},
                deps=deps,
            )
        return result, token

    def to_images(result):
        return result.reshape(HW, HW, n, cb).transpose(2, 0, 1, 3)

    sent, pins = send_outs(1, tot3b)
    eg, own2, oth2 = call(
        functools.partial(expand_back_kernel, nz, count),
        "expand_back",
        [sds((nz, rows, cb), BF), half_f, half_b],
        sc,
        e,
        up3,
        tot3,
        tot3b,
        out_par,
        expand_q,
        deps=sent,
    )
    expand_parts = call(
        functools.partial(expand_wgrad_kernel, nz),
        "expand_wgrad",
        sds((NQ, nz, QW, cb), BF),
        sc,
        sa,
        sa_rec,
        eg,
        limit=12,
    )

    def pick(k, parts, *more, deps=()):
        return call(
            functools.partial(pick_kernel, nz, k),
            "pick",
            sds((nz, parts.shape[2] + sum(v.shape[2] for v in more), parts.shape[3]), BF),
            sc,
            parts,
            *more,
            deps=deps,
        )

    def gather_home(picks, deps=()):
        shape = picks[0].shape[1:]
        return call(
            functools.partial(home_kernel, nz),
            "home",
            [sds(shape, F32)] + [sds(shape, BF)] * (nz - 1),
            sc,
            picks[0],
            *[over_dp(picks[k], k) for k in range(1, NQ)],
            deps=deps,
        )

    def total_of(pieces, deps=()):
        low = call(
            total_kernel,
            "total",
            sds(pieces[0].shape, BF),
            pieces[0],
            *[over_z(pieces[d], -d) for d in range(1, nz)],
            specs=[VMEM] * nz,
            deps=deps,
        )
        k = NQ
        while k < nd:
            low = (low.astype(F32) + over_dp(low, k).astype(F32)).astype(BF)
            k *= 2
        return low

    def to_all_dp(low):
        return [low] + [over_dp(low, k) for k in range(1, NQ)]

    rec2 = over_core(oth2)
    up2, sums2b = call(
        functools.partial(second_up_kernel, count),
        "second_up",
        [half_f, sum2_s],
        sc,
        own2,
        rec2,
        v2,
        tot2,
        mid_par,
        deps=[expand_parts],
    )
    mid2b = over_all_dp(sums2b)
    tot2b = over_all_z(mid2b, *pins)
    sent, pins = send_outs(2, tot2b)
    expand_picks = [pick(k, expand_parts, deps=[mid2b]) for k in range(NQ)]
    cg, up1, sums1b = call(
        functools.partial(conv_back_kernel, count, images),
        "conv_back",
        [half_b, half_f, sum2_s],
        sc,
        up2,
        v2,
        tot2,
        tot2b,
        mid_par,
        diag,
        own1,
        rec1,
        tot1,
        scratch=[pad_s, pltpu.VMEM((HW * images, QW), F32)],
        deps=sent,
    )
    expand_pieces = gather_home(expand_picks, [sums1b])
    expand_low = total_of(expand_pieces)
    tot1b = over_all_z(over_all_dp(sums1b, expand_pieces[0]), *pins, expand_low)
    fg = call(
        functools.partial(first_grad_kernel, count),
        "first_grad",
        half_b,
        sc,
        up1,
        own1,
        rec1,
        tot1,
        tot1b,
        mid_par,
    )
    fg_rec = over_core(fg)
    def input_block(d, *deps):
        return call(
            functools.partial(input_grad_kernel, d),
            "input_grad",
            sds((rows, cb), BF),
            sc,
            fg,
            fg_rec,
            up3,
            reduce_q,
            deps=deps,
        )

    first = input_block(2)
    reduce_parts = call(
        functools.partial(reduce_wgrad_kernel, nz),
        "reduce_wgrad",
        sds((NQ, nz, cb, QW), BF),
        sc,
        fg,
        fg_rec,
        *pixels,
        limit=12,
        deps=[first],
    )
    conv_parts = call(
        functools.partial(conv_wgrad_kernel, images, mb),
        "conv_wgrad",
        sds((NQ, nz, tap_lines(mb), QW), BF),
        sc,
        act,
        cg,
        scratch=[pad_s],
        deps=[reduce_parts],
    )
    _, pins = send_outs(3, tot1b)

    def later(value, *deps):
        shape = sds(value.shape, value.dtype)
        body = functools.partial(pass_kernel, 0)
        return call(body, "pass", shape, value, specs=[VMEM], deps=deps)

    expand_home = to_all_dp(expand_low)
    reduce_picks = [
        pick(k, reduce_parts, conv_parts, deps=expand_home[1:]) for k in range(NQ)
    ]
    final = nz - 1
    input_blocks = {2: first}
    last = reduce_picks[1]
    for d in list(range(3, nz)) + [1, 0]:
        last = input_block(d, last)
        input_blocks[d] = last
    output, token = place([v for v in outs if v[1] == 0])
    pieces = gather_home(reduce_picks, [last, token])
    output, _ = place([v for v in outs if v[1] > 0], output)
    moved = [(0, 0, input_blocks[0])]
    moved += [(d, 0, over_z(input_blocks[d], -d)) for d in range(2, final)]
    placed, token = place(moved)
    reduce_low = total_of(pieces, [token] + pins)
    reduce_home = to_all_dp(reduce_low)
    second = later(input_blocks[1], reduce_low)
    second_moved = over_z(second, -1)
    placed, _ = place([(1, 0, second_moved)], placed)

    def my_mid(total):
        lanes = lax.dynamic_slice_in_dim(total.transpose(1, 0, 2).reshape(2, 2 * QW), z * mb, mb, 1)
        return [lanes[1], lanes[0]]

    mid_grads = jnp.stack(my_mid(tot1b) + my_mid(tot2b))
    mine3 = lax.dynamic_index_in_dim(tot3b, z, 0, keepdims=False)
    out_grads = jnp.stack([mine3[1], mine3[0]])

    expand_wgrad, reduce_wgrad, tap_grad, total_sq = call(
        functools.partial(grads_kernel, nz),
        "grads",
        [
            sds((MID, cb), F32),
            sds((cb, MID), F32),
            sds((9, GW, mb), F32),
            sds((8, 128), F32),
        ],
        sc,
        *reduce_home,
        *expand_home,
        mid_grads,
        out_grads,
        scratch=[
            pltpu.VMEM((NQ, cb + tap_lines(mb), QW), BF),
            pltpu.VMEM((NQ, QW, cb), BF),
        ],
        deps=[second],
    )
    group_wgrad = tap_grad.reshape(group_weight.shape)
    total_sq = over_all_z(total_sq + over_core(total_sq), second_moved)
    moved = over_z(later(input_blocks[final], second_moved), -final)
    input_grad, _ = place([(final, 0, moved)], placed)
    grad_norm = jnp.sqrt(total_sq[0, 0])
    clip_scale = jnp.minimum(1.0, clip_norm / (grad_norm + 1e-06))
    reduce_out = adam_step(
        reduce_weight,
        reduce_wgrad * clip_scale,
        reduce_first,
        reduce_second,
        1.0 / jnp.sqrt(1.0 * CIN),
        0.1,
    )
    group_out = adam_step(
        group_weight,
        group_wgrad * clip_scale,
        group_first,
        group_second,
        1.0 / jnp.sqrt(9.0 * GW),
        0.1,
    )
    expand_out = adam_step(
        expand_weight,
        expand_wgrad * clip_scale,
        expand_first,
        expand_second,
        1.0 / jnp.sqrt(1.0 * MID),
        0.1,
    )
    mid_out = adam_step(mid_norms, mid_grads * clip_scale, mid_first, mid_second, 0.5, 0.0)
    out_out = adam_step(out_norms, out_grads * clip_scale, out_first, out_second, 0.5, 0.0)
    return (
        to_images(output),
        to_images(input_grad),
        grad_norm,
        *reduce_out,
        *group_out,
        *expand_out,
        *mid_out,
        *out_out,
    )


def solution(mesh):
    images = P("dp", None, None, "group")
    rows, cols = P("group", None), P(None, "group")
    kernel = P(None, None, None, "group")
    in_specs = (
        (images, P("dp", None), images) + (rows,) * 3 + (kernel,) * 3 + (cols,) * 3 + (cols,) * 6
    )
    out_specs = (images, images, P()) + (rows,) * 4 + (kernel,) * 4 + (cols,) * 4 + (cols,) * 8
    return jax.shard_map(shards, mesh=mesh, in_specs=in_specs, out_specs=out_specs, check_vma=False)
```

```python
import functools

import jax
import jax.numpy as jnp
from jax import lax
from jax.experimental import pallas as pl
from jax.experimental.pallas import tpu as pltpu
from jax.sharding import PartitionSpec as P

CIN = 2048
GW = 32
HW = 7
STEP = 10
MID = 1024
SRC = 9
NQ = 4
QW = MID // NQ
SPOTS = HW * HW

norm_eps = 1e-05
adam_eps = 1e-08
clip_norm = 1.0
moment_decay = 0.5

GELU_K = 0.7978845608028654
GELU_C = 0.044715
BF = jnp.bfloat16
F32 = jnp.float32


def dot(a, b):
    return jnp.dot(a, b, preferred_element_type=F32)


def dot_t(a, b):
    return lax.dot_general(a, b, (((1,), (1,)), ((), ())), preferred_element_type=F32)


def dot_rows(a, b):
    return lax.dot_general(a, b, (((0,), (0,)), ((), ())), preferred_element_type=F32)


def gelu(u):
    t = jnp.tanh(u * (GELU_K * GELU_C * (u * u) + GELU_K))
    return u * (0.5 * t + 0.5)


def gelu_both(u):
    u2 = u * u
    part = 0.5 * jnp.tanh(u * (GELU_K * GELU_C * u2 + GELU_K)) + 0.5
    bend = u * (6.0 * GELU_K * GELU_C * u2 + 2.0 * GELU_K)
    return u * part, part * (bend * (1.0 - part) + 1.0)


def norm_rows(total, squares, count):
    center = total / count
    spread = squares / count - center * center
    return center, lax.rsqrt(spread + norm_eps)


VMEM = pl.BlockSpec(memory_space=pltpu.VMEM)
SMEM = pl.BlockSpec(memory_space=pltpu.SMEM)
ANY = pl.BlockSpec(memory_space=pl.ANY)


def call(body, name, out_shape, *inputs, scratch=(), limit=8, specs=None, deps=(), **more):
    used, unused = len(inputs), len(deps)

    def inner(*refs):
        body(*refs[:used], *refs[used + unused :])

    return pl.pallas_call(
        inner,
        in_specs=(specs or [SMEM] + [VMEM] * (used - 1)) + [ANY] * unused,
        out_specs=more.pop("out_specs", jax.tree.map(lambda _: VMEM, out_shape)),
        out_shape=out_shape,
        scratch_shapes=list(scratch),
        compiler_params=pltpu.CompilerParams(vmem_limit_bytes=limit << 20),
        cost_estimate=pl.CostEstimate(flops=1024, bytes_accessed=1024, transcendentals=0),
        name=name,
        **more,
    )(*inputs, *deps)


def sds(shape, dtype):
    return jax.ShapeDtypeStruct(shape, dtype)


def tiles(rows, body, carry):
    size = 32 if rows % 32 == 0 else 16

    def step(i, c):
        return body(pl.ds(pl.multiple_of(i * size, size), size), c)

    trips = rows // size
    unroll = max(u for u in range(1, 9) if trips % u == 0)
    return lax.fori_loop(0, trips, step, carry, unroll=unroll)


def fold(x):
    return jnp.sum(x.reshape(x.shape[0] // 8, 8, x.shape[1]), axis=0)


def no_sums(width):
    return (jnp.zeros((8, width), F32), jnp.zeros((8, width), F32))


def put_sums(sums, index, pair):
    rows = jnp.concatenate([jnp.sum(v, axis=0, keepdims=True) for v in pair], axis=0)
    sums[pl.ds(index, 1)] = rows[None]


def own_at(sc, h):
    return 2 * sc[1] + h


def other_at(sc, h):
    return 2 * (1 - sc[1]) + h


def source_at(sc, nz, d):
    return lax.rem(sc[2] + (nz - d), nz)


def lanes_of(refs):
    return jnp.concatenate([r[...] for r in refs], axis=1)


def four(sc, own, rec):
    return [own.at[0], own.at[1], rec.at[0], rec.at[1]]


def four_at(sc):
    return [own_at(sc, 0), own_at(sc, 1), other_at(sc, 0), other_at(sc, 1)]


def split3(x):
    high = x.astype(BF)
    rest = x - high.astype(F32)
    middle = rest.astype(BF)
    return high, middle, (rest - middle.astype(F32)).astype(BF)


def tap_spot(t, mb):
    parts = QW // mb
    each = -(-9 // parts)
    return (t % each) * 8, t // each * mb


def tap_lines(mb):
    lines = -(-9 // (QW // mb)) * 8
    return lines + lines % 16


def join_taps(cells, mb):
    each = tap_lines(mb) // 8
    empty = jnp.zeros((8, mb), F32)
    grid = [[empty] * (QW // mb) for _ in range(each)]
    for t, cell in enumerate(cells):
        line, lane = tap_spot(t, mb)
        grid[line // 8][lane // mb] = cell
    rows = [jnp.concatenate(row, axis=1) for row in grid]
    return jnp.concatenate(rows, axis=0).astype(BF)


def bundle_kernel(sc, reduce_piece, expand_piece, taps, norms, out):
    cb, mb = reduce_piece.shape[0], norms.shape[1]
    at = pl.ds(pl.multiple_of(sc[0] * 8, 8), 8)
    tail = cb + tap_lines(mb)
    out[:cb] = reduce_piece[...]
    out[cb:tail] = join_taps([taps[t, at] for t in range(9)], mb)
    parts = [v.astype(F32) for v in split3(norms[...])]
    empty = jnp.zeros((8, mb), F32)
    grid = [[empty] * (QW // mb) for _ in range(2)]
    for t, part in enumerate(parts):
        grid[t * mb // QW][t * mb % QW // mb] = part
    rows = [jnp.concatenate(row, axis=1) for row in grid]
    out[tail : tail + 16] = jnp.concatenate(rows, axis=0).astype(BF)
    for t in range(QW // cb):
        out[tail + 16 :, t * cb : (t + 1) * cb] = expand_piece[t * cb : (t + 1) * cb]


def stack_kernel(lines, *refs):
    reduce_part, expand_part = refs[-2:]
    for d, ref in enumerate(refs[:-2]):
        reduce_part[0, d] = ref[:lines]
        expand_part[0, d] = ref[lines:]


def pair_kernel(a, b, out):
    out[0] = a[...].reshape(out.shape[1:])
    out[1] = b[...].reshape(out.shape[1:])


def spread_kernel(nz, sc, *refs):
    (a0, a1, a2), (b0, b2, b1) = refs[:3], refs[3:6]
    reduce_w, expand_w, diag, mid_par, out_par, taps, norms = refs[6:]
    firsts = [a0.at[0], a1.at[0], a2.at[0], a2.at[1]]
    seconds = [b0.at[0], b1.at[0], b2.at[0], b1.at[1]]
    cb, mb = reduce_w.shape[2], norms.shape[2]
    tail = cb + tap_lines(mb)
    for d in range(nz):
        zs = source_at(sc, nz, d)
        for k in range(NQ):
            q = sc[0] ^ k
            reduce_w[q, d] = firsts[k][d, :cb]
            for t in range(QW // cb):
                expand_w[q, d, t * cb : (t + 1) * cb] = seconds[k][d, :, t * cb : (t + 1) * cb]
            block = firsts[k][d, cb:tail].astype(F32)
            at = pl.ds(pl.multiple_of(q * 8, 8), 8)
            for t in range(9):
                line, lane = tap_spot(t, mb)
                taps[zs, t, at] = block[line : line + 8, lane : lane + mb]
        block = firsts[0][d, tail : tail + 16].astype(F32)
        total = jnp.zeros((8, mb), F32)
        for t in range(3):
            line, lane = t * mb // QW * 8, t * mb % QW
            total = total + block[line : line + 8, lane : lane + mb]
        norms[zs] = total
    keep = group_mask()
    half = nz // 2
    for h in range(2):
        mine = range(h * half, (h + 1) * half)
        mid_par[h] = jnp.concatenate([norms[v][:4] for v in mine], axis=1)
        for t in range(9):
            cell = jnp.concatenate([taps[v, t] for v in mine], axis=1)
            full = jnp.concatenate([cell] * (QW // GW), axis=0)
            diag[h, t] = jnp.where(keep, full, 0.0).astype(BF)
    per = cb // mb
    for v in range(nz):
        lines = norms[v]
        out_par[v] = jnp.concatenate(
            [
                jnp.concatenate([lines[4 + r * per + j : 5 + r * per + j] for j in range(per)], axis=1)
                for r in range(2)
            ],
            axis=0,
        )


def group_mask():
    group_row = lax.broadcasted_iota(jnp.int32, (QW, QW), 0) // GW
    group_col = lax.broadcasted_iota(jnp.int32, (QW, QW), 1) // GW
    return group_row == group_col


def cut_kernel(nz, d, low, sc, cot, out, sem):
    spots, images = out.shape[:2]
    start = pl.multiple_of(lax.rem(sc[2] + d, nz) * images, images)
    copy = pltpu.make_async_copy(cot.at[low : low + spots, pl.ds(start, images)], out, sem)
    copy.start()
    copy.wait()


def pick_kernel(nz, k, sc, parts, *refs):
    q, out = sc[0] ^ k, refs[-1]
    cb = parts.shape[2]
    for d in range(nz):
        out[d, :cb] = parts[q, d]
        for taps in refs[:-1]:
            out[d, cb:] = taps[q, source_at(sc, nz, d)]


def total_kernel(*refs):
    total = refs[0][...].astype(F32)
    for ref in refs[1:-1]:
        total = total + ref[...].astype(F32)
    refs[-1][...] = total.astype(refs[-1].dtype)


def home_kernel(nz, sc, *refs):
    parts, outs = refs[:NQ], refs[NQ:]
    for d in range(nz):
        total = parts[0][d].astype(F32)
        for k in range(1, NQ):
            total = total + parts[k][d].astype(F32)
        outs[d][...] = total.astype(outs[d].dtype)


def pick3(masks, values):
    return masks[0] * values[0] + masks[1] * values[1] + masks[2] * values[2]


def crop_kernel(nz, d, sc, src, off, out):
    images, lanes = out.shape[1:]
    start = pl.multiple_of(lax.rem(sc[2] + d, nz) * images, images)
    at = pl.ds(start, images)
    row = jnp.broadcast_to(off[at, 0:1], (images, 128))
    col = jnp.broadcast_to(off[at, 1:2], (images, 128))
    row_masks = [(row == a).astype(F32).astype(BF) for a in range(3)]
    col_masks = [(col == a).astype(F32).astype(BF) for a in range(3)]
    for base in range(0, lanes, 128):
        span = slice(base, base + 128)
        lines = []
        for i in range(SRC):
            cells = [src[i, j, at, span] for j in range(SRC)]
            lines.append([pick3(col_masks, cells[j : j + 3]) for j in range(HW)])
            if i >= 2:
                for j in range(HW):
                    cell = pick3(row_masks, [line[j] for line in lines[i - 2 : i + 1]])
                    out[(i - 2) * HW + j, :, span] = cell


def reduce_kernel(nz, sc, *refs):
    xs, (w, own, other) = refs[:nz], refs[nz:]
    x = lanes_of(xs)
    for h in range(2):
        own[h] = dot(x, w[own_at(sc, h)].reshape(x.shape[1], QW))
        other[h] = dot(x, w[other_at(sc, h)].reshape(x.shape[1], QW)).astype(BF)


def first_sums_kernel(sc, own, rec, sums):
    for h in range(2):

        def body(at, c):
            v = own[h, at] + rec[h, at].astype(F32)
            return c[0] + fold(v), c[1] + fold(v * v)

        put_sums(sums, h, tiles(own.shape[1], body, no_sums(QW)))


def zero_border(pad, images):
    span = pad.shape[1]
    pad[0] = jnp.zeros_like(pad[0])
    pad[SRC - 1] = jnp.zeros_like(pad[0])
    edge = jnp.zeros((HW, images, pad.shape[2]), pad.dtype)
    pad[1 : HW + 1, 0:images] = edge
    pad[1 : HW + 1, span - images : span] = edge


def each_cell(images, body, carry):
    def line(i, c):
        for j in range(HW):
            at = pl.ds(pl.multiple_of((i * HW + j) * images, images), images)
            c = body(i, j, at, c)
        return c

    return lax.fori_loop(0, HW, line, carry)


def conv_kernel(count, images, sc, own, rec, tot, par, diag, act, v2, sums, pad):
    rows = HW * images
    zero_border(pad, images)
    for h in range(2):
        center, inv = norm_rows(tot[h, 0:1], tot[h, 1:2], count)
        gain, shift = par[h, 0:1], par[h, 1:2]

        def fill(i, j, at, c):
            v = own[h, at] + rec[h, at].astype(F32)
            a = gelu((v - center) * inv * gain + shift).astype(BF)
            act[h, at] = a
            pad[i + 1, (j + 1) * images : (j + 2) * images] = a
            return c

        each_cell(images, fill, 0)

        def taps(i, c):
            acc = jnp.zeros((rows, QW), F32)
            for di in range(3):
                line = pad.at[i + di]
                for dj in range(3):
                    acc = acc + dot(line[dj * images : dj * images + rows], diag[h, di * 3 + dj])
            v2[h, pl.ds(pl.multiple_of(i * rows, rows), rows)] = acc
            return c[0] + fold(acc), c[1] + fold(acc * acc)

        put_sums(sums, h, lax.fori_loop(0, HW, taps, no_sums(QW)))


def second_act_kernel(count, sc, v2, tot, par, out):
    for h in range(2):
        center, inv = norm_rows(tot[h, 0:1], tot[h, 1:2], count)
        gain, shift = par[h, 2:3], par[h, 3:4]

        def body(at, c):
            out[h, at] = gelu((v2[h, at] - center) * inv * gain + shift).astype(BF)
            return c

        tiles(v2.shape[1], body, 0)


def expand_kernel(nz, sc, own, rec, w, e, sums):
    x = lanes_of(four(sc, own, rec))
    for d in range(nz):
        e[d] = dot(x, jnp.concatenate([w[k, d] for k in four_at(sc)], axis=0))

        def body(at, c):
            v = e[d, at]
            return c[0] + fold(v), c[1] + fold(v * v)

        put_sums(sums, source_at(sc, nz, d), tiles(e.shape[1], body, no_sums(e.shape[2])))


def up_kernel(nz, count, pieces, earlier, sc, e, tot, par, *refs):
    many = len(pieces)
    xs, refs = refs[:many], refs[many:]
    cots, refs = refs[: sum(pieces.values())], refs[sum(pieces.values()) + 2 * earlier :]
    outs, (up, sums) = refs[:many], refs[many:]
    used = 0
    for j, d in enumerate(pieces):
        zs = source_at(sc, nz, d)
        t = tot[zs]
        center, inv = norm_rows(t[0:1], t[1:2], count)
        gain, shift = par[zs, 0:1], par[zs, 1:2]
        base = 0
        pair = no_sums(e.shape[2])
        for cot in cots[used : used + pieces[d]]:

            def body(local, c):
                size = local.size
                at = pl.ds(pl.multiple_of(local.start + base, size), size)
                hat = (e[d, at] - center) * inv
                value, slope = gelu_both(hat * gain + shift + xs[j][at].astype(F32))
                outs[j][at] = value.astype(BF)
                u = cot[local].astype(F32) * slope
                up[d, at] = u
                return c[0] + fold(u), c[1] + fold(u * hat)

            pair = tiles(cot.shape[0], body, pair)
            base += cot.shape[0]
        used += pieces[d]
        put_sums(sums, zs, pair)


def add_kernel(a, b, out):
    out[...] = a[...] + b[...]


def pass_kernel(low, value, out):
    out[...] = value[low : low + out.shape[0]]


def expand_back_kernel(nz, count, sc, e, up, tot, tot_b, par, w, eg, own, *others):
    for d in range(nz):
        zs = source_at(sc, nz, d)
        t, b = tot[zs], tot_b[zs]
        center, inv = norm_rows(t[0:1], t[1:2], count)
        factor, mean_d, mean_x = inv * par[zs, 0:1], b[0:1] / count, b[1:2] / count

        def body(at, c):
            hat = (e[d, at] - center) * inv
            eg[d, at] = (factor * (up[d, at] - mean_d - hat * mean_x)).astype(BF)
            return c

        tiles(e.shape[1], body, 0)
    grads = lanes_of([eg.at[d] for d in range(nz)])
    for h in range(2):
        weights = lanes_of([w.at[other_at(sc, h), d] for d in range(nz)])
        others[h][...] = dot_t(grads, weights).astype(BF)
    for h in range(2):
        own[h] = dot_t(grads, lanes_of([w.at[own_at(sc, h), d] for d in range(nz)]))


def second_up_kernel(count, sc, own, rec0, rec1, v2, tot, par, up, sums):
    for h in range(2):
        center, inv = norm_rows(tot[h, 0:1], tot[h, 1:2], count)
        gain, shift = par[h, 2:3], par[h, 3:4]

        def body(at, c):
            hat = (v2[h, at] - center) * inv
            received = (rec0, rec1)[h][at].astype(F32)
            u = (own[h, at] + received) * gelu_both(hat * gain + shift)[1]
            up[h, at] = u
            return c[0] + fold(u), c[1] + fold(u * hat)

        put_sums(sums, h, tiles(v2.shape[1], body, no_sums(QW)))


def conv_back_kernel(
    count, images, sc, up2, v2, tot2, tot2b, par, diag, own, rec, tot1, cg, up1, sums, pad, temp
):
    rows = HW * images
    zero_border(pad, images)
    for h in range(2):
        center2, inv2 = norm_rows(tot2[h, 0:1], tot2[h, 1:2], count)
        factor = inv2 * par[h, 2:3]
        mean_d, mean_x = tot2b[h, 0:1] / count, tot2b[h, 1:2] / count

        def fill(i, j, at, c):
            hat = (v2[h, at] - center2) * inv2
            g = (factor * (up2[h, at] - mean_d - hat * mean_x)).astype(BF)
            cg[h, at] = g
            pad[i + 1, (j + 1) * images : (j + 2) * images] = g
            return c

        each_cell(images, fill, 0)
        center, inv = norm_rows(tot1[h, 0:1], tot1[h, 1:2], count)
        gain, shift = par[h, 0:1], par[h, 1:2]

        def taps(i, c):
            acc = jnp.zeros((rows, QW), F32)
            for di in range(3):
                line = pad.at[i + 2 - di]
                for dj in range(3):
                    start = (2 - dj) * images
                    acc = acc + dot_t(line[start : start + rows], diag[h, di * 3 + dj])
            temp[...] = acc
            for j in range(HW):
                at = pl.ds(pl.multiple_of(i * rows + j * images, images), images)
                hat = (own[h, at] + rec[h, at].astype(F32) - center) * inv
                u = temp[j * images : (j + 1) * images] * gelu_both(hat * gain + shift)[1]
                up1[h, at] = u
                c = (c[0] + fold(u), c[1] + fold(u * hat))
            return c

        put_sums(sums, h, lax.fori_loop(0, HW, taps, no_sums(QW)))


def first_grad_kernel(count, sc, up1, own, rec, tot, tot_b, par, out):
    for h in range(2):
        center, inv = norm_rows(tot[h, 0:1], tot[h, 1:2], count)
        factor = inv * par[h, 0:1]
        mean_d, mean_x = tot_b[h, 0:1] / count, tot_b[h, 1:2] / count

        def body(at, c):
            hat = (own[h, at] + rec[h, at].astype(F32) - center) * inv
            out[h, at] = (factor * (up1[h, at] - mean_d - hat * mean_x)).astype(BF)
            return c

        tiles(up1.shape[1], body, 0)


def input_grad_kernel(d, sc, own, rec, up, w, out):
    weights = lanes_of([w.at[k, d] for k in four_at(sc)])
    out[...] = (up[d] + dot_t(lanes_of(four(sc, own, rec)), weights)).astype(BF)


def reduce_wgrad_kernel(nz, sc, own, rec, *refs):
    xs, out = refs[:nz], refs[nz]
    grads = lanes_of(four(sc, own, rec))
    for d in range(nz):
        g = dot_rows(xs[d][...], grads).astype(BF)
        for j, k in enumerate(four_at(sc)):
            out[k, d] = g[:, j * QW : (j + 1) * QW]


def expand_wgrad_kernel(nz, sc, own, rec, eg, out):
    width = eg.shape[2]
    grads = lanes_of([eg.at[d] for d in range(nz)])
    for ref, k in zip(four(sc, own, rec), four_at(sc)):
        g = dot_rows(ref[...], grads).astype(BF)
        for d in range(nz):
            out[k, d] = g[:, d * width : (d + 1) * width]


def conv_wgrad_kernel(images, mb, sc, act, cg, out, pad):
    rows = HW * images
    keep = group_mask()
    zero_border(pad, images)
    for h in range(2):
        for i in range(HW):
            pad[i + 1, images : images + rows] = act[h, i * rows : (i + 1) * rows]
        grad = cg[h]
        cells = []
        for di in range(3):
            for dj in range(3):
                window = pad[di : di + HW, dj * images : dj * images + rows]
                full = dot_rows(window.reshape(HW * rows, QW), grad)
                full = jnp.where(keep, full, 0.0)
                cells.append(jnp.sum(full.reshape(QW // GW, GW, QW), axis=0))
        for q in range(NQ):
            for a in range(QW // mb):
                pieces = [c[q * 8 : q * 8 + 8, a * mb : (a + 1) * mb] for c in cells]
                out[q, h * (QW // mb) + a] = join_taps(pieces, mb)


def square_sum(x):
    return jnp.sum(x.reshape(x.shape[0] // 8, 8, x.shape[1]), axis=0)


def lane_fold(x):
    return sum(x[:, j : j + 128] for j in range(0, x.shape[1], 128)) if x.shape[1] > 128 else x


def grads_kernel(nz, sc, *refs):
    firsts, seconds, (mid, out) = refs[:NQ], refs[NQ : 2 * NQ], refs[2 * NQ : 2 * NQ + 2]
    expand, reduce, taps, squares, first, second = refs[2 * NQ + 2 :]
    cb, mb = reduce.shape[0], taps.shape[2]
    half = nz // 2
    for k in range(NQ):
        first[sc[0] ^ k] = firsts[k][...]
        second[sc[0] ^ k] = seconds[k][...]
    total = jnp.zeros((8, 128), F32)
    for q in range(NQ):
        for a in range(half):
            start = (((q % 2) * half + a) * 2 + q // 2) * mb
            piece = second[q, a * mb : (a + 1) * mb].astype(F32)
            expand[start : start + mb] = piece
            total = total + lane_fold(square_sum(piece * piece))
            piece = first[q, :cb, a * mb : (a + 1) * mb]
            reduce[:, start : start + mb] = piece.astype(F32)
        block = first[q, cb:].astype(F32)
        for t in range(9):
            line, lane = tap_spot(t, mb)
            taps[t, q * 8 : (q + 1) * 8] = block[line : line + 8, lane : lane + mb]
        full = first[q].astype(F32)
        total = total + lane_fold(square_sum(full * full))
    extra = jnp.sum(mid[...] * mid[...]) + jnp.sum(out[...] * out[...])
    corner = lax.broadcasted_iota(jnp.int32, (8, 128), 0) + lax.broadcasted_iota(
        jnp.int32, (8, 128), 1
    )
    total = total + jnp.where(corner == 0, extra, 0.0)
    squares[...] = jnp.broadcast_to(jnp.sum(total, keepdims=True), (8, 128))


def place_kernel(nz, d, low, sc, block, *refs):
    out, token, sem = refs[-3:]
    token[...] = jnp.zeros_like(token)
    spots, images = block.shape[:2]
    start = pl.multiple_of(lax.rem(sc[2] + d, nz) * images, images)
    copy = pltpu.make_async_copy(block, out.at[low : low + spots, pl.ds(start, images)], sem)
    copy.start()
    copy.wait()


def adam_step(weight, gradient, momentum, variance, learn_rate, decay_rate):
    momentum_new = moment_decay * momentum + (1.0 - moment_decay) * gradient
    variance_new = moment_decay * variance + (1.0 - moment_decay) * gradient * gradient
    correction = 1.0 - moment_decay**STEP
    direction = momentum_new / correction / (jnp.sqrt(variance_new / correction) + adam_eps)
    weight_new = weight - learn_rate * (direction + decay_rate * weight)
    return (weight_new, momentum_new, variance_new, weight_new.astype(BF))


def shards(
    source,
    offsets,
    cotangent,
    reduce_weight,
    reduce_first,
    reduce_second,
    group_weight,
    group_first,
    group_second,
    expand_weight,
    expand_first,
    expand_second,
    mid_norms,
    mid_first,
    mid_second,
    out_norms,
    out_first,
    out_second,
):
    nd, ng = lax.axis_size("dp"), lax.axis_size("group")
    nz = ng // 2
    gi = lax.axis_index("group")
    z, core = gi // 2, gi % 2
    p = lax.axis_index("dp") % NQ
    sc = jnp.stack([p, core, z]).astype(jnp.int32)
    n = source.shape[0]
    images = n // nz
    rows = SPOTS * images
    cb = source.shape[3]
    mb = group_weight.shape[3]
    zh = nz // 2
    count = float(SPOTS * n * nd)

    def over_z(value, d):
        pairs = [(2 * a + c, 2 * ((a + d) % nz) + c) for a in range(nz) for c in range(2)]
        return lax.ppermute(value, "group", pairs)

    def over_core(value):
        return lax.ppermute(value, "group", [(a, a ^ 1) for a in range(ng)])

    def over_dp(value, k):
        return lax.ppermute(value, "dp", [(a, a ^ k) for a in range(nd)])

    def pinned_add(a, b, pins):
        shape = sds(a.shape, F32)
        return call(add_kernel, "add", shape, a, b, specs=[VMEM] * 2, deps=pins)

    def over_all_dp(value, *pins):
        k = 1
        while k < nd:
            other = over_dp(value, k)
            k *= 2
            if k < nd or not pins:
                value = value + other
            else:
                value = pinned_add(value, other, pins)
        return value

    def over_all_z(value, *pins):
        k = 2
        while k < ng:
            other = lax.ppermute(value, "group", [(a, a ^ k) for a in range(ng)])
            k *= 2
            if k < ng or not pins:
                value = value + other
            else:
                value = pinned_add(value, other, pins)
        return value

    def everywhere(value, *pins):
        return over_all_z(over_all_dp(value), *pins)

    src = source.transpose(1, 2, 0, 3)
    crops = []
    order = [1] + list(range(2, nz))[::-1] + [0]
    for d in order:
        crop = call(
            functools.partial(crop_kernel, nz, d),
            "crop",
            sds((SPOTS, images, cb), BF),
            sc,
            src,
            offsets,
            deps=crops[-1:],
        ).reshape(rows, cb)
        crops.append(crop)
    pixels = [over_z(crops[order.index(d)], d) if d else crops[-1] for d in range(nz)]

    col_starts = [((p % 2) * zh + j) * 2 * mb + (p // 2) * mb for j in range(zh)]
    reduce_piece = jnp.concatenate(
        [lax.dynamic_slice_in_dim(reduce_weight, s, mb, 1) for s in col_starts], axis=1
    ).astype(BF)
    expand_piece = (
        lax.dynamic_slice(
            expand_weight.reshape(nz, 2, mb, cb),
            ((p % 2) * zh, p // 2, 0, 0),
            (zh, 1, mb, cb),
        )
        .reshape(QW, cb)
        .astype(BF)
    )

    pack = jnp.concatenate([mid_norms, out_norms.reshape(-1, mb)], axis=0)
    bundle = call(
        bundle_kernel,
        "bundle",
        sds((2 * cb + tap_lines(mb) + 16, QW), BF),
        sc,
        reduce_piece,
        expand_piece,
        group_weight.reshape(9, GW, mb),
        pack,
        deps=crops[:1],
    )

    lines = cb + tap_lines(mb) + 16
    parts = [sds((1, nz, lines, QW), BF), sds((1, nz, cb, QW), BF)]

    def pair(a, b, shape, *deps):
        return call(pair_kernel, "pair", sds((2,) + shape, BF), a, b, specs=[VMEM] * 2, deps=deps)

    first_w, second_w = call(
        functools.partial(stack_kernel, lines),
        "stack",
        parts,
        bundle,
        *[over_z(bundle, d) for d in range(1, nz)],
        specs=[VMEM] * nz,
        deps=[crops[-1], pixels[1]],
    )

    first_x, second_y = over_dp(first_w, 1), over_dp(second_w, 2)
    first_y, second_x = (
        over_dp(pair(first_w, first_x, first_w.shape[1:], pixels[-1]), 2),
        over_dp(pair(second_w, second_y, second_w.shape[1:], pixels[-1]), 1),
    )
    reduce_q, expand_q, diag, mid_par, out_par = call(
        functools.partial(spread_kernel, nz),
        "spread",
        [
            sds((NQ, nz, cb, QW), BF),
            sds((NQ, nz, QW, cb), BF),
            sds((2, 9, QW, QW), BF),
            sds((2, 4, QW), F32),
            sds((nz, 2, cb), F32),
        ],
        sc,
        first_w,
        first_x,
        first_y,
        second_w,
        second_y,
        second_x,
        scratch=[pltpu.VMEM((nz, 9, GW, mb), F32), pltpu.VMEM((nz, 8, mb), F32)],
    )

    cot = cotangent.transpose(1, 2, 0, 3).reshape(SPOTS, n, cb)

    def cut(d, low, high, *deps):
        return call(
            functools.partial(cut_kernel, nz, d, low),
            "cut",
            sds((high - low, images, cb), BF),
            sc,
            cot,
            specs=[SMEM, ANY],
            scratch=[pltpu.SemaphoreType.DMA],
            deps=deps,
        ).reshape((high - low) * images, cb)

    def turn(d):
        return 0 if d == 1 else (1 if d == nz - 1 else 2)

    half_f, half_b = sds((2, rows, QW), F32), sds((2, rows, QW), BF)
    sum2_s, sumz_s = sds((2, 2, QW), F32), sds((nz, 2, cb), F32)
    pad_s = pltpu.VMEM((SRC, SRC * images, QW), BF)

    own1, oth1 = call(
        functools.partial(reduce_kernel, nz),
        "reduce",
        [half_f, half_b],
        sc,
        *pixels,
        reduce_q,
        limit=16,
        deps=[diag, mid_par, out_par, expand_q],
    )
    rec1 = over_core(oth1)
    turns = [[d for d in range(1, nz) if turn(d) == t] for t in range(3)]
    split = SPOTS // 2
    out_turns = [
        [(d, 0, SPOTS) for d in turns[0]],
        [(d, 0, SPOTS) for d in turns[1]],
        [(d, 0, split) for d in turns[2]],
        [(d, split, SPOTS) for d in turns[2]],
    ]
    cot_turns = [
        [(d, 0, SPOTS) for d in turns[0]],
        [(d, 0, SPOTS) for d in turns[1]] + [(d, 0, 10) for d in turns[2]],
        [(d, 10, 30) for d in turns[2]],
        [(d, 30, SPOTS) for d in turns[2]],
    ]
    cots = {0: [cut(0, 0, SPOTS, diag)]}

    def send_cots(t, *deps):
        pieces = [cut(*spot, *deps) for spot in cot_turns[t]]
        moved = [over_z(piece, spot[0]) for spot, piece in zip(cot_turns[t], pieces)]
        for spot, piece in zip(cot_turns[t], moved):
            cots.setdefault(spot[0], []).append(piece)
        return pieces, moved

    sent, pins = send_cots(0, oth1)
    sums1 = call(first_sums_kernel, "first_sums", sum2_s, sc, own1, rec1, deps=sent)
    tot1 = everywhere(sums1, *pins)
    sent, pins = send_cots(1, tot1)
    act, v2, sums2 = call(
        functools.partial(conv_kernel, count, images),
        "conv",
        [half_b, half_f, sum2_s],
        sc,
        own1,
        rec1,
        tot1,
        mid_par,
        diag,
        scratch=[pad_s],
        deps=sent,
    )
    tot2 = everywhere(sums2, *pins)
    sent, pins = send_cots(2, tot2)
    sent_more, last_cots = send_cots(3, tot2)
    sa = call(
        functools.partial(second_act_kernel, count),
        "second_act",
        half_b,
        sc,
        v2,
        tot2,
        mid_par,
        deps=sent + sent_more,
    )
    sa_rec = over_core(sa)
    e, sums3 = call(
        functools.partial(expand_kernel, nz),
        "expand",
        [sds((nz, rows, cb), F32), sumz_s],
        sc,
        sa,
        sa_rec,
        expand_q,
        limit=12,
    )
    tot3 = everywhere(sums3, *pins)
    def upward(ds, *earlier, deps=()):
        many = len(ds)
        pieces = {d: len(cots[d]) for d in ds}
        at = 4 + many + sum(pieces.values())
        res = call(
            functools.partial(up_kernel, nz, count, pieces, len(earlier) // 2),
            "up",
            [sds((rows, cb), BF)] * many + [sds((nz, rows, cb), F32), sumz_s],
            sc,
            e,
            tot3,
            out_par,
            *[pixels[d] for d in ds],
            *[piece for d in ds for piece in cots[d]],
            *earlier,
            input_output_aliases={at: many, at + 1: many + 1} if earlier else {},
            deps=deps,
        )
        return dict(zip(ds, res[:many])), res[many], res[many + 1]

    early, up3, sums3b = upward(turns[0], deps=last_cots)
    values, up3, sums3b = upward([d for d in range(nz) if d not in turns[0]], up3, sums3b)
    values.update(early)
    outs = [(0, 0, values[0])]

    def send_outs(t, *deps):
        pieces, moved = [], []
        for d, low, high in out_turns[t]:
            piece = values[d]
            if deps:
                piece = call(
                    functools.partial(pass_kernel, low * images),
                    "pass",
                    sds(((high - low) * images, cb), BF),
                    piece,
                    specs=[VMEM],
                    deps=deps,
                )
            pieces.append(piece)
            moved.append(over_z(piece, -d))
            outs.append((d, low, moved[-1]))
        return pieces, moved

    sent, pins = send_outs(0)
    tot3b = everywhere(sums3b, *pins)

    def place(pieces, result=None, *deps):
        for d, low, piece in pieces:
            extra = () if result is None else (result,)
            result, token = call(
                functools.partial(place_kernel, nz, d, low),
                "place",
                [sds((SPOTS, n, cb), BF), sds((8, 128), F32)],
                sc,
                piece.reshape(-1, images, cb),
                *extra,
                specs=[SMEM, VMEM] + [ANY] * len(extra),
                out_specs=[ANY, VMEM],
                scratch=[pltpu.SemaphoreType.DMA],
                input_output_aliases={2: 0} if extra else {},
                deps=deps,
            )
        return result, token

    def to_images(result):
        return result.reshape(HW, HW, n, cb).transpose(2, 0, 1, 3)

    sent, pins = send_outs(1, tot3b)
    eg, own2, *oth2 = call(
        functools.partial(expand_back_kernel, nz, count),
        "expand_back",
        [sds((nz, rows, cb), BF), half_f] + [sds((rows, QW), BF)] * 2,
        sc,
        e,
        up3,
        tot3,
        tot3b,
        out_par,
        expand_q,
        deps=sent,
    )
    expand_parts = call(
        functools.partial(expand_wgrad_kernel, nz),
        "expand_wgrad",
        sds((NQ, nz, QW, cb), BF),
        sc,
        sa,
        sa_rec,
        eg,
        limit=12,
    )

    def pick(k, parts, *more, deps=()):
        return call(
            functools.partial(pick_kernel, nz, k),
            "pick",
            sds((nz, parts.shape[2] + sum(v.shape[2] for v in more), parts.shape[3]), BF),
            sc,
            parts,
            *more,
            deps=deps,
        )

    def gather_home(picks, deps=()):
        shape = picks[0].shape[1:]
        return call(
            functools.partial(home_kernel, nz),
            "home",
            [sds(shape, F32)] + [sds(shape, BF)] * (nz - 1),
            sc,
            picks[0],
            *[over_dp(picks[k], k) for k in range(1, NQ)],
            deps=deps,
        )

    def total_of(pieces, deps=()):
        low = call(
            total_kernel,
            "total",
            sds(pieces[0].shape, BF),
            pieces[0],
            *[over_z(pieces[d], -d) for d in range(1, nz)],
            specs=[VMEM] * nz,
            deps=deps,
        )
        k = NQ
        while k < nd:
            low = (low.astype(F32) + over_dp(low, k).astype(F32)).astype(BF)
            k *= 2
        return low

    def to_all_dp(low):
        return [low] + [over_dp(low, k) for k in range(1, NQ)]

    rec2 = [over_core(v) for v in oth2]
    up2, sums2b = call(
        functools.partial(second_up_kernel, count),
        "second_up",
        [half_f, sum2_s],
        sc,
        own2,
        *rec2,
        v2,
        tot2,
        mid_par,
        deps=[expand_parts],
    )
    mid2b = over_all_dp(sums2b)
    tot2b = over_all_z(mid2b, *pins)
    sent, pins = send_outs(2, tot2b)
    expand_picks = [pick(k, expand_parts, deps=[mid2b]) for k in range(NQ)]
    cg, up1, sums1b = call(
        functools.partial(conv_back_kernel, count, images),
        "conv_back",
        [half_b, half_f, sum2_s],
        sc,
        up2,
        v2,
        tot2,
        tot2b,
        mid_par,
        diag,
        own1,
        rec1,
        tot1,
        scratch=[pad_s, pltpu.VMEM((HW * images, QW), F32)],
        deps=sent,
    )
    expand_pieces = gather_home(expand_picks, [sums1b])
    expand_low = total_of(expand_pieces)
    tot1b = over_all_z(over_all_dp(sums1b, expand_pieces[0]), *pins, expand_low)
    fg = call(
        functools.partial(first_grad_kernel, count),
        "first_grad",
        half_b,
        sc,
        up1,
        own1,
        rec1,
        tot1,
        tot1b,
        mid_par,
    )
    fg_rec = over_core(fg)
    def input_block(d, *deps):
        return call(
            functools.partial(input_grad_kernel, d),
            "input_grad",
            sds((rows, cb), BF),
            sc,
            fg,
            fg_rec,
            up3,
            reduce_q,
            deps=deps,
        )

    first = input_block(2)
    reduce_parts = call(
        functools.partial(reduce_wgrad_kernel, nz),
        "reduce_wgrad",
        sds((NQ, nz, cb, QW), BF),
        sc,
        fg,
        fg_rec,
        *pixels,
        limit=12,
        deps=[first],
    )
    conv_parts = call(
        functools.partial(conv_wgrad_kernel, images, mb),
        "conv_wgrad",
        sds((NQ, nz, tap_lines(mb), QW), BF),
        sc,
        act,
        cg,
        scratch=[pad_s],
        deps=[reduce_parts],
    )
    _, pins = send_outs(3, tot1b)

    def later(value, *deps):
        shape = sds(value.shape, value.dtype)
        body = functools.partial(pass_kernel, 0)
        return call(body, "pass", shape, value, specs=[VMEM], deps=deps)

    expand_home = to_all_dp(expand_low)
    reduce_picks = [
        pick(k, reduce_parts, conv_parts, deps=expand_home[1:]) for k in range(NQ)
    ]
    final = nz - 1
    input_blocks = {2: first}
    last = reduce_picks[1]
    for d in list(range(3, nz)) + [1, 0]:
        last = input_block(d, last)
        input_blocks[d] = last
    output, token = place([v for v in outs if v[1] == 0])
    pieces = gather_home(reduce_picks, [last, token])
    output, _ = place([v for v in outs if v[1] > 0], output)
    moved = [(0, 0, input_blocks[0])]
    moved += [(d, 0, over_z(input_blocks[d], -d)) for d in range(2, final)]
    placed, token = place(moved)
    reduce_low = total_of(pieces, [token] + pins)
    reduce_home = to_all_dp(reduce_low)
    second = later(input_blocks[1], reduce_low)
    second_moved = over_z(second, -1)
    placed, _ = place([(1, 0, second_moved)], placed)

    def my_mid(total):
        lanes = lax.dynamic_slice_in_dim(total.transpose(1, 0, 2).reshape(2, 2 * QW), z * mb, mb, 1)
        return [lanes[1], lanes[0]]

    mid_grads = jnp.stack(my_mid(tot1b) + my_mid(tot2b))
    mine3 = lax.dynamic_index_in_dim(tot3b, z, 0, keepdims=False)
    out_grads = jnp.stack([mine3[1], mine3[0]])

    expand_wgrad, reduce_wgrad, tap_grad, total_sq = call(
        functools.partial(grads_kernel, nz),
        "grads",
        [
            sds((MID, cb), F32),
            sds((cb, MID), F32),
            sds((9, GW, mb), F32),
            sds((8, 128), F32),
        ],
        sc,
        *reduce_home,
        *expand_home,
        mid_grads,
        out_grads,
        scratch=[
            pltpu.VMEM((NQ, cb + tap_lines(mb), QW), BF),
            pltpu.VMEM((NQ, QW, cb), BF),
        ],
        deps=[second],
    )
    group_wgrad = tap_grad.reshape(group_weight.shape)
    total_sq = over_all_z(total_sq + over_core(total_sq), second_moved)
    moved = over_z(later(input_blocks[final], second_moved), -final)
    input_grad, _ = place([(final, 0, moved)], placed)
    grad_norm = jnp.sqrt(total_sq[0, 0])
    clip_scale = jnp.minimum(1.0, clip_norm / (grad_norm + 1e-06))
    reduce_out = adam_step(
        reduce_weight,
        reduce_wgrad * clip_scale,
        reduce_first,
        reduce_second,
        1.0 / jnp.sqrt(1.0 * CIN),
        0.1,
    )
    group_out = adam_step(
        group_weight,
        group_wgrad * clip_scale,
        group_first,
        group_second,
        1.0 / jnp.sqrt(9.0 * GW),
        0.1,
    )
    expand_out = adam_step(
        expand_weight,
        expand_wgrad * clip_scale,
        expand_first,
        expand_second,
        1.0 / jnp.sqrt(1.0 * MID),
        0.1,
    )
    mid_out = adam_step(mid_norms, mid_grads * clip_scale, mid_first, mid_second, 0.5, 0.0)
    out_out = adam_step(out_norms, out_grads * clip_scale, out_first, out_second, 0.5, 0.0)
    return (
        to_images(output),
        to_images(input_grad),
        grad_norm,
        *reduce_out,
        *group_out,
        *expand_out,
        *mid_out,
        *out_out,
    )


def solution(mesh):
    images = P("dp", None, None, "group")
    rows, cols = P("group", None), P(None, "group")
    kernel = P(None, None, None, "group")
    in_specs = (
        (images, P("dp", None), images) + (rows,) * 3 + (kernel,) * 3 + (cols,) * 3 + (cols,) * 6
    )
    out_specs = (images, images, P()) + (rows,) * 4 + (kernel,) * 4 + (cols,) * 4 + (cols,) * 8
    return jax.shard_map(shards, mesh=mesh, in_specs=in_specs, out_specs=out_specs, check_vma=False)
```
